512 devices in a mesh: gx: 16 (over z_lo, x), gy: 32 (over z_hi, y, core).
Axes of the slice: x: 4, y: 8, z: 8 (z_hi: 2, z_lo: 4; z = z_hi * 4 + z_lo), core: 2. Of those that a mesh axis runs over, the one named last changes fastest.
Arguments:
- momentum_distribution: float32 [19, 8, 64, 4096], P(None, None, 'gx', 'gy'), may hold values from 0.02 to 0.05
- energy_distribution: float32 [7, 8, 64, 4096], P(None, None, 'gx', 'gy'), may hold values from 0.05 to 0.2
- metal_warmness: float32 [8, 32, 4096], P(None, 'gx', 'gy'), may hold values from 0.5 to 1.5
- metal_indicator: int32 [8, 32, 4096], P(None, 'gx', 'gy'), may hold values 0 or 1
- interface_holder: int32 [16, 4096, 1], P('gx', 'gy'), may hold values from 0 to 31; in each aligned block of 128 rows (0 to 127, 128 to 255, ..., all dimensions but the last counted through in order) at most 8 rows name the same one
- brick_tallies: int32 [16, 32], P('gx', 'gy'), may hold values from 96 to 128, as said below
- boundary_brick_index: int32 [16, 4096], P('gx', 'gy'), may hold values from 0 to 511, as said below
- metal_face_index: int32 [16, 4096], P('gx', 'gy'), may hold values from 0 to 255
Outputs:
- flow_out: float32 [19, 8, 64, 4096], P(None, None, 'gx', 'gy')
- heat_out: float32 [7, 8, 64, 4096], P(None, None, 'gx', 'gy')
- solid_out: float32 [8, 32, 4096], P(None, 'gx', 'gy')
The draws below stay inside these ranges and needn't reach their ends.
Inputs may be any that keep to these rules, and one draw needn't show every extreme that they name: `interface_holder`: within the 128 rows of one brick, live or not, at most 8 name one owner; some brick reaches 8. `brick_tallies`: some brick has all 128 rows live. `boundary_brick_index`: the 128 entries of one brick are distinct.
All inputs are finite; a program needn't handle non-finite values. No bound on the sum of `metal_indicator` on one device may be relied on, other than what follows from the above.
Results may differ from the reference program's by a relative error of at most 0.0001.
Values sent between devices are 32-bit elements; how exact they have to be, the bound alone decides.
A program may use at most 64 MiB of HBM per device.

```python
import math
import jax
import jax.numpy as jnp
import numpy as np

BX = 4
BY = 128
NZ = 8
SXD = 2
SYD = 128
METAL_STRATA = 8
ROWS = 128
STEPS = 3
CAP = 8
FLUID_SPAN_EAST = 64
FLUID_SPAN_NORTH = 4096
METAL_SPAN_EAST = 32
METAL_SPAN_NORTH = 4096
N_GX = 16
N_GY = 32


def draw_brick_tallies(key, part):
    key = jax.random.fold_in(key, 11)
    key_base, key_full = jax.random.split(key)
    drawn = jax.random.randint(key_base, (N_GX, N_GY), 3 * ROWS // 4, ROWS + 1)
    chosen = jax.random.randint(key_full, (), 0, N_GX * N_GY)
    places = jnp.arange(N_GX * N_GY, dtype=jnp.int32).reshape(N_GX, N_GY)
    return jnp.where(places == chosen, ROWS, drawn).astype(jnp.int32)


def draw_boundary_brick_index(key, part):
    key = jax.random.fold_in(key, 23)
    keys = jax.random.split(key, N_GX * N_GY)
    orders = jax.vmap(lambda single: jax.random.permutation(single, BX * BY)[:ROWS])(keys)
    return orders.reshape(N_GX, N_GY * ROWS).astype(jnp.int32)


def touch_ends(values, own_key, least, high):
    index_at = [jax.random.randint(jax.random.fold_in(own_key, axis), (), 0, length) for axis, length in enumerate(values.shape)]
    widest = values.shape.index(max(values.shape))
    next_to = index_at[:widest] + [(index_at[widest] + 1) % values.shape[widest]] + index_at[widest + 1:]
    return values.at[tuple(index_at)].set(least).at[tuple(next_to)].set(high)


def level_of(stream_key, shape, shards, least, largest):
    factor_of = 1.0
    for position, blocks in shards:
        draws = jax.random.uniform(jax.random.fold_in(jax.random.fold_in(stream_key, 6), position), (blocks,), jnp.float32, least / len(shards), largest / len(shards))
        factor_of = factor_of * jnp.repeat(jnp.exp(draws), shape[position] // blocks).reshape((-1,) + (1,) * (len(shape) - 1 - position))
    return factor_of


def shared_out(own_key, own, number, rows, count, top, limit, slope):
    ranking = jax.random.permutation(own_key, count)
    packed, common = load_shares(count, rows * top, limit, slope, True), load_shares(count, rows * top, limit, slope, False)
    places = jnp.arange(count)

    def named(lengths, turn):
        used = int((lengths > 0).sum())
        fixed = max(1, used // 4)
        passed = fixed + (places - fixed + turn * (used - fixed)) % max(1, count - fixed)
        return jnp.zeros((count,), jnp.int32).at[ranking[jnp.where(places < fixed, places, passed)]].set(jnp.asarray(lengths, jnp.int32))

    lengths = jnp.where(number % 4 == 0, named(packed, number // 4), named(common, number - number // 4 - 1))
    mixed = jax.random.permutation(jax.random.fold_in(own, 3), count)
    giver, receiver = mixed[0:count // 2 * 2:2], mixed[1:count // 2 * 2:2]
    margin = jnp.minimum(lengths[giver] - 1, limit - lengths[receiver]) // 2
    margin = jnp.where((giver == ranking[0]) | (receiver == ranking[0]) | (lengths[receiver] == 0), 0, jnp.maximum(margin, 0))
    passed = jax.random.randint(jax.random.fold_in(own, 4), (count // 2,), 0, 1 << 20) % (margin + 1)
    lengths = lengths.at[giver].add(-passed).at[receiver].add(passed)
    members = jnp.searchsorted(jnp.cumsum(lengths), jnp.arange(rows * top), side="right").astype(jnp.int32)
    listing = members.reshape(top, rows).T
    listing = listing[jax.random.permutation(jax.random.fold_in(own, 1), rows)]
    turn = jax.random.randint(jax.random.fold_in(own, 2), (rows, 1), 0, top)
    return jnp.take_along_axis(listing, (jnp.arange(top)[None, :] + turn) % top, axis=1)


def load_shares(count, total, limit, skew, full):
    weights = [(1 << 20) // math.isqrt(grade ** skew) + 1 for grade in range(1, count + 1)]
    largest = limit if full else min(limit, max(-(-total // count), total * weights[0] // sum(weights)))
    least = 1 if total - largest >= count - 1 else 0
    holding, spare = [largest] + [least] * (count - 1), total - largest - least * (count - 1)
    while spare > 0:
        movable = [i for i in range(1, count) if holding[i] < largest] or [i for i in range(1, count) if holding[i] < limit]
        pool, remaining = sum([weights[i] for i in movable]), spare
        for i in movable:
            addition = min(limit - holding[i], max(1, remaining * weights[i] // pool), spare)
            holding[i] = holding[i] + addition
            spare = spare - addition
    return np.array(holding)


def setup_inputs(seed: int = 0) -> dict:
    splits = jax.random.split(jax.random.key(seed), 9)
    momentum_distribution = jnp.clip(0.02 + 0.030000001 * jax.random.uniform(splits[0], (19, NZ, FLUID_SPAN_EAST, FLUID_SPAN_NORTH), jnp.float32) ** level_of(splits[0], (19, NZ, FLUID_SPAN_EAST, FLUID_SPAN_NORTH), ((2, 16), (3, 32)), -0.2, 0.2), 0.02, 0.05)
    energy_distribution = jnp.clip(0.05 + 0.15 * jax.random.uniform(splits[1], (7, NZ, FLUID_SPAN_EAST, FLUID_SPAN_NORTH), jnp.float32) ** level_of(splits[1], (7, NZ, FLUID_SPAN_EAST, FLUID_SPAN_NORTH), ((2, 16), (3, 32)), -0.2, 0.2), 0.05, 0.2)
    metal_warmness = jnp.clip(0.5 + 1.0 * jax.random.uniform(splits[2], (METAL_STRATA, METAL_SPAN_EAST, METAL_SPAN_NORTH), jnp.float32) ** level_of(splits[2], (METAL_STRATA, METAL_SPAN_EAST, METAL_SPAN_NORTH), ((1, 16), (2, 32)), -0.2, 0.2), 0.5, 1.5)
    metal_indicator = touch_ends((jax.random.randint(splits[3], (METAL_STRATA, METAL_SPAN_EAST, METAL_SPAN_NORTH), 0, 4) < 3).astype(jnp.int32), jax.random.fold_in(splits[3], 1), 0, 1)
    interface_holder_keys = jax.random.split(jax.random.fold_in(splits[4], 1), N_GX * (N_GY * ROWS) // ROWS)
    interface_holder_turns = jax.random.permutation(jax.random.fold_in(splits[4], 3), N_GX * (N_GY * ROWS) // ROWS)
    interface_holder = jax.vmap(lambda own, number: shared_out(jax.random.fold_in(splits[4], 2), own, number, ROWS, N_GY, 1, CAP, 2))(interface_holder_keys, interface_holder_turns).reshape((N_GX, N_GY * ROWS, 1))
    brick_tallies = draw_brick_tallies(jax.random.fold_in(splits[8], 71), 0)
    boundary_brick_index = draw_boundary_brick_index(jax.random.fold_in(splits[8], 71), 0)
    metal_face_index = touch_ends(jax.random.randint(splits[7], (N_GX, N_GY * ROWS), 0, SXD * SYD), jax.random.fold_in(splits[7], 1), 0, (SXD * SYD) - 1).astype(jnp.int32)
    return dict(momentum_distribution=momentum_distribution, energy_distribution=energy_distribution, metal_warmness=metal_warmness, metal_indicator=metal_indicator, interface_holder=interface_holder, brick_tallies=brick_tallies, boundary_brick_index=boundary_brick_index, metal_face_index=metal_face_index)


VELOCITY = [(0, 0, 0), (1, 0, 0), (-1, 0, 0), (0, 1, 0), (0, -1, 0), (0, 0, 1), (0, 0, -1),
            (1, 1, 0), (-1, -1, 0), (1, -1, 0), (-1, 1, 0), (1, 0, 1), (-1, 0, -1), (1, 0, -1), (-1, 0, 1),
            (0, 1, 1), (0, -1, -1), (0, 1, -1), (0, -1, 1)]
WEIGHT_FLOW = [1.0 / 3.0] + [1.0 / 18.0] * 6 + [1.0 / 36.0] * 12
WARMTH_LATTICE_W = [0.25] + [0.125] * 6
ALL_VEL = VELOCITY + VELOCITY[:7]
relax_flow = 0.8
relax_heat = 0.7
solid_dt = 0.04
film_coef = 1.0


def opposite_of(main_launcher):
    local = main_launcher if main_launcher < 19 else main_launcher - 19
    vector = VELOCITY[local]
    target = VELOCITY.index((-vector[0], -vector[1], -vector[2]))
    return target if main_launcher < 19 else target + 19


def directed(states, axis):
    total = jnp.zeros_like(states[0])
    for main_launcher in range(states.shape[0]):
        if VELOCITY[main_launcher][axis] == 1:
            total = total + states[main_launcher]
        elif VELOCITY[main_launcher][axis] == -1:
            total = total - states[main_launcher]
    return total


def bgk_scattering(momentum_distribution, energy_distribution):
    density = jnp.sum(momentum_distribution, 0)
    velo_x = directed(momentum_distribution, 0) / density
    velo_y = directed(momentum_distribution, 1) / density
    velo_z = directed(momentum_distribution, 2) / density
    speed_sq = velo_x * velo_x + velo_y * velo_y + velo_z * velo_z
    momentum_after_bump = []
    for main_launcher in range(19):
        vector = VELOCITY[main_launcher]
        lattice_heading = vector[0] * velo_x + vector[1] * velo_y + vector[2] * velo_z
        maxwellian_balance = WEIGHT_FLOW[main_launcher] * density * (1.0 + 3.0 * lattice_heading + 4.5 * lattice_heading * lattice_heading - 1.5 * speed_sq)
        momentum_after_bump.append(momentum_distribution[main_launcher] - (momentum_distribution[main_launcher] - maxwellian_balance) / relax_flow)
    site_warmness = jnp.sum(energy_distribution, 0)
    energy_after_bump = []
    for main_launcher in range(7):
        vector = VELOCITY[main_launcher]
        lattice_heading = vector[0] * velo_x + vector[1] * velo_y + vector[2] * velo_z
        maxwellian_balance = WARMTH_LATTICE_W[main_launcher] * site_warmness * (1.0 + 4.0 * lattice_heading)
        energy_after_bump.append(energy_distribution[main_launcher] - (energy_distribution[main_launcher] - maxwellian_balance) / relax_heat)
    return jnp.stack(momentum_after_bump), jnp.stack(energy_after_bump), site_warmness


def propagate_bounce(displaced_field, piled_arrays, interface_warmness, coated_mask_value):
    strata_count = piled_arrays.shape[1]
    result = []
    for main_launcher in range(26):
        lift = ALL_VEL[main_launcher][2]
        if lift == 0:
            result.append(displaced_field[main_launcher])
        elif lift == 1:
            lowest_plane = piled_arrays[opposite_of(main_launcher), 0]
            if main_launcher == 24:
                lowest_plane = jnp.where(coated_mask_value > 0.5, 0.25 * interface_warmness - lowest_plane, lowest_plane)
            result.append(jnp.concatenate([lowest_plane[None], displaced_field[main_launcher][:strata_count - 1]], 0))
        else:
            upper = piled_arrays[opposite_of(main_launcher), strata_count - 1]
            result.append(jnp.concatenate([displaced_field[main_launcher][1:], upper[None]], 0))
    joined = jnp.stack(result)
    return joined[:19], joined[19:]


def spread_warmth(field_pad, cond_pad):
    size_z = field_pad.shape[0] - 2
    size_x = field_pad.shape[1] - 2
    size_y = field_pad.shape[2] - 2
    centre_field = field_pad[1:1 + size_z, 1:1 + size_x, 1:1 + size_y]
    centre_cond = cond_pad[1:1 + size_z, 1:1 + size_x, 1:1 + size_y]
    total = jnp.zeros_like(centre_field)
    for shift_vec in [(1, 0, 0), (-1, 0, 0), (0, 1, 0), (0, -1, 0), (0, 0, 1), (0, 0, -1)]:
        near_field = field_pad[1 + shift_vec[0]:1 + shift_vec[0] + size_z, 1 + shift_vec[1]:1 + shift_vec[1] + size_x,
                               1 + shift_vec[2]:1 + shift_vec[2] + size_y]
        near_cond = cond_pad[1 + shift_vec[0]:1 + shift_vec[0] + size_z, 1 + shift_vec[1]:1 + shift_vec[1] + size_x,
                             1 + shift_vec[2]:1 + shift_vec[2] + size_y]
        face = 2.0 * centre_cond * near_cond / (centre_cond + near_cond)
        total = total + face * (near_field - centre_field)
    return total


def march_forward(field, increment_amount, forcing_term):
    strata_count = field.shape[0]
    placed = jnp.concatenate([jnp.zeros((strata_count - 1,) + forcing_term.shape, field.dtype), forcing_term[None]], 0)
    return field + solid_dt * (increment_amount + placed)


def reference(momentum_distribution, energy_distribution, metal_warmness, metal_indicator, interface_holder, brick_tallies, boundary_brick_index, metal_face_index):
    number_format = momentum_distribution.dtype
    owners = interface_holder[:, :, 0]
    column = jnp.arange(N_GY * ROWS, dtype=jnp.int32)
    brick = column // ROWS
    within = column % ROWS
    active_flag = (within[None, :] < jnp.repeat(brick_tallies, ROWS, axis=1)).astype(number_format)
    row_gx = jnp.arange(N_GX, dtype=jnp.int32)[:, None]
    coolant_span_east = row_gx * BX + boundary_brick_index // BY
    coolant_span_north = brick[None, :] * BY + boundary_brick_index % BY
    metal_east_index = row_gx * SXD + metal_face_index // SYD
    metal_north_index = owners * SYD + metal_face_index % SYD
    coated_mask_value = jnp.zeros((FLUID_SPAN_EAST, FLUID_SPAN_NORTH), number_format).at[coolant_span_east, coolant_span_north].add(active_flag)
    nominal_diffusivity = 0.2 + 0.8 * metal_indicator.astype(number_format)
    for _ in range(STEPS):
        momentum_after_bump, energy_after_bump, site_warmness = bgk_scattering(momentum_distribution, energy_distribution)
        coolant_lines = site_warmness[0][coolant_span_east, coolant_span_north]
        current_boundary = metal_warmness[METAL_STRATA - 1]
        gain = active_flag * film_coef * (coolant_lines - current_boundary[metal_east_index, metal_north_index])
        forcing_term = jnp.zeros((METAL_SPAN_EAST, METAL_SPAN_NORTH), number_format).at[metal_east_index, metal_north_index].add(gain)
        fourier_diffusion_step = nominal_diffusivity * (1.0 + 0.5 * metal_warmness)
        increment_amount = spread_warmth(jnp.pad(metal_warmness, 1), jnp.pad(fourier_diffusion_step, 1))
        metal_warmness = march_forward(metal_warmness, increment_amount, forcing_term)
        interface_lines = metal_warmness[METAL_STRATA - 1][metal_east_index, metal_north_index]
        interface_warmness = jnp.zeros((FLUID_SPAN_EAST, FLUID_SPAN_NORTH), number_format).at[coolant_span_east, coolant_span_north].add(active_flag * interface_lines)
        piled_arrays = jnp.concatenate([momentum_after_bump, energy_after_bump], 0)
        displaced_field = jnp.stack([jnp.roll(piled_arrays[main_launcher], (ALL_VEL[main_launcher][0], ALL_VEL[main_launcher][1]), axis=(1, 2))
                             for main_launcher in range(26)])
        momentum_distribution, energy_distribution = propagate_bounce(displaced_field, piled_arrays, interface_warmness, coated_mask_value)
    return momentum_distribution, energy_distribution, metal_warmness
```

```python
import functools

import jax
import jax.numpy as jnp
from jax import lax
from jax.experimental import pallas as pl
from jax.experimental.pallas import tpu as pltpu
from jax.sharding import PartitionSpec as P

MESH = pl.DeviceIdType.MESH
F32 = jnp.float32
STEPS = 3
CAP = 8

VELOCITY = [
    (0, 0, 0),
    (1, 0, 0),
    (-1, 0, 0),
    (0, 1, 0),
    (0, -1, 0),
    (0, 0, 1),
    (0, 0, -1),
    (1, 1, 0),
    (-1, -1, 0),
    (1, -1, 0),
    (-1, 1, 0),
    (1, 0, 1),
    (-1, 0, -1),
    (1, 0, -1),
    (-1, 0, 1),
    (0, 1, 1),
    (0, -1, -1),
    (0, 1, -1),
    (0, -1, 1),
]
OPPOSITE = [VELOCITY.index((-a, -b, -c)) for a, b, c in VELOCITY]
ORDER = [1, 7, 9, 11, 13, 2, 8, 10, 12, 14, 0, 3, 4, 5, 6, 15, 16, 17, 18]
PLACE = {q: n for n, q in enumerate(ORDER)}
FLOW_UP = [3, 7, 10, 15, 17]
FLOW_DOWN = [4, 8, 9, 16, 18]
HEAT_UP = [3]
HEAT_DOWN = [4]
DT = 0.04
ROOM = 63 * 1024 * 1024


def lane_of(shape):
    return lax.broadcasted_iota(jnp.int32, shape, len(shape) - 1)


def sub_of(shape):
    return lax.broadcasted_iota(jnp.int32, shape, len(shape) - 2)


def turn(value, amount, axis):
    size = value.shape[axis]
    amount = amount % size
    return value if amount == 0 else pltpu.roll(value, amount, axis)


def collide_flow(state, post, velocity):
    total, moved = None, [None, None, None]
    for q in range(19):
        value = state[q]
        total = value if total is None else total + value
        for axis in range(3):
            if VELOCITY[q][axis] == 1:
                moved[axis] = value if moved[axis] is None else moved[axis] + value
            elif VELOCITY[q][axis] == -1:
                moved[axis] = -value if moved[axis] is None else moved[axis] - value
    inverse = 1.0 / total
    speed = [part * inverse for part in moved]
    for axis in range(3):
        velocity[axis] = speed[axis]
    base = 1.0 - 1.5 * (speed[0] * speed[0] + speed[1] * speed[1] + speed[2] * speed[2])
    post[1:5, PLACE[0]] = (1.25 / 3.0) * total * base - 0.25 * state[0]
    axial = (1.25 / 18.0) * total
    diagonal = (1.25 / 36.0) * total
    for q in range(1, 19):
        if OPPOSITE[q] < q:
            continue
        along = None
        for axis in range(3):
            c = VELOCITY[q][axis]
            if c:
                term = speed[axis] if c == 1 else -speed[axis]
                along = term if along is None else along + term
        even = base + 4.5 * along * along
        odd = 3.0 * along
        scale = axial if q < 7 else diagonal
        post[1:5, PLACE[q]] = scale * (even + odd) - 0.25 * state[q]
        post[1:5, PLACE[OPPOSITE[q]]] = scale * (even - odd) - 0.25 * state[OPPOSITE[q]]


def collide_heat(state, post, velocity):
    keep = 1.0 - 1.0 / 0.7
    warmth = state[0]
    for q in range(1, 7):
        warmth = warmth + state[q]
    post[1:5, 0] = keep * state[0] + (0.25 / 0.7) * warmth
    part = (0.125 / 0.7) * warmth
    for axis in range(3):
        tilt = part * (4.0 * velocity[axis])
        for q in (1 + 2 * axis, 2 + 2 * axis):
            sign = tilt if q == 1 + 2 * axis else -tilt
            post[1:5, q] = keep * state[q] + (part + sign)


def pack_edges(post, rows_up, rows_down, shift_up, shift_down):
    lane = lane_of((8, 128))
    up = down = jnp.zeros((8, 128), F32)
    for n, (a, b) in enumerate(zip(rows_up, rows_down)):
        for x in range(4):
            k = 4 * n + x
            up = jnp.where(lane == k, turn(post[x + 1 - shift_up[n], a], k + 1, 1), up)
            down = jnp.where(lane == k, turn(post[x + 1 - shift_down[n], b], k, 1), down)
    return up, down


def moved_flat(post, row, vector, n, tile):
    cx, cy = vector[0], vector[1]
    value = post[1 - cx : 5 - cx, row]
    if cy == 0:
        return value
    edge = jnp.stack([turn(tile, (128 if cy == 1 else 127) - (4 * n + x), 1) for x in range(4)])
    lane = lane_of((4, 8, 128))
    if cy == 1:
        return jnp.where(lane == 0, edge, turn(value, 1, 2))
    return jnp.where(lane == 127, edge, turn(value, 127, 2))


def lifted(value, cz, bounce):
    if cz == 0:
        return value
    layer = sub_of((4, 8, 128))
    if cz == 1:
        return jnp.where(layer == 0, bounce, turn(value, 1, 1))
    return jnp.where(layer == 7, bounce, turn(value, 7, 1))


def stream_flow(post, from_below, from_above, put):
    for q in range(19):
        vector = VELOCITY[q]
        n, tile = 0, None
        if vector[1] == 1:
            n, tile = FLOW_UP.index(q), from_below
        elif vector[1] == -1:
            n, tile = FLOW_DOWN.index(q), from_above
        value = moved_flat(post, PLACE[q], vector, n, tile)
        put(q, lifted(value, vector[2], post[1:5, PLACE[OPPOSITE[q]]]))


def stream_heat(post, from_below, from_above, covered, put):
    for q in range(7):
        vector = VELOCITY[q]
        value = moved_flat(post, q, vector, 0, from_below if vector[1] == 1 else from_above)
        bounce = post[1:5, OPPOSITE[q]]
        if q == 5:
            bounce = jnp.where(covered > 0.5, -bounce, bounce)
        put(q, lifted(value, vector[2], bounce))


def conduct_of(warmth, k):
    return k * (1.0 + 0.5 * warmth)


def fluxes(field, k, low_x, low_xk, high_x, high_xk, low_y, low_yk, high_y, high_yk, gates):
    gate_low_x, gate_high_x, gate_low_y, gate_high_y = gates
    lane, layer = lane_of((8, 128)), sub_of((8, 128))
    cond = [conduct_of(field[x], k[x]) for x in range(2)]
    result = []

    def face(a, ca, b, cb):
        return 2.0 * ca * cb / (ca + cb) * (b - a)

    inner = face(field[0], cond[0], field[1], cond[1])
    for x in range(2):
        here, c = field[x], cond[x]
        if x == 0:
            total = inner + gate_low_x * face(here, c, low_x, conduct_of(low_x, low_xk))
        else:
            total = gate_high_x * face(here, c, high_x, conduct_of(high_x, high_xk)) - inner
        below = jnp.where(lane == 0, turn(low_y[x], 1, 1), turn(here, 1, 1))
        below_k = jnp.where(lane == 0, turn(low_yk[x], 1, 1), turn(k[x], 1, 1))
        above = jnp.where(lane == 127, turn(high_y[x], 127, 1), turn(here, 127, 1))
        above_k = jnp.where(lane == 127, turn(high_yk[x], 127, 1), turn(k[x], 127, 1))
        total = total + jnp.where(lane == 0, gate_low_y, 1.0) * face(here, c, below, conduct_of(below, below_k))
        total = total + jnp.where(lane == 127, gate_high_y, 1.0) * face(here, c, above, conduct_of(above, above_k))
        down = face(here, c, turn(here, 1, 0), turn(c, 1, 0))
        up = face(here, c, turn(here, 7, 0), turn(c, 7, 0))
        total = total + jnp.where(layer == 0, 0.0, down) + jnp.where(layer == 7, 0.0, up)
        result.append(total)
    return result


def kernel(
    nx,
    ny,
    f_hbm,
    g_hbm,
    s_hbm,
    m_hbm,
    owner_hbm,
    tally_hbm,
    wall_hbm,
    face_hbm,
    f_out,
    g_out,
    s_out,
    f_in,
    g_in,
    s_in,
    m_in,
    owner_in,
    tally_in,
    wall_in,
    face_in,
    flow,
    heat,
    post_f,
    post_g,
    speeds,
    x_out,
    x_in,
    y_out,
    y_in,
    flow_out,
    flow_in,
    wall_mask,
    covered_ref,
    cell_ref,
    slot_key,
    early,
    got_early,
    late,
    got_late,
    mid,
    got_mid,
    third,
    got_third,
    answer_out,
    got_answer,
    i_sem,
    n_send,
    n_recv,
    g_send,
    g_recv,
):
    arrivals = []
    for n, (source, target) in enumerate(
        (
            (g_hbm, g_in),
            (f_hbm, f_in),
            (s_hbm, s_in),
            (m_hbm, m_in),
            (owner_hbm, owner_in),
            (tally_hbm, tally_in),
            (wall_hbm, wall_in),
            (face_hbm, face_in),
        )
    ):
        made = pltpu.make_async_copy(source, target, i_sem.at[n])
        made.start()
        arrivals.append(made)

    i, j = lax.axis_index("gx"), lax.axis_index("gy")
    right, left = lax.rem(i + 1, nx), lax.rem(i + nx - 1, nx)
    upper, lower = lax.rem(j + 1, ny), lax.rem(j + ny - 1, ny)
    barrier = pltpu.get_barrier_semaphore()
    for device in ((right, j), (left, j), (i, upper), (i, lower)):
        pl.semaphore_signal(barrier, inc=1, device_id=device, device_id_type=MESH)

    @pl.loop(1, ny)
    def _(o):
        pl.semaphore_signal(barrier, inc=1, device_id=(i, lax.rem(j + o, ny)), device_id_type=MESH)

    counter = [0]

    def copy(source, target, device):
        n = counter[0]
        counter[0] += 1
        made = pltpu.make_async_remote_copy(
            src_ref=source,
            dst_ref=target,
            send_sem=n_send.at[n],
            recv_sem=n_recv.at[n],
            device_id=device,
            device_id_type=MESH,
        )
        made.start()
        return made

    def settle(copies):
        for made in copies:
            made.wait()

    def send_flow_x(t):
        return [
            copy(post_f.at[t, 4, pl.ds(0, 5)], post_f.at[t, 0, pl.ds(0, 5)], (right, j)),
            copy(post_f.at[t, 1, pl.ds(5, 5)], post_f.at[t, 5, pl.ds(5, 5)], (left, j)),
        ]

    def send_flow_y(t):
        up, down = pack_edges(
            post_f.at[t],
            [PLACE[q] for q in FLOW_UP],
            [PLACE[q] for q in FLOW_DOWN],
            [VELOCITY[q][0] for q in FLOW_UP],
            [VELOCITY[q][0] for q in FLOW_DOWN],
        )
        flow_out[t, 0] = up
        flow_out[t, 1] = down
        return [
            copy(flow_out.at[t, 0], flow_in.at[t, 0], (i, upper)),
            copy(flow_out.at[t, 1], flow_in.at[t, 1], (i, lower)),
        ]

    def send_x(r, right_tiles, left_tiles):
        span = pl.ds(0, len(right_tiles))
        for n, (a, b) in enumerate(zip(right_tiles, left_tiles)):
            x_out[r, 0, n], x_out[r, 1, n] = a, b
        return [
            copy(x_out.at[r, 0, span], x_in.at[r, 0, span], (right, j)),
            copy(x_out.at[r, 1, span], x_in.at[r, 1, span], (left, j)),
        ]

    def send_y(r, up_tiles, down_tiles):
        span = pl.ds(0, len(up_tiles))
        for n, (a, b) in enumerate(zip(up_tiles, down_tiles)):
            y_out[r, 0, n], y_out[r, 1, n] = a, b
        return [
            copy(y_out.at[r, 0, span], y_in.at[r, 0, span], (i, upper)),
            copy(y_out.at[r, 1, span], y_in.at[r, 1, span], (i, lower)),
        ]

    def send_solid(r, field):
        return send_y(r, field, field) + send_x(r, [field[1]], [field[0]])

    def send_heat(t):
        post = post_g.at[t]
        up, down = pack_edges(post, [3], [4], [0], [0])
        return send_y(3 + t, [up], [down]) + send_x(3 + t, [post[4, 1]], [post[1, 2]])

    def to_all(source, target, pair, personal):
        @pl.loop(0, ny - 1)
        def _(s):
            pltpu.make_async_remote_copy(
                src_ref=source.at[s] if personal else source.at[0],
                dst_ref=target.at[ny - 2 - s],
                send_sem=g_send.at[pair],
                recv_sem=g_recv.at[pair],
                device_id=(i, lax.rem(j + 2 * ny - 1 - s, ny)),
                device_id_type=MESH,
            ).start()

        target[ny - 1] = source[ny - 1 if personal else 0]

    def from_all(target, pair):
        span = pl.ds(0, ny - 1)
        pltpu.make_async_copy(target.at[span], target.at[span], g_recv.at[pair]).wait()

    def all_sent(target, pair):
        span = pl.ds(0, ny - 1)
        pltpu.make_async_copy(target.at[span], target.at[span], g_send.at[pair]).wait()

    for n in (2, 3):
        arrivals[n].wait()
    solid_0 = [s_in[pl.ds(x, 8, stride=2), :] for x in range(2)]
    k = [0.2 + 0.8 * m_in[pl.ds(x, 8, stride=2), :].astype(F32) for x in range(2)]
    pl.semaphore_wait(barrier, ny - 1 + 4)
    solid_x_halo = send_x(0, [solid_0[1], k[1]], [solid_0[0], k[0]])
    solid_y_halo = send_y(0, solid_0 + k, solid_0 + k)

    square = (128, 128)
    lane, sub = lane_of(square), sub_of(square)
    lane_8, sub_8 = lane_of((8, 128)), sub_of((8, 128))
    lane_32, sub_32 = lane_of((32, 128)), sub_of((32, 128))
    diagonal = lane == sub

    def column(row):
        return jnp.sum(jnp.where(diagonal, jnp.broadcast_to(row, square), 0.0), axis=1, keepdims=True)

    def as_row(col):
        return jnp.sum(jnp.where(diagonal, jnp.broadcast_to(col, square), 0.0), axis=0, keepdims=True)

    for n in (4, 5, 6, 7):
        arrivals[n].wait()
    owner = owner_in[...]
    face_index = face_in[...]
    wall = wall_in[...]
    live = lane_of((1, 128)) < jnp.broadcast_to(tally_in[...], (1, 128))
    block = (j - owner - 1) & (ny - 1)
    cell_row = jnp.where(live, owner * 256 + face_index, -1).astype(F32)
    live_col = column(jnp.where(live, 1.0, 0.0))
    block_row = block.astype(F32)
    block_col = column(block_row)
    face_col = column(face_index.astype(F32))
    wall_y_col = column((wall & 127).astype(F32))
    wall_x_col = column((wall >> 7).astype(F32))
    rank_col = jnp.sum(
        jnp.where((jnp.broadcast_to(block_row, square) == block_col) & (lane < sub), 1.0, 0.0),
        axis=1,
        keepdims=True,
    )
    lane_f = lane.astype(F32)
    wall_hit = jnp.where(lane_f == wall_y_col, live_col, 0.0)
    for x in range(4):
        wall_mask[x] = jnp.where(wall_x_col == float(x), wall_hit, 0.0)
    slot_key[...] = jnp.where((lane & 7).astype(F32) == rank_col, jnp.broadcast_to(live_col, square), 0.0)
    to_owner = jnp.where(jnp.broadcast_to(block_row, (32, 128)) == sub_32.astype(F32), 1.0, 0.0)

    def at_wall(rows):
        total = wall_mask[0] * rows[0]
        for x in range(1, 4):
            total = total + wall_mask[x] * rows[x]
        return jnp.sum(total, axis=1, keepdims=True)

    def on_wall(col):
        return [jnp.sum(wall_mask[x] * col, axis=0, keepdims=True) for x in range(4)]

    def slots(first, second):
        fields = jnp.where(lane < 8, first, jnp.where(lane < 16, second, 0.0))
        return jnp.dot(
            to_owner, fields * slot_key[...], precision=lax.Precision.HIGHEST, preferred_element_type=F32
        )

    def fill(buffer, n, value):
        buffer[:, n, :] = jnp.broadcast_to(value, (32, 128))

    arrivals[0].wait()
    for q in range(7):
        for x in range(4):
            heat[q, x] = g_in[q, pl.ds(x, 8, stride=4), :]

    def wall_sums():
        total = heat[0, :, 0:1, :]
        for q in range(1, 7):
            total = total + heat[q, :, 0:1, :]
        return [total[x] for x in range(4)]

    t1_col = at_wall(wall_sums())
    fill(early, 0, cell_row)
    fill(early, 1, as_row(t1_col))
    early[:, 2, :] = slots(t1_col, face_col + 1.0)
    row_lane = lane_of((1, 128))
    k_top = [k[x][7:8] for x in range(2)]
    k_inner = jnp.where(row_lane == 1, turn(k_top[1], 1, 1), turn(k_top[1], 127, 1))
    fill(early, 3, jnp.where((row_lane == 0) | (row_lane == 127), k_top[0], k_inner))
    for x in range(2):
        fill(early, 4 + x, solid_0[x][7:8])
    to_all(early, got_early, 0, True)

    arrivals[1].wait()
    for q in range(19):
        for x in range(4):
            flow[q, x] = f_in[q, pl.ds(x, 8, stride=4), :]
    collide_flow(flow, post_f.at[0], speeds.at[0])
    collide_heat(heat, post_g.at[0], speeds.at[0])
    heat_halo = send_heat(0)
    flow_halo = send_flow_x(0)

    gates_x = (jnp.where(i == 0, 0.0, 1.0), jnp.where(i == nx - 1, 0.0, 1.0))
    gates_y = (jnp.where(j == 0, 0.0, 1.0), jnp.where(j == ny - 1, 0.0, 1.0))

    def conduct(field, r, inner=False):
        change = fluxes(
            field,
            k,
            x_in[r, 0, 0],
            x_in[0, 0, 1],
            x_in[r, 1, 0],
            x_in[0, 1, 1],
            field if inner else [y_in[r, 0, x] for x in range(2)],
            k if inner else [y_in[0, 0, 2 + x] for x in range(2)],
            field if inner else [y_in[r, 1, x] for x in range(2)],
            k if inner else [y_in[0, 1, 2 + x] for x in range(2)],
            gates_x + ((0.0, 0.0) if inner else gates_y),
        )
        return [field[x] + DT * change[x] for x in range(2)]

    def move_heat(t, put):
        post_g[t, 0, 1] = x_in[3 + t, 0, 0]
        post_g[t, 5, 2] = x_in[3 + t, 1, 0]
        stream_heat(post_g.at[t], y_in[3 + t, 0, 0], y_in[3 + t, 1, 0], covered_ref[...], put)

    def move_flow(t, put):
        stream_flow(post_f.at[t], flow_in[t, 0], flow_in[t, 1], put)

    def put_heat(q, value):
        heat[q] = value

    def put_flow(q, value):
        flow[q] = value

    settle(solid_x_halo)
    inner_1 = conduct(solid_0, 0, inner=True)
    for x in range(2):
        late[0, x : x + 1, :] = inner_1[x][7:8]
    to_all(late, got_late, 1, False)

    cell_ref[...] = jnp.broadcast_to(column(cell_row), square)
    for x in range(4):
        covered_ref[x] = jnp.broadcast_to(jnp.sum(wall_mask[x], axis=0, keepdims=True), (8, 128))
    face_hit = jnp.where(lane_f == column((face_index & 127).astype(F32)), 1.0, 0.0)
    lane_64 = lane_of((128, 64))
    face_x_col = column((face_index >> 7).astype(F32))
    pick = jnp.where(
        ((lane_64 & 31).astype(F32) == block_col) & ((lane_64 >> 5).astype(F32) == face_x_col), 1.0, 0.0
    )

    settle(heat_halo)
    move_heat(0, put_heat)
    third[:, 0, :] = slots(at_wall(wall_sums()), 0.0)
    to_all(third, got_third, 2, True)

    settle(flow_halo)
    flow_halo = send_flow_y(0)
    settle(solid_y_halo)
    p1 = conduct(solid_0, 0)

    from_all(got_early, 0)

    def slot_columns(value, field):
        return [
            jnp.broadcast_to(
                jnp.sum(jnp.where(lane_32 == 8 * field + c, value, 0.0), axis=1, keepdims=True), (32, 128)
            )
            for c in range(CAP)
        ]

    faces = slot_columns(got_early[:, 2, :], 1)

    def own_sums(fields):
        result = []
        for x in range(2):
            place = (lane_32 + (128 * x + 1)).astype(F32)
            totals = [jnp.zeros((32, 128), F32) for _ in fields]
            for c in range(CAP):
                hit = faces[c] == place
                for n, field in enumerate(fields):
                    totals[n] = totals[n] + jnp.where(hit, 1.0 if field is None else field[c], 0.0)
            result.append([jnp.sum(total, axis=0, keepdims=True) for total in totals])
        return result

    def on_top(value, row):
        return value + jnp.where(sub_8 == 7, jnp.broadcast_to(row, (8, 128)), 0.0)

    sums = own_sums([slot_columns(got_early[:, 2, :], 0), None])
    many = [sums[x][1] for x in range(2)]
    solid_1 = [on_top(p1[x], DT * (sums[x][0] - many[x] * solid_0[x][7:8])) for x in range(2)]
    solid_halo = send_solid(1, solid_1)

    def same_cell(ref, n, count):
        cells = cell_ref[...]

        def body(b, carry):
            hit = cells == got_early[b, 0:1, :]
            total = carry[0] + jnp.where(hit, ref[b, n : n + 1, :], 0.0)
            if count:
                return total, carry[1] + jnp.where(hit, 1.0, 0.0)
            return (total,)

        zero = jnp.zeros(square, F32)
        return lax.fori_loop(0, ny, body, (zero, zero) if count else (zero,))

    total_1, number = same_cell(got_early, 1, True)
    number_col = jnp.sum(number, axis=1, keepdims=True)
    edge_k = got_early[:, 3, :]
    crossing = []
    for x in range(2):
        here = got_early[:, 4 + x, :]
        here_k = edge_k if x == 0 else jnp.where(lane_32 == 0, turn(edge_k, 127, 1), turn(edge_k, 1, 1))
        beyond, beyond_k = (turn(turn(part, 1, 0), 127, 1) for part in (here, here_k))
        c, cb = conduct_of(here, here_k), conduct_of(beyond, beyond_k)
        up = 2.0 * c * cb / (c + cb) * (beyond - here)
        up = jnp.where((lane_32 == 127) & (sub_32 != j), up, 0.0)
        crossing.append(DT * (up - turn(turn(up, 31, 0), 1, 1)))
    settle(flow_halo)
    move_flow(0, put_flow)
    collide_flow(flow, post_f.at[1], speeds.at[1])
    flow_halo = send_flow_x(1)

    from_all(got_late, 1)
    surfaces = jnp.concatenate(
        [
            jnp.concatenate([got_late[:, x, :] + crossing[x] for x in range(2)], axis=0),
            jnp.concatenate([got_early[:, 4 + x, :] for x in range(2)], axis=0),
        ],
        axis=1,
    )
    picked = jnp.dot(pick, surfaces, precision=lax.Precision.HIGHEST, preferred_element_type=F32)
    w1_col = jnp.sum(
        face_hit * (picked[:, 0:128] - DT * number_col * picked[:, 128:256]) + DT * total_1,
        axis=1,
        keepdims=True,
    )

    def warm_wall(col):
        rows = on_wall(col)
        for x in range(4):
            heat[5, x] = heat[5, x] + jnp.where(sub_8 == 0, 0.25 * rows[x], 0.0)

    warm_wall(w1_col)
    collide_heat(heat, post_g.at[1], speeds.at[1])
    heat_halo = send_heat(1)

    from_all(got_third, 2)
    rest = own_sums([slot_columns(got_third[:, 0, :], 0)])
    settle(solid_halo)
    solid_2 = conduct(solid_1, 1)
    solid_2 = [
        on_top(solid_2[x], DT * (rest[x][0] - 0.75 * many[x] * solid_1[x][7:8])) for x in range(2)
    ]
    solid_halo = send_solid(2, solid_2)

    def at_slots(rows, field, total):
        for c in range(CAP):
            first = faces[c] == (lane_32 + 1).astype(F32)
            second = faces[c] == (lane_32 + 129).astype(F32)
            at_cell = jnp.where(first, rows[0][7:8], jnp.where(second, rows[1][7:8], 0.0))
            total = jnp.where(lane_32 == 8 * field + c, jnp.sum(at_cell, axis=1, keepdims=True), total)
        return total

    answer = at_slots(solid_2, 1, jnp.zeros((32, 128), F32))
    settle(heat_halo)
    move_heat(1, put_heat)
    a3_col = at_wall(wall_sums())
    fill(mid, 0, as_row(a3_col))
    mid[:, 1, :] = jnp.where(lane_32 < 8, slots(a3_col, 0.0), answer)
    to_all(mid, got_mid, 3, True)

    settle(flow_halo)
    flow_halo = send_flow_y(1)

    settle(solid_halo)
    p3 = conduct(solid_2, 2)
    p3 = [on_top(p3[x], (-0.75 * DT) * many[x] * solid_2[x][7:8]) for x in range(2)]
    answer_out[:, 0, :] = at_slots(p3, 0, jnp.zeros((32, 128), F32))
    to_all(answer_out, got_answer, 4, True)

    settle(flow_halo)
    move_flow(1, put_flow)
    collide_flow(flow, post_f.at[2], speeds.at[2])
    flow_halo = send_flow_x(2)

    pick_owner = jnp.where(lane_of((128, 32)).astype(F32) == block_col, 1.0, 0.0)

    def replies(value, field):
        found = jnp.dot(pick_owner, value, precision=lax.Precision.HIGHEST, preferred_element_type=F32)
        return jnp.where((lane - 8 * field).astype(F32) == rank_col, found, 0.0)

    from_all(got_mid, 3)
    w2_col = jnp.sum(replies(got_mid[:, 1, :], 1), axis=1, keepdims=True)
    warm_wall(w2_col)
    collide_heat(heat, post_g.at[2], speeds.at[2])
    heat_halo = send_heat(2)

    settle(flow_halo)
    flow_halo = send_flow_y(2)
    (total_3,) = same_cell(got_mid, 0, False)
    last = own_sums([slot_columns(got_mid[:, 1, :], 0)])
    for x in range(2):
        s_out[pl.ds(x, 8, stride=2), :] = on_top(p3[x], DT * last[x][0])

    from_all(got_answer, 4)
    w3_col = jnp.sum(replies(got_answer[:, 0, :], 0) + DT * total_3, axis=1, keepdims=True)
    w3_rows = on_wall(w3_col)

    settle(flow_halo)

    def write_flow(q, value):
        for x in range(4):
            f_out[q, pl.ds(x, 8, stride=4), :] = value[x]

    move_flow(2, write_flow)

    settle(heat_halo)

    def write_heat(q, value):
        for x in range(4):
            row = value[x]
            if q == 5:
                row = row + jnp.where(sub_8 == 0, 0.25 * w3_rows[x], 0.0)
            g_out[q, pl.ds(x, 8, stride=4), :] = row

    move_heat(2, write_heat)

    for n, target in enumerate((got_early, got_late, got_third, got_mid, got_answer)):
        all_sent(target, n)


def finish(*refs):
    sources, targets, sems = refs[0:3], refs[3:6], refs[6]
    copies = [pltpu.make_async_copy(a, b, sems.at[n]) for n, (a, b) in enumerate(zip(sources, targets))]
    for made in copies:
        made.start()
    for made in copies:
        made.wait()


def on_device(nx, ny, flow, heat, solid, metal, owner, tally, wall, face):
    vmem = functools.partial(pltpu.VMEM, dtype=F32)
    tile = (8, 128)
    copies = 3 * 4 + 6 * 4
    results = (
        jax.ShapeDtypeStruct((19, 32, 128), F32),
        jax.ShapeDtypeStruct((7, 32, 128), F32),
        jax.ShapeDtypeStruct((16, 128), F32),
    )
    out = pl.pallas_call(
        functools.partial(kernel, nx, ny),
        out_shape=tuple(pltpu.VMEM(result.shape, result.dtype) for result in results),
        in_specs=[pl.BlockSpec(memory_space=pltpu.HBM)] * 8,
        out_specs=[pl.BlockSpec(memory_space=pltpu.VMEM)] * 3,
        scratch_shapes=[
            vmem((19, 32, 128)),
            vmem((7, 32, 128)),
            vmem((16, 128)),
            pltpu.VMEM((16, 128), jnp.int32),
            pltpu.VMEM((1, 128), jnp.int32),
            pltpu.VMEM((1, 1), jnp.int32),
            pltpu.VMEM((1, 128), jnp.int32),
            pltpu.VMEM((1, 128), jnp.int32),
            vmem((19, 4) + tile),
            vmem((7, 4) + tile),
            vmem((STEPS, 6, 19) + tile),
            vmem((STEPS, 6, 7) + tile),
            vmem((STEPS, 3, 4) + tile),
            vmem((6, 2, 2) + tile),
            vmem((6, 2, 2) + tile),
            vmem((6, 2, 4) + tile),
            vmem((6, 2, 4) + tile),
            vmem((STEPS, 2) + tile),
            vmem((STEPS, 2) + tile),
            vmem((4, 128, 128)),
            vmem((4,) + tile),
            vmem((128, 128)),
            vmem((128, 128)),
            vmem((32, 6, 128)),
            vmem((32, 6, 128)),
            vmem((1, 2, 128)),
            vmem((32, 2, 128)),
            vmem((32, 2, 128)),
            vmem((32, 2, 128)),
            vmem((32, 1, 128)),
            vmem((32, 1, 128)),
            vmem((32, 1, 128)),
            vmem((32, 1, 128)),
            pltpu.SemaphoreType.DMA((8,)),
            pltpu.SemaphoreType.DMA((copies,)),
            pltpu.SemaphoreType.DMA((copies,)),
            pltpu.SemaphoreType.DMA((5,)),
            pltpu.SemaphoreType.DMA((5,)),
        ],
        compiler_params=pltpu.CompilerParams(
            collective_id=0, has_side_effects=True, vmem_limit_bytes=ROOM
        ),
        name="coupled_steps",
    )(
        flow.reshape(19, 32, 128),
        heat.reshape(7, 32, 128),
        solid.reshape(16, 128),
        metal.reshape(16, 128),
        owner.reshape(1, 128),
        tally,
        wall,
        face,
    )
    out = pl.pallas_call(
        finish,
        out_shape=results,
        in_specs=[pl.BlockSpec(memory_space=pltpu.VMEM)] * 3,
        out_specs=[pl.BlockSpec(memory_space=pltpu.HBM)] * 3,
        scratch_shapes=[pltpu.SemaphoreType.DMA((3,))],
        name="write_out",
    )(*out)
    return out[0].reshape(19, 8, 4, 128), out[1].reshape(7, 8, 4, 128), out[2].reshape(8, 2, 128)


def solution(mesh):
    placed = (
        P(None, None, "gx", "gy"),
        P(None, None, "gx", "gy"),
        P(None, "gx", "gy"),
        P(None, "gx", "gy"),
        P("gx", "gy", None),
        P("gx", "gy"),
        P("gx", "gy"),
        P("gx", "gy"),
    )
    return jax.shard_map(
        functools.partial(on_device, mesh.shape["gx"], mesh.shape["gy"]),
        mesh=mesh,
        in_specs=placed,
        out_specs=(P(None, None, "gx", "gy"), P(None, None, "gx", "gy"), P(None, "gx", "gy")),
        check_vma=False,
    )
```

```python
import functools

import jax
import jax.numpy as jnp
from jax import lax
from jax.experimental import pallas as pl
from jax.experimental.pallas import tpu as pltpu
from jax.sharding import PartitionSpec as P

MESH = pl.DeviceIdType.MESH
F32 = jnp.float32
STEPS = 3
CAP = 8

VELOCITY = [
    (0, 0, 0),
    (1, 0, 0),
    (-1, 0, 0),
    (0, 1, 0),
    (0, -1, 0),
    (0, 0, 1),
    (0, 0, -1),
    (1, 1, 0),
    (-1, -1, 0),
    (1, -1, 0),
    (-1, 1, 0),
    (1, 0, 1),
    (-1, 0, -1),
    (1, 0, -1),
    (-1, 0, 1),
    (0, 1, 1),
    (0, -1, -1),
    (0, 1, -1),
    (0, -1, 1),
]
OPPOSITE = [VELOCITY.index((-a, -b, -c)) for a, b, c in VELOCITY]
ORDER = [1, 7, 9, 11, 13, 2, 8, 10, 12, 14, 0, 3, 4, 5, 6, 15, 16, 17, 18]
PLACE = {q: n for n, q in enumerate(ORDER)}
DT = 0.04
ROOM = 63 * 1024 * 1024


def lane_of(shape):
    return lax.broadcasted_iota(jnp.int32, shape, len(shape) - 1)


def sub_of(shape):
    return lax.broadcasted_iota(jnp.int32, shape, len(shape) - 2)


def turn(value, amount, axis):
    size = value.shape[axis]
    amount = amount % size
    return value if amount == 0 else pltpu.roll(value, amount, axis)


def collide_flow(state, post, velocity, span):
    total, moved = None, [None, None, None]
    for q in range(19):
        value = state[q, :, :, span]
        total = value if total is None else total + value
        for axis in range(3):
            if VELOCITY[q][axis] == 1:
                moved[axis] = value if moved[axis] is None else moved[axis] + value
            elif VELOCITY[q][axis] == -1:
                moved[axis] = -value if moved[axis] is None else moved[axis] - value
    inverse = 1.0 / total
    speed = [part * inverse for part in moved]
    for axis in range(3):
        velocity[axis, :, :, span] = speed[axis]
    base = 1.0 - 1.5 * (speed[0] * speed[0] + speed[1] * speed[1] + speed[2] * speed[2])
    post[1:5, PLACE[0], :, span] = (1.25 / 3.0) * total * base - 0.25 * state[0, :, :, span]
    axial = (1.25 / 18.0) * total
    diagonal = (1.25 / 36.0) * total
    for q in range(1, 19):
        p = OPPOSITE[q]
        if p < q:
            continue
        along = None
        for axis in range(3):
            c = VELOCITY[q][axis]
            if c:
                term = speed[axis] if c == 1 else -speed[axis]
                along = term if along is None else along + term
        even = base + 4.5 * along * along
        odd = 3.0 * along
        scale = axial if q < 7 else diagonal
        post[1:5, PLACE[q], :, span] = scale * (even + odd) - 0.25 * state[q, :, :, span]
        post[1:5, PLACE[p], :, span] = scale * (even - odd) - 0.25 * state[p, :, :, span]


def collide_heat(state, post, velocity, span):
    keep = 1.0 - 1.0 / 0.7
    warmth = state[0, :, :, span]
    for q in range(1, 7):
        warmth = warmth + state[q, :, :, span]
    post[1:5, 0, :, span] = keep * state[0, :, :, span] + (0.25 / 0.7) * warmth
    part = (0.125 / 0.7) * warmth
    for axis in range(3):
        tilt = part * (4.0 * velocity[axis, :, :, span])
        for q in (1 + 2 * axis, 2 + 2 * axis):
            sign = tilt if q == 1 + 2 * axis else -tilt
            post[1:5, q, :, span] = keep * state[q, :, :, span] + (part + sign)


def lifted(value, cz, bounce):
    if cz == 0:
        return value
    layer = sub_of(value.shape)
    if cz == 1:
        return jnp.where(layer == 0, bounce, turn(value, 1, 1))
    return jnp.where(layer == 7, bounce, turn(value, 7, 1))


def stream(post, places, covered, put):
    for q, place in enumerate(places):
        cx, cy, cz = VELOCITY[q]
        value = turn(post[1 - cx : 5 - cx, place], cy, 2)
        bounce = None
        if cz:
            bounce = post[1:5, places[OPPOSITE[q]]]
            if covered is not None and q == 5:
                bounce = jnp.where(covered > 0.5, -bounce, bounce)
        put(q, lifted(value, cz, bounce))


FLOW_PLACES = [PLACE[q] for q in range(19)]
HEAT_PLACES = list(range(7))


def conduct_of(warmth, k):
    return k * (1.0 + 0.5 * warmth)


def fluxes(field, k, low_x, low_xk, high_x, high_xk, gates):
    gate_low_x, gate_high_x, gate_low_y, gate_high_y = gates
    shape = field[0].shape
    lane, layer = lane_of(shape), sub_of(shape)
    cond = [conduct_of(field[x], k[x]) for x in range(2)]
    result = []

    def face(a, ca, b, cb):
        return 2.0 * ca * cb / (ca + cb) * (b - a)

    inner = face(field[0], cond[0], field[1], cond[1])
    for x in range(2):
        here, c = field[x], cond[x]
        if x == 0:
            total = inner + gate_low_x * face(here, c, low_x, conduct_of(low_x, low_xk))
        else:
            total = gate_high_x * face(here, c, high_x, conduct_of(high_x, high_xk)) - inner
        above = face(here, c, turn(here, -1, 1), turn(c, -1, 1))
        below = -turn(above, 1, 1)
        total = total + jnp.where(lane == 127, gate_high_y, 1.0) * above
        total = total + jnp.where(lane == 0, gate_low_y, 1.0) * below
        up = face(here, c, turn(here, 7, 0), turn(c, 7, 0))
        down = -turn(up, 1, 0)
        total = total + jnp.where(layer == 0, 0.0, down) + jnp.where(layer == 7, 0.0, up)
        result.append(total)
    return result


def kernel(
    nx,
    ny,
    f_hbm,
    g_hbm,
    s_hbm,
    m_hbm,
    owner_hbm,
    tally_hbm,
    wall_hbm,
    face_hbm,
    f_out,
    g_out,
    s_out,
    f_in,
    g_in,
    s_in,
    m_in,
    owner_in,
    tally_in,
    wall_in,
    face_in,
    flow,
    heat,
    post_f,
    post_g,
    speeds,
    solid_k,
    solid_low_x,
    solid_high_x,
    solid_low_y,
    solid_high_y,
    columns,
    columns_low,
    columns_high,
    quick,
    got_quick,
    wall_mask,
    covered_ref,
    cell_ref,
    slot_key,
    early,
    got_early,
    late,
    got_late,
    third,
    got_third,
    mid,
    got_mid,
    answer_out,
    got_answer,
    i_sem,
    n_send,
    n_recv,
    g_send,
    g_recv,
):
    arrivals = []
    for n, (source, target) in enumerate(
        (
            (g_hbm, g_in),
            (f_hbm, f_in),
            (s_hbm, s_in),
            (m_hbm, m_in),
            (owner_hbm, owner_in),
            (tally_hbm, tally_in),
            (wall_hbm, wall_in),
            (face_hbm, face_in),
        )
    ):
        made = pltpu.make_async_copy(source, target, i_sem.at[n])
        made.start()
        arrivals.append(made)

    i, j = lax.axis_index("gx"), lax.axis_index("gy")
    right, left = lax.rem(i + 1, nx), lax.rem(i + nx - 1, nx)
    upper, lower = lax.rem(j + 1, ny), lax.rem(j + ny - 1, ny)
    barrier = pltpu.get_barrier_semaphore()
    for device in ((right, j), (left, j)):
        pl.semaphore_signal(barrier, inc=1, device_id=device, device_id_type=MESH)

    @pl.loop(1, ny)
    def _(o):
        pl.semaphore_signal(barrier, inc=1, device_id=(i, lax.rem(j + o, ny)), device_id_type=MESH)

    sent = []

    def copy(source, target, device, goes=None, comes=None):
        n = len(sent)
        made = pltpu.make_async_remote_copy(
            src_ref=source,
            dst_ref=target,
            send_sem=n_send.at[n],
            recv_sem=n_recv.at[n],
            device_id=device,
            device_id_type=MESH,
        )
        if goes is None:
            made.start()
        else:
            pl.when(goes)(made.start)
        sent.append((made, goes))
        return made, comes

    def settle(copies):
        for made, comes in copies:
            if comes is None:
                made.wait_recv()
            else:
                pl.when(comes)(made.wait_recv)

    def to_right(source, target):
        return copy(source, target, (right, j), i < nx - 1, i > 0)

    def to_left(source, target):
        return copy(source, target, (left, j), i > 0, i < nx - 1)

    def send_flow(t):
        return [
            copy(post_f.at[t, 4, pl.ds(0, 5)], post_f.at[t, 0, pl.ds(0, 5)], (right, j)),
            copy(post_f.at[t, 1, pl.ds(5, 5)], post_f.at[t, 5, pl.ds(5, 5)], (left, j)),
        ]

    def send_heat(t):
        return [
            copy(post_g.at[t, 4, 1], post_g.at[t, 0, 1], (right, j)),
            copy(post_g.at[t, 1, 2], post_g.at[t, 5, 2], (left, j)),
        ]

    def send_solid(r, lanes):
        return [
            to_right(solid_k.at[2 * r + 1, :, lanes], solid_low_x.at[r, :, lanes]),
            to_left(solid_k.at[2 * r, :, lanes], solid_high_x.at[r, :, lanes]),
        ]

    def to_all(source, target, pair, personal):
        @pl.loop(0, ny - 1)
        def _(s):
            pltpu.make_async_remote_copy(
                src_ref=source.at[s] if personal else source.at[0],
                dst_ref=target.at[ny - 2 - s],
                send_sem=g_send.at[pair],
                recv_sem=g_recv.at[pair],
                device_id=(i, lax.rem(j + 2 * ny - 1 - s, ny)),
                device_id_type=MESH,
            ).start()

        target[ny - 1] = source[ny - 1 if personal else 0]

    def from_all(target, pair):
        span = pl.ds(0, ny - 1)
        pltpu.make_async_copy(target.at[span], target.at[span], g_recv.at[pair]).wait()

    def all_sent(target, pair):
        span = pl.ds(0, ny - 1)
        pltpu.make_async_copy(target.at[span], target.at[span], g_send.at[pair]).wait()

    here, beyond, whole = pl.ds(0, 128), pl.ds(128, 128), pl.ds(0, 256)

    for n in (2, 3):
        arrivals[n].wait()
    for x in range(2):
        solid_k[x, :, here] = s_in[pl.ds(x, 8, stride=2), :]
        solid_k[6 + x, :, here] = 0.2 + 0.8 * m_in[pl.ds(x, 8, stride=2), :].astype(F32)
    solid_0 = [solid_k[x, :, here] for x in range(2)]
    k_here = [solid_k[6 + x, :, here] for x in range(2)]
    pl.semaphore_wait(barrier, ny - 1 + 2)
    solid_x_halo = send_solid(0, here) + send_solid(3, here)

    square = (128, 128)
    lane, sub = lane_of(square), sub_of(square)
    lane_8, sub_8 = lane_of((8, 128)), sub_of((8, 128))
    lane_32, sub_32 = lane_of((32, 128)), sub_of((32, 128))
    row_lane = lane_of((1, 128))
    diagonal = lane == sub

    def column(row):
        return jnp.sum(jnp.where(diagonal, jnp.broadcast_to(row, square), 0.0), axis=1, keepdims=True)

    def as_row(col):
        return jnp.sum(jnp.where(diagonal, jnp.broadcast_to(col, square), 0.0), axis=0, keepdims=True)

    for n in (4, 5, 6, 7):
        arrivals[n].wait()
    owner = owner_in[...]
    face_index = face_in[...]
    wall = wall_in[...]
    live = lane_of((1, 128)) < jnp.broadcast_to(tally_in[...], (1, 128))
    block = (j - owner - 1) & (ny - 1)
    cell_row = jnp.where(live, owner * 256 + face_index, -1).astype(F32)
    cell_col = column(cell_row)
    live_col = column(jnp.where(live, 1.0, 0.0))
    block_row = block.astype(F32)
    block_col = column(block_row)
    face_col = column(face_index.astype(F32))
    wall_y_col = column((wall & 127).astype(F32))
    wall_x_col = column((wall >> 7).astype(F32))
    rank_col = jnp.sum(
        jnp.where((jnp.broadcast_to(block_row, square) == block_col) & (lane < sub), 1.0, 0.0),
        axis=1,
        keepdims=True,
    )
    lane_f = lane.astype(F32)
    wall_hit = jnp.where(lane_f == wall_y_col, live_col, 0.0)
    for x in range(4):
        wall_mask[x] = jnp.where(wall_x_col == float(x), wall_hit, 0.0)
    slot_key[...] = jnp.where((lane & 7).astype(F32) == rank_col, jnp.broadcast_to(live_col, square), 0.0)
    to_owner = jnp.where(jnp.broadcast_to(block_row, (32, 128)) == sub_32.astype(F32), 1.0, 0.0)

    def at_wall(rows):
        total = wall_mask[0] * rows[0]
        for x in range(1, 4):
            total = total + wall_mask[x] * rows[x]
        return jnp.sum(total, axis=1, keepdims=True)

    def on_wall(col):
        return [jnp.sum(wall_mask[x] * col, axis=0, keepdims=True) for x in range(4)]

    def slots(first, second):
        fields = jnp.where(lane < 8, first, jnp.where(lane < 16, second, 0.0))
        return jnp.dot(
            to_owner, fields * slot_key[...], precision=lax.Precision.HIGHEST, preferred_element_type=F32
        )

    def fill(buffer, n, value):
        buffer[:, n, :] = jnp.broadcast_to(value, (32, 128))

    arrivals[0].wait()
    for q in range(7):
        for x in range(4):
            heat[q, x, :, here] = g_in[q, pl.ds(x, 8, stride=4), :]

    def wall_sums():
        total = heat[0, :, 0:1, here]
        for q in range(1, 7):
            total = total + heat[q, :, 0:1, here]
        return [total[x] for x in range(4)]

    t1_col = at_wall(wall_sums())
    fill(early, 0, cell_row)
    fill(early, 1, as_row(t1_col))
    early[:, 2, :] = slots(t1_col, face_col + 1.0)
    k_top = [k_here[x][7:8] for x in range(2)]
    k_inner = jnp.where(row_lane == 1, turn(k_top[1], 1, 1), turn(k_top[1], 127, 1))
    fill(early, 3, jnp.where((row_lane == 0) | (row_lane == 127), k_top[0], k_inner))
    for x in range(2):
        fill(early, 4 + x, solid_0[x][7:8])
    to_all(early, got_early, 0, True)

    arrivals[1].wait()
    for q in range(19):
        for x in range(4):
            flow[q, x, :, here] = f_in[q, pl.ds(x, 8, stride=4), :]
    named = on_wall(cell_col + 1.0)
    named_8 = jnp.zeros((8, 128), F32)
    for x in range(4):
        named_8 = jnp.where((sub_8 & 3) == x, named[x], named_8)
    units = [(flow, q, x) for q in range(19) for x in range(4)] + [(heat, q, x) for q in range(7) for x in range(4)]
    for tile in range(5):
        packed = jnp.zeros((8, 128), F32)
        for n in range(21):
            place = 21 * tile + n
            value = named_8
            if place < len(units):
                ref, q, x = units[place]
                value = ref[q, x, :, here]
            packed = jnp.where((lane_8 >= 6 * n) & (lane_8 < 6 * n + 6), turn(value, 6 * n + 3, 1), packed)
        columns[tile] = packed
    column_halo = [copy(columns, columns_low, (i, upper)), copy(columns, columns_high, (i, lower))]
    both = [solid_k.at[pl.ds(0, 2), :, here], solid_k.at[pl.ds(6, 2), :, here]]
    solid_y_halo = [
        made
        for n, part in enumerate(both)
        for made in (copy(part, solid_low_y.at[n], (i, upper)), copy(part, solid_high_y.at[n], (i, lower)))
    ]

    collide_flow(flow, post_f.at[0], speeds.at[0], here)
    collide_heat(heat, post_g.at[0], speeds.at[0], here)
    up = down = jnp.zeros((1, 128), F32)
    for x in range(4):
        up = jnp.where(row_lane == x, turn(post_g[0, x + 1, 3, 0:1, here], x + 1, 1), up)
        down = jnp.where(row_lane == x, turn(post_g[0, x + 1, 4, 0:1, here], x, 1), down)
    quick[0], quick[1] = up, down
    quick[2], quick[3] = post_g[0, 4, 1, 0:1, here], post_g[0, 1, 2, 0:1, here]
    quick_halo = [
        copy(quick.at[0], got_quick.at[0], (i, upper)),
        copy(quick.at[1], got_quick.at[1], (i, lower)),
        copy(quick.at[2], got_quick.at[2], (right, j)),
        copy(quick.at[3], got_quick.at[3], (left, j)),
    ]

    gates_x = (jnp.where(i == 0, 0.0, 1.0), jnp.where(i == nx - 1, 0.0, 1.0))
    gates_y = (jnp.where(j == 0, 0.0, 1.0), jnp.where(j == ny - 1, 0.0, 1.0))

    def conduct(field, r, k, span, y_gates):
        change = fluxes(
            field,
            k,
            jnp.where(i > 0, solid_low_x[r, :, span], field[0]),
            jnp.where(i > 0, solid_low_x[3, :, span], k[0]),
            jnp.where(i < nx - 1, solid_high_x[r, :, span], field[1]),
            jnp.where(i < nx - 1, solid_high_x[3, :, span], k[1]),
            gates_x + y_gates,
        )
        return [field[x] + DT * change[x] for x in range(2)]

    settle(solid_x_halo)
    inner_1 = conduct(solid_0, 0, k_here, here, (0.0, 0.0))
    for x in range(2):
        late[0, x : x + 1, :] = inner_1[x][7:8]
    to_all(late, got_late, 1, False)

    for x in range(4):
        covered_ref[x, :, here] = jnp.broadcast_to(jnp.sum(wall_mask[x], axis=0, keepdims=True), (8, 128))
    settle(quick_halo)
    rest_rows = []
    for x in range(4):
        post = lambda q, at=x: post_g[0, at + 1, q, 0:1, here]
        total = post(0) + (post_g[0, x, 1, 0:1, here] if x else got_quick[2])
        total = total + (post_g[0, x + 2, 2, 0:1, here] if x < 3 else got_quick[3])
        total = total + jnp.where(row_lane == 0, turn(got_quick[0], 128 - x, 1), turn(post(3), 1, 1))
        total = total + jnp.where(row_lane == 127, turn(got_quick[1], 127 - x, 1), turn(post(4), 127, 1))
        wall_post = post(6)
        total = total + jnp.where(covered_ref[x, 0:1, here] > 0.5, -wall_post, wall_post)
        rest_rows.append(total + post_g[0, x + 1, 6, 1:2, here])
    a2_col = at_wall(rest_rows)
    third[:, 0, :] = slots(a2_col, 0.0)
    fill(third, 1, as_row(a2_col))
    to_all(third, got_third, 2, True)

    settle(solid_y_halo)
    for x in range(2):
        for n, at in ((0, 0), (1, 6)):
            solid_k[at + x, :, beyond] = jnp.where(lane_8 < 64, solid_high_y[n, x], solid_low_y[n, x])
    solid_x_halo = send_solid(0, beyond) + send_solid(3, beyond)
    settle(column_halo)
    named_beyond = None
    for tile in range(5):
        low, high = columns_low[tile], columns_high[tile]
        for n in range(21):
            place = 21 * tile + n
            value = jnp.where(lane_8 < 64, turn(high, 125 - 6 * n, 1), turn(low, 125 - 6 * n, 1))
            if place < len(units):
                ref, q, x = units[place]
                ref[q, x, :, beyond] = value
            else:
                named_beyond = value
    collide_flow(flow, post_f.at[0], speeds.at[0], beyond)
    collide_heat(heat, post_g.at[0], speeds.at[0], beyond)
    heat_halo = send_heat(0)
    flow_halo = send_flow(0)
    for x in range(4):
        covered_ref[x, :, beyond] = jnp.where(jnp.broadcast_to(named_beyond[x : x + 1], (8, 128)) > 0.5, 1.0, 0.0)
    halo_lanes = (126, 127, 0, 1)
    halo_cells = [
        jnp.sum(
            jnp.where(lane_8 == jnp.where(sub_8 < 4, halo_lanes[n], halo_lanes[n + 1]), named_beyond, 0.0),
            axis=1,
            keepdims=True,
        )
        - 1.0
        for n in (0, 2)
    ]
    rows_col = jnp.concatenate([cell_col] + halo_cells, axis=0)
    cell_ref[...] = jnp.broadcast_to(rows_col, (144, 128))
    rows_cell = cell_ref[...].astype(jnp.int32)
    lane_144 = lane_of((144, 128))
    face_hit = jnp.where(lane_144 == (rows_cell & 127), 1.0, 0.0)
    rows_place = ((j - (rows_cell >> 8) - 1) & 31) + 32 * ((rows_cell >> 7) & 1)
    pick = jnp.where(lane_144 == rows_place, 1.0, 0.0)[:, 0:64]

    def put_heat(q, value):
        heat[q] = value

    def put_flow(q, value):
        flow[q] = value

    settle(heat_halo)
    stream(post_g.at[0], HEAT_PLACES, covered_ref[...], put_heat)
    settle(flow_halo)
    stream(post_f.at[0], FLOW_PLACES, None, put_flow)
    collide_flow(flow, post_f.at[1], speeds.at[1], whole)
    flow_halo = send_flow(1)

    settle(solid_x_halo)
    k = [solid_k[6 + x] for x in range(2)]
    field_0 = [solid_k[x] for x in range(2)]
    p1 = conduct(field_0, 0, k, whole, gates_y)

    from_all(got_early, 0)

    def slot_columns(value, field):
        return [
            jnp.broadcast_to(
                jnp.sum(jnp.where(lane_32 == 8 * field + c, value, 0.0), axis=1, keepdims=True), (32, 128)
            )
            for c in range(CAP)
        ]

    faces = slot_columns(got_early[:, 2, :], 1)

    def own_sums(fields):
        result = []
        for x in range(2):
            place = (lane_32 + (128 * x + 1)).astype(F32)
            totals = [jnp.zeros((32, 128), F32) for _ in fields]
            for c in range(CAP):
                hit = faces[c] == place
                for n, field in enumerate(fields):
                    totals[n] = totals[n] + jnp.where(hit, 1.0 if field is None else field[c], 0.0)
            result.append([jnp.sum(total, axis=0, keepdims=True) for total in totals])
        return result

    def halo_sums(fields):
        cells = got_early[:, 0, :]
        result = []
        for x in range(2):
            rows = [jnp.zeros((1, 128), F32) for _ in fields]
            for at in halo_lanes:
                there = (j + (1 if at < 64 else -1)) * 256 + 128 * x + at
                hit = cells == jnp.full((32, 128), there, jnp.int32).astype(F32)
                for n, field in enumerate(fields):
                    total = jnp.sum(jnp.where(hit, 1.0 if field is None else field, 0.0), axis=0, keepdims=True)
                    total = jnp.sum(total, axis=1, keepdims=True)
                    rows[n] = jnp.where(row_lane == at, total, rows[n])
            result.append(rows)
        return result

    def joined(own, halo):
        return [
            [jnp.concatenate([a, b], axis=1) for a, b in zip(own[x], halo[x])] for x in range(2)
        ]

    top_256 = sub_of((8, 256)) == 7

    def on_top(value, row):
        return value + jnp.where(top_256, jnp.broadcast_to(row, (8, 256)), 0.0)

    sums = joined(
        own_sums([slot_columns(got_early[:, 2, :], 0), None]), halo_sums([got_early[:, 1, :], None])
    )
    many = [sums[x][1] for x in range(2)]
    solid_1 = [on_top(p1[x], DT * (sums[x][0] - many[x] * field_0[x][7:8])) for x in range(2)]
    for x in range(2):
        solid_k[2 + x] = solid_1[x]
    solid_halo = send_solid(1, whole)

    def same_cell(ref, n, count, many_rows):
        cells = cell_ref[0:many_rows]

        def body(b, carry):
            hit = cells == got_early[b, 0:1, :]
            total = carry[0] + jnp.where(hit, ref[b, n : n + 1, :], 0.0)
            if count:
                return total, carry[1] + jnp.where(hit, 1.0, 0.0)
            return (total,)

        zero = jnp.zeros((many_rows, 128), F32)
        return lax.fori_loop(0, ny, body, (zero, zero) if count else (zero,))

    total_1, number = same_cell(got_early, 1, True, 144)
    number_col = jnp.sum(number, axis=1, keepdims=True)
    edge_k = got_early[:, 3, :]
    crossing = []
    for x in range(2):
        inside = got_early[:, 4 + x, :]
        inside_k = edge_k if x == 0 else jnp.where(lane_32 == 0, turn(edge_k, 127, 1), turn(edge_k, 1, 1))
        outside, outside_k = (turn(turn(part, 1, 0), 127, 1) for part in (inside, inside_k))
        c, cb = conduct_of(inside, inside_k), conduct_of(outside, outside_k)
        rise = 2.0 * c * cb / (c + cb) * (outside - inside)
        rise = jnp.where((lane_32 == 127) & (sub_32 != j), rise, 0.0)
        crossing.append(DT * (rise - turn(turn(rise, 31, 0), 1, 1)))

    from_all(got_late, 1)
    surfaces = jnp.concatenate(
        [
            jnp.concatenate([got_late[:, x, :] + crossing[x] for x in range(2)], axis=0),
            jnp.concatenate([got_early[:, 4 + x, :] for x in range(2)], axis=0),
        ],
        axis=1,
    )
    picked = jnp.dot(pick, surfaces, precision=lax.Precision.HIGHEST, preferred_element_type=F32)
    w1_col = jnp.sum(
        face_hit * (picked[:, 0:128] - DT * number_col * picked[:, 128:256]) + DT * total_1,
        axis=1,
        keepdims=True,
    )

    def warm_wall(col):
        rows = on_wall(col[0:128])
        for x in range(4):
            outer = jnp.zeros((1, 128), F32)
            for n, at in enumerate(halo_lanes):
                outer = jnp.where(row_lane == at, col[128 + 4 * n + x : 129 + 4 * n + x], outer)
            outer = jnp.where(covered_ref[x, 0:1, beyond] > 0.5, outer, 0.0)
            heat[5, x, 0:1, here] = heat[5, x, 0:1, here] + 0.25 * rows[x]
            heat[5, x, 0:1, beyond] = heat[5, x, 0:1, beyond] + 0.25 * outer

    warm_wall(w1_col)
    collide_heat(heat, post_g.at[1], speeds.at[1], whole)
    heat_halo = send_heat(1)

    from_all(got_third, 2)
    rest = joined(own_sums([slot_columns(got_third[:, 0, :], 0)]), halo_sums([got_third[:, 1, :]]))
    settle(solid_halo)
    solid_2 = conduct(solid_1, 1, k, whole, gates_y)
    solid_2 = [
        on_top(solid_2[x], DT * (rest[x][0] - 0.75 * many[x] * solid_1[x][7:8])) for x in range(2)
    ]
    for x in range(2):
        solid_k[4 + x] = solid_2[x]
        fill(mid, 2 + x, solid_2[x][7:8, 0:128])
    solid_halo = send_solid(2, whole)

    settle(heat_halo)
    stream(post_g.at[1], HEAT_PLACES, covered_ref[...], put_heat)
    a3_col = at_wall(wall_sums())
    fill(mid, 0, as_row(a3_col))
    mid[:, 1, :] = slots(a3_col, 0.0)
    to_all(mid, got_mid, 3, True)

    settle(solid_halo)
    p3 = conduct(solid_2, 2, k, whole, gates_y)
    p3 = [on_top(p3[x], (-0.75 * DT) * many[x] * solid_2[x][7:8])[:, 0:128] for x in range(2)]
    answer = jnp.zeros((32, 128), F32)
    for c in range(CAP):
        first = faces[c] == (lane_32 + 1).astype(F32)
        second = faces[c] == (lane_32 + 129).astype(F32)
        at_cell = jnp.where(first, p3[0][7:8], jnp.where(second, p3[1][7:8], 0.0))
        answer = jnp.where(lane_32 == c, jnp.sum(at_cell, axis=1, keepdims=True), answer)
    answer_out[:, 0, :] = answer
    to_all(answer_out, got_answer, 4, True)

    settle(flow_halo)
    stream(post_f.at[1], FLOW_PLACES, None, put_flow)
    collide_flow(flow, post_f.at[2], speeds.at[2], whole)
    flow_halo = send_flow(2)

    from_all(got_mid, 3)
    surfaces = jnp.concatenate([got_mid[:, 2 + x, :] for x in range(2)], axis=0)
    picked = jnp.dot(pick, surfaces, precision=lax.Precision.HIGHEST, preferred_element_type=F32)
    w2_col = jnp.sum(face_hit * picked, axis=1, keepdims=True)
    warm_wall(w2_col)
    collide_heat(heat, post_g.at[2], speeds.at[2], whole)
    heat_halo = send_heat(2)

    (total_3,) = same_cell(got_mid, 0, False, 128)
    last = own_sums([slot_columns(got_mid[:, 1, :], 0)])
    for x in range(2):
        s_out[pl.ds(x, 8, stride=2), :] = p3[x] + jnp.where(sub_8 == 7, DT * last[x][0], 0.0)

    settle(flow_halo)

    def write_flow(q, value):
        for x in range(4):
            f_out[q, pl.ds(x, 8, stride=4), :] = value[x, :, 0:128]

    stream(post_f.at[2], FLOW_PLACES, None, write_flow)

    from_all(got_answer, 4)
    pick_owner = jnp.where(lane_of((128, 32)).astype(F32) == block_col, 1.0, 0.0)
    found = jnp.dot(pick_owner, got_answer[:, 0, :], precision=lax.Precision.HIGHEST, preferred_element_type=F32)
    w3_col = jnp.sum(jnp.where(lane_f == rank_col, found, 0.0) + DT * total_3, axis=1, keepdims=True)
    w3_rows = on_wall(w3_col)

    settle(heat_halo)

    def write_heat(q, value):
        for x in range(4):
            row = value[x, :, 0:128]
            if q == 5:
                row = row + jnp.where(sub_8 == 0, 0.25 * w3_rows[x], 0.0)
            g_out[q, pl.ds(x, 8, stride=4), :] = row

    stream(post_g.at[2], HEAT_PLACES, covered_ref[...], write_heat)

    for n, target in enumerate((got_early, got_late, got_third, got_mid, got_answer)):
        all_sent(target, n)
    for made, goes in sent:
        if goes is None:
            made.wait_send()
        else:
            pl.when(goes)(made.wait_send)


def finish(*refs):
    sources, targets, sems = refs[0:3], refs[3:6], refs[6]
    copies = [pltpu.make_async_copy(a, b, sems.at[n]) for n, (a, b) in enumerate(zip(sources, targets))]
    for made in copies:
        made.start()
    for made in copies:
        made.wait()


def on_device(nx, ny, flow, heat, solid, metal, owner, tally, wall, face):
    vmem = functools.partial(pltpu.VMEM, dtype=F32)
    tile, wide = (8, 128), (8, 256)
    copies = 40
    results = (
        jax.ShapeDtypeStruct((19, 32, 128), F32),
        jax.ShapeDtypeStruct((7, 32, 128), F32),
        jax.ShapeDtypeStruct((16, 128), F32),
    )
    out = pl.pallas_call(
        functools.partial(kernel, nx, ny),
        out_shape=tuple(pltpu.VMEM(result.shape, result.dtype) for result in results),
        in_specs=[pl.BlockSpec(memory_space=pltpu.HBM)] * 8,
        out_specs=[pl.BlockSpec(memory_space=pltpu.VMEM)] * 3,
        scratch_shapes=[
            vmem((19, 32, 128)),
            vmem((7, 32, 128)),
            vmem((16, 128)),
            pltpu.VMEM((16, 128), jnp.int32),
            pltpu.VMEM((1, 128), jnp.int32),
            pltpu.VMEM((1, 1), jnp.int32),
            pltpu.VMEM((1, 128), jnp.int32),
            pltpu.VMEM((1, 128), jnp.int32),
            vmem((19, 4) + wide),
            vmem((7, 4) + wide),
            vmem((STEPS, 6, 19) + wide),
            vmem((STEPS, 6, 7) + wide),
            vmem((STEPS, 3, 4) + wide),
            vmem((8,) + wide),
            vmem((4,) + wide),
            vmem((4,) + wide),
            vmem((2, 2) + tile),
            vmem((2, 2) + tile),
            vmem((5,) + tile),
            vmem((5,) + tile),
            vmem((5,) + tile),
            vmem((4, 1, 128)),
            vmem((4, 1, 128)),
            vmem((4, 128, 128)),
            vmem((4,) + wide),
            vmem((144, 128)),
            vmem((128, 128)),
            vmem((32, 6, 128)),
            vmem((32, 6, 128)),
            vmem((1, 2, 128)),
            vmem((32, 2, 128)),
            vmem((32, 2, 128)),
            vmem((32, 2, 128)),
            vmem((32, 4, 128)),
            vmem((32, 4, 128)),
            vmem((32, 1, 128)),
            vmem((32, 1, 128)),
            pltpu.SemaphoreType.DMA((8,)),
            pltpu.SemaphoreType.DMA((copies,)),
            pltpu.SemaphoreType.DMA((copies,)),
            pltpu.SemaphoreType.DMA((5,)),
            pltpu.SemaphoreType.DMA((5,)),
        ],
        compiler_params=pltpu.CompilerParams(
            collective_id=0, has_side_effects=True, vmem_limit_bytes=ROOM
        ),
        name="coupled_steps",
    )(
        flow.reshape(19, 32, 128),
        heat.reshape(7, 32, 128),
        solid.reshape(16, 128),
        metal.reshape(16, 128),
        owner.reshape(1, 128),
        tally,
        wall,
        face,
    )
    out = pl.pallas_call(
        finish,
        out_shape=results,
        in_specs=[pl.BlockSpec(memory_space=pltpu.VMEM)] * 3,
        out_specs=[pl.BlockSpec(memory_space=pltpu.HBM)] * 3,
        scratch_shapes=[pltpu.SemaphoreType.DMA((3,))],
        compiler_params=pltpu.CompilerParams(vmem_limit_bytes=1024 * 1024),
        name="write_out",
    )(*out)
    return out[0].reshape(19, 8, 4, 128), out[1].reshape(7, 8, 4, 128), out[2].reshape(8, 2, 128)


def solution(mesh):
    placed = (
        P(None, None, "gx", "gy"),
        P(None, None, "gx", "gy"),
        P(None, "gx", "gy"),
        P(None, "gx", "gy"),
        P("gx", "gy", None),
        P("gx", "gy"),
        P("gx", "gy"),
        P("gx", "gy"),
    )
    return jax.shard_map(
        functools.partial(on_device, mesh.shape["gx"], mesh.shape["gy"]),
        mesh=mesh,
        in_specs=placed,
        out_specs=(P(None, None, "gx", "gy"), P(None, None, "gx", "gy"), P(None, "gx", "gy")),
        check_vma=False,
    )
```

```python
import functools

import jax
import jax.numpy as jnp
from jax import lax
from jax.experimental import pallas as pl
from jax.experimental.pallas import tpu as pltpu
from jax.sharding import PartitionSpec as P

MESH = pl.DeviceIdType.MESH
F32 = jnp.float32
STEPS = 3
CAP = 8

VELOCITY = [
    (0, 0, 0),
    (1, 0, 0),
    (-1, 0, 0),
    (0, 1, 0),
    (0, -1, 0),
    (0, 0, 1),
    (0, 0, -1),
    (1, 1, 0),
    (-1, -1, 0),
    (1, -1, 0),
    (-1, 1, 0),
    (1, 0, 1),
    (-1, 0, -1),
    (1, 0, -1),
    (-1, 0, 1),
    (0, 1, 1),
    (0, -1, -1),
    (0, 1, -1),
    (0, -1, 1),
]
OPPOSITE = [VELOCITY.index((-a, -b, -c)) for a, b, c in VELOCITY]
ORDER = [1, 7, 9, 11, 13, 2, 8, 10, 12, 14, 0, 3, 4, 5, 6, 15, 16, 17, 18]
PLACE = {q: n for n, q in enumerate(ORDER)}
DT = 0.04
ROOM = 63 * 1024 * 1024


def lane_of(shape):
    return lax.broadcasted_iota(jnp.int32, shape, len(shape) - 1)


def sub_of(shape):
    return lax.broadcasted_iota(jnp.int32, shape, len(shape) - 2)


def turn(value, amount, axis):
    size = value.shape[axis]
    amount = amount % size
    return value if amount == 0 else pltpu.roll(value, amount, axis)


def collide_flow(state, post, velocity, span):
    total, moved = None, [None, None, None]
    for q in range(19):
        value = state[q, :, :, span]
        total = value if total is None else total + value
        for axis in range(3):
            if VELOCITY[q][axis] == 1:
                moved[axis] = value if moved[axis] is None else moved[axis] + value
            elif VELOCITY[q][axis] == -1:
                moved[axis] = -value if moved[axis] is None else moved[axis] - value
    inverse = 1.0 / total
    speed = [part * inverse for part in moved]
    for axis in range(3):
        velocity[axis, :, :, span] = speed[axis]
    base = 1.0 - 1.5 * (speed[0] * speed[0] + speed[1] * speed[1] + speed[2] * speed[2])
    post[1:5, PLACE[0], :, span] = (1.25 / 3.0) * total * base - 0.25 * state[0, :, :, span]
    axial = (1.25 / 18.0) * total
    diagonal = (1.25 / 36.0) * total
    for q in range(1, 19):
        p = OPPOSITE[q]
        if p < q:
            continue
        along = None
        for axis in range(3):
            c = VELOCITY[q][axis]
            if c:
                term = speed[axis] if c == 1 else -speed[axis]
                along = term if along is None else along + term
        even = base + 4.5 * along * along
        odd = 3.0 * along
        scale = axial if q < 7 else diagonal
        post[1:5, PLACE[q], :, span] = scale * (even + odd) - 0.25 * state[q, :, :, span]
        post[1:5, PLACE[p], :, span] = scale * (even - odd) - 0.25 * state[p, :, :, span]


def collide_heat(state, post, velocity, span, x_done=None):
    keep = 1.0 - 1.0 / 0.7
    warmth = state[0, :, :, span]
    for q in range(1, 7):
        warmth = warmth + state[q, :, :, span]
    part = (0.125 / 0.7) * warmth
    for axis in range(3):
        tilt = part * (4.0 * velocity[axis, :, :, span])
        for q in (1 + 2 * axis, 2 + 2 * axis):
            sign = tilt if q == 1 + 2 * axis else -tilt
            post[1:5, q, :, span] = keep * state[q, :, :, span] + (part + sign)
        if axis == 0 and x_done is not None:
            x_done()
    post[1:5, 0, :, span] = keep * state[0, :, :, span] + (0.25 / 0.7) * warmth


def pick_rows(pick, value):
    parts, rest = [], value
    for _ in range(3):
        parts.append(rest.astype(jnp.bfloat16))
        rest = rest - parts[-1].astype(F32)
    found = jnp.dot(
        pick.astype(jnp.bfloat16), jnp.concatenate(parts, axis=1), preferred_element_type=F32
    )
    width = value.shape[1]
    return found[:, 0:width] + (found[:, width : 2 * width] + found[:, 2 * width :])


def lifted(value, cz, bounce):
    if cz == 0:
        return value
    layer = sub_of(value.shape)
    if cz == 1:
        return jnp.where(layer == 0, bounce, turn(value, 1, 1))
    return jnp.where(layer == 7, bounce, turn(value, 7, 1))


def stream(post, places, covered, put):
    for q, place in enumerate(places):
        cx, cy, cz = VELOCITY[q]
        value = turn(post[1 - cx : 5 - cx, place], cy, 2)
        bounce = None
        if cz:
            bounce = post[1:5, places[OPPOSITE[q]]]
            if covered is not None and q == 5:
                bounce = jnp.where(covered > 0.5, -bounce, bounce)
        put(q, lifted(value, cz, bounce))


FLOW_PLACES = [PLACE[q] for q in range(19)]
HEAT_PLACES = list(range(7))


def conduct_of(warmth, k):
    return k * (1.0 + 0.5 * warmth)


def fluxes(field, k, low_x, low_xk, high_x, high_xk, gates):
    gate_low_x, gate_high_x, gate_low_y, gate_high_y = gates
    shape = field[0].shape
    lane, layer = lane_of(shape), sub_of(shape)
    cond = [conduct_of(field[x], k[x]) for x in range(2)]
    result = []

    def face(a, ca, b, cb):
        return 2.0 * ca * cb / (ca + cb) * (b - a)

    inner = face(field[0], cond[0], field[1], cond[1])
    for x in range(2):
        here, c = field[x], cond[x]
        if x == 0:
            total = inner + gate_low_x * face(here, c, low_x, conduct_of(low_x, low_xk))
        else:
            total = gate_high_x * face(here, c, high_x, conduct_of(high_x, high_xk)) - inner
        above = face(here, c, turn(here, -1, 1), turn(c, -1, 1))
        below = -turn(above, 1, 1)
        total = total + jnp.where(lane == 127, gate_high_y, 1.0) * above
        total = total + jnp.where(lane == 0, gate_low_y, 1.0) * below
        up = face(here, c, turn(here, 7, 0), turn(c, 7, 0))
        down = -turn(up, 1, 0)
        total = total + jnp.where(layer == 0, 0.0, down) + jnp.where(layer == 7, 0.0, up)
        result.append(total)
    return result


def kernel(
    nx,
    ny,
    f_hbm,
    g_hbm,
    s_hbm,
    m_hbm,
    owner_hbm,
    tally_hbm,
    wall_hbm,
    face_hbm,
    f_out,
    g_out,
    s_out,
    f_in,
    g_in,
    s_in,
    m_in,
    owner_in,
    tally_in,
    wall_in,
    face_in,
    flow,
    heat,
    post_f,
    post_g,
    speeds,
    solid_k,
    solid_low_x,
    solid_high_x,
    solid_low_y,
    solid_high_y,
    columns,
    columns_low,
    columns_high,
    quick,
    got_quick,
    wall_mask,
    covered_ref,
    cell_ref,
    slot_key,
    early,
    near_early,
    got_early,
    late,
    near_late,
    got_late,
    third,
    near_third,
    got_third,
    mid,
    got_mid,
    answer_out,
    got_answer,
    i_sem,
    n_send,
    n_recv,
    g_send,
    g_recv,
):
    arrivals = []
    for n, (source, target) in enumerate(
        (
            (g_hbm, g_in),
            (f_hbm, f_in),
            (s_hbm, s_in),
            (m_hbm, m_in),
            (owner_hbm, owner_in),
            (tally_hbm, tally_in),
            (wall_hbm, wall_in),
            (face_hbm, face_in),
        )
    ):
        made = pltpu.make_async_copy(source, target, i_sem.at[n])
        made.start()
        arrivals.append(made)

    i, j = lax.axis_index("gx"), lax.axis_index("gy")
    right, left = lax.rem(i + 1, nx), lax.rem(i + nx - 1, nx)
    upper, lower = lax.rem(j + 1, ny), lax.rem(j + ny - 1, ny)
    along = ny // 4
    y = lax.rem(j // 2, along)
    corner = j // (2 * along) * 2 + lax.rem(j, 2)

    def seat(corner_there, y_there):
        return corner_there // 2 * (2 * along) + 2 * y_there + lax.rem(corner_there, 2)

    barrier = pltpu.get_barrier_semaphore()
    greeted = [(i, seat(lax.rem(corner + d, 4), y)) for d in (2, 3, 1)]
    greeted += [(i, seat(corner, lax.rem(y + d, along))) for d in (4, 3, 5, 2, 6, 1, 7)]
    greeted += [(right, j), (left, j), (i, upper), (i, lower)]
    for device in greeted:
        pl.semaphore_signal(barrier, inc=1, device_id=device, device_id_type=MESH)

    sent = []

    def copy(source, target, device, goes=None, comes=None):
        n = len(sent)
        made = pltpu.make_async_remote_copy(
            src_ref=source,
            dst_ref=target,
            send_sem=n_send.at[n],
            recv_sem=n_recv.at[n],
            device_id=device,
            device_id_type=MESH,
        )
        if goes is None:
            made.start()
        else:
            pl.when(goes)(made.start)
        sent.append((made, goes))
        return made, comes

    def settle(copies):
        for made, comes in copies:
            if comes is None:
                made.wait_recv()
            else:
                pl.when(comes)(made.wait_recv)

    def to_right(source, target):
        return copy(source, target, (right, j), i < nx - 1, i > 0)

    def to_left(source, target):
        return copy(source, target, (left, j), i > 0, i < nx - 1)

    def send_flow(t):
        return [
            copy(post_f.at[t, 4, pl.ds(0, 5)], post_f.at[t, 0, pl.ds(0, 5)], (right, j)),
            copy(post_f.at[t, 1, pl.ds(5, 5)], post_f.at[t, 5, pl.ds(5, 5)], (left, j)),
        ]

    def send_heat(t):
        return [
            copy(post_g.at[t, 4, 1], post_g.at[t, 0, 1], (right, j)),
            copy(post_g.at[t, 1, 2], post_g.at[t, 5, 2], (left, j)),
        ]

    def send_solid(r, lanes):
        return [
            to_right(solid_k.at[2 * r + 1, :, lanes], solid_low_x.at[r, :, lanes]),
            to_left(solid_k.at[2 * r, :, lanes], solid_high_x.at[r, :, lanes]),
        ]

    def round_first(source, near, pair, personal):
        for d in (2, 3, 1):
            there = lax.rem(corner + d, 4)
            pltpu.make_async_remote_copy(
                src_ref=source.at[there] if personal else source.at[0],
                dst_ref=near.at[corner],
                send_sem=g_send.at[pair],
                recv_sem=g_recv.at[pair],
                device_id=(i, seat(there, y)),
                device_id_type=MESH,
            ).start()
        near[corner] = source[corner] if personal else source[0]

    def round_second(near, target, pair):
        got_bytes(target, 3, pair)
        for d in (4, 3, 5, 2, 6, 1, 7):
            for half in range(2):
                pltpu.make_async_remote_copy(
                    src_ref=near.at[pl.ds(2 * half, 2)],
                    dst_ref=target.at[pl.ds(2 * along * half + 2 * y, 2)],
                    send_sem=g_send.at[pair + 1],
                    recv_sem=g_recv.at[pair + 1],
                    device_id=(i, seat(corner, lax.rem(y + d, along))),
                    device_id_type=MESH,
                ).start()
        for half in range(2):
            for c in range(2):
                target[2 * along * half + 2 * y + c] = near[2 * half + c]

    def to_all(source, target, pair):
        @pl.loop(0, ny - 1)
        def _(o):
            there = lax.rem(j + 1 + lax.rem(o + ny // 2 - 1, ny - 1), ny)
            pltpu.make_async_remote_copy(
                src_ref=source.at[there],
                dst_ref=target.at[j],
                send_sem=g_send.at[pair],
                recv_sem=g_recv.at[pair],
                device_id=(i, there),
                device_id_type=MESH,
            ).start()

        target[j] = source[j]

    def got_bytes(target, blocks, pair):
        span = pl.ds(0, blocks)
        pltpu.make_async_copy(target.at[span], target.at[span], g_recv.at[pair]).wait()

    def sent_bytes(target, blocks, pair):
        span = pl.ds(0, blocks)
        pltpu.make_async_copy(target.at[span], target.at[span], g_send.at[pair]).wait()

    here, beyond, whole = pl.ds(0, 128), pl.ds(128, 128), pl.ds(0, 256)

    for n in (2, 3):
        arrivals[n].wait()
    for x in range(2):
        solid_k[x, :, here] = s_in[pl.ds(x, 8, stride=2), :]
        solid_k[6 + x, :, here] = 0.2 + 0.8 * m_in[pl.ds(x, 8, stride=2), :].astype(F32)
    solid_0 = [solid_k[x, :, here] for x in range(2)]
    k_here = [solid_k[6 + x, :, here] for x in range(2)]
    pl.semaphore_wait(barrier, len(greeted))
    solid_x_halo = send_solid(0, here) + send_solid(3, here)

    lane_8, sub_8 = lane_of((8, 128)), sub_of((8, 128))
    arrivals[0].wait()
    for q in range(7):
        for x in range(4):
            heat[q, x, :, here] = g_in[q, pl.ds(x, 8, stride=4), :]
    arrivals[1].wait()
    for q in range(19):
        for x in range(4):
            flow[q, x, :, here] = f_in[q, pl.ds(x, 8, stride=4), :]
    units = [(flow, q, x) for q in range(19) for x in range(4)] + [(heat, q, x) for q in range(7) for x in range(4)]
    for tile in range(5):
        packed = jnp.zeros((8, 128), F32)
        for n, (ref, q, x) in enumerate(units[21 * tile : 21 * tile + 21]):
            inside = (lane_8 >= 6 * n) & (lane_8 < 6 * n + 6)
            packed = jnp.where(inside, turn(ref[q, x, :, here], 6 * n + 3, 1), packed)
        columns[tile] = packed
    column_halo = [
        copy(columns.at[pl.ds(0, 5)], columns_low.at[pl.ds(0, 5)], (i, upper)),
        copy(columns.at[pl.ds(0, 5)], columns_high.at[pl.ds(0, 5)], (i, lower)),
    ]
    both = [solid_k.at[pl.ds(0, 2), :, here], solid_k.at[pl.ds(6, 2), :, here]]
    solid_y_halo = [
        made
        for n, part in enumerate(both)
        for made in (copy(part, solid_low_y.at[n], (i, upper)), copy(part, solid_high_y.at[n], (i, lower)))
    ]

    square = (128, 128)
    lane, sub = lane_of(square), sub_of(square)
    lane_32, sub_32 = lane_of((32, 128)), sub_of((32, 128))
    row_lane = lane_of((1, 128))
    diagonal = lane == sub

    def as_row(col):
        return jnp.sum(jnp.where(diagonal, jnp.broadcast_to(col, square), 0.0), axis=0, keepdims=True)

    for n in (4, 5, 6, 7):
        arrivals[n].wait()
    owner = owner_in[...]
    face_index = face_in[...]
    wall = wall_in[...]
    live = lane_of((1, 128)) < jnp.broadcast_to(tally_in[...], (1, 128))
    owner_y = (owner >> 1) & (along - 1)
    owner_corner = ((owner >> 1) // along) * 2 + (owner & 1)
    cell_row = jnp.where(live, owner * 256 + face_index, -1).astype(F32)
    small = [owner, owner_y, face_index >> 7, face_index & 127, wall >> 7, wall & 127]
    rows_8 = jnp.zeros((8, 128), F32)
    for n, row in enumerate([value.astype(F32) for value in small] + [jnp.where(live, 1.0, 0.0)]):
        rows_8 = jnp.where(sub_8 == n, row, rows_8)
    turned = lax.dot_general(
        jnp.where(diagonal, 1.0, 0.0).astype(jnp.bfloat16),
        rows_8.astype(jnp.bfloat16),
        (((1,), (1,)), ((), ())),
        preferred_element_type=F32,
    )
    owner_col, owner_y_col, face_x_col, face_y_col, wall_x_col, wall_y_col, live_col = (
        jnp.sum(jnp.where(lane_of((128, 8)) == n, turned, 0.0), axis=1, keepdims=True) for n in range(7)
    )
    owner_row = owner.astype(F32)
    face_col = 128.0 * face_x_col + face_y_col
    cell_col = jnp.where(live_col > 0.5, 256.0 * owner_col + face_col, -1.0)
    rank_col = jnp.sum(
        jnp.where((jnp.broadcast_to(owner_row, square) == owner_col) & (lane < sub), 1.0, 0.0),
        axis=1,
        keepdims=True,
    )
    lane_f = lane.astype(F32)
    wall_hit = jnp.where(lane_f == wall_y_col, live_col, 0.0)
    for x in range(4):
        wall_mask[x] = jnp.where(wall_x_col == float(x), wall_hit, 0.0)
    slot_key[...] = jnp.where(
        ((lane >> 4).astype(F32) == owner_y_col) & ((lane & 7).astype(F32) == rank_col),
        jnp.broadcast_to(live_col, square),
        0.0,
    )
    to_corner = jnp.where(jnp.broadcast_to(owner_corner, (8, 128)) == sub_8, 1.0, 0.0)

    def at_wall(rows):
        total = wall_mask[0] * rows[0]
        for x in range(1, 4):
            total = total + wall_mask[x] * rows[x]
        return jnp.sum(total, axis=1, keepdims=True)

    def on_wall(col):
        return [jnp.sum(wall_mask[x] * col, axis=0, keepdims=True) for x in range(4)]

    def slots(buffer, n, first, second):
        fields = jnp.where((lane & 8) == 0, first, second)
        value = pick_rows(to_corner, fields * slot_key[...])
        for there in range(4):
            buffer[there, n : n + 1, :] = value[there : there + 1]

    def fill(buffer, n, value):
        buffer[:, n, :] = jnp.broadcast_to(value, (buffer.shape[0], 128))

    warmth = heat[0, :, 0:1, here]
    for q in range(1, 7):
        warmth = warmth + heat[q, :, 0:1, here]
    t1_col = at_wall([warmth[x] for x in range(4)])
    fill(early, 0, cell_row)
    fill(early, 1, as_row(t1_col))
    slots(early, 2, t1_col, face_col + 1.0)
    k_top = [k_here[x][7:8] for x in range(2)]
    k_inner = jnp.where(row_lane == 1, turn(k_top[1], 1, 1), turn(k_top[1], 127, 1))
    fill(early, 3, jnp.where((row_lane == 0) | (row_lane == 127), k_top[0], k_inner))
    for x in range(2):
        fill(early, 4 + x, solid_0[x][7:8])
    round_first(early, near_early, 0, True)

    named = on_wall(cell_col + 1.0)
    named_8 = jnp.zeros((8, 128), F32)
    for x in range(4):
        named_8 = jnp.where((sub_8 & 3) == x, named[x], named_8)
    columns[5] = named_8
    column_halo += [
        copy(columns.at[5], columns_low.at[5], (i, upper)),
        copy(columns.at[5], columns_high.at[5], (i, lower)),
    ]
    collide_flow(flow, post_f.at[0], speeds.at[0], here)
    collide_heat(heat, post_g.at[0], speeds.at[0], here)
    up = down = jnp.zeros((1, 128), F32)
    for x in range(4):
        up = jnp.where(row_lane == x, turn(post_g[0, x + 1, 3, 0:1, here], x + 1, 1), up)
        down = jnp.where(row_lane == x, turn(post_g[0, x + 1, 4, 0:1, here], x, 1), down)
    quick[0], quick[1] = up, down
    quick[2], quick[3] = post_g[0, 4, 1, 0:1, here], post_g[0, 1, 2, 0:1, here]
    quick_halo = [
        copy(quick.at[0], got_quick.at[0], (i, upper)),
        copy(quick.at[1], got_quick.at[1], (i, lower)),
        copy(quick.at[2], got_quick.at[2], (right, j)),
        copy(quick.at[3], got_quick.at[3], (left, j)),
    ]

    gates_x = (jnp.where(i == 0, 0.0, 1.0), jnp.where(i == nx - 1, 0.0, 1.0))
    gates_y = (jnp.where(j == 0, 0.0, 1.0), jnp.where(j == ny - 1, 0.0, 1.0))

    def conduct(field, r, k, span, y_gates):
        change = fluxes(
            field,
            k,
            jnp.where(i > 0, solid_low_x[r, :, span], field[0]),
            jnp.where(i > 0, solid_low_x[3, :, span], k[0]),
            jnp.where(i < nx - 1, solid_high_x[r, :, span], field[1]),
            jnp.where(i < nx - 1, solid_high_x[3, :, span], k[1]),
            gates_x + y_gates,
        )
        return [field[x] + DT * change[x] for x in range(2)]

    settle(solid_x_halo)
    inner_1 = conduct(solid_0, 0, k_here, here, (0.0, 0.0))
    for x in range(2):
        late[0, x : x + 1, :] = inner_1[x][7:8]
    round_first(late, near_late, 2, False)

    for x in range(4):
        covered_ref[x, :, here] = jnp.broadcast_to(jnp.sum(wall_mask[x], axis=0, keepdims=True), (8, 128))
    round_second(near_early, got_early, 0)
    settle(solid_y_halo)
    for x in range(2):
        for n, at in ((0, 0), (1, 6)):
            solid_k[at + x, :, beyond] = jnp.where(lane_8 < 64, solid_high_y[n, x], solid_low_y[n, x])
    solid_x_halo = send_solid(0, beyond) + send_solid(3, beyond)
    settle(column_halo)
    for tile in range(5):
        low, high = columns_low[tile], columns_high[tile]
        for n, (ref, q, x) in enumerate(units[21 * tile : 21 * tile + 21]):
            ref[q, x, :, beyond] = jnp.where(lane_8 < 64, turn(high, 125 - 6 * n, 1), turn(low, 125 - 6 * n, 1))
    named_beyond = jnp.where(lane_8 < 64, columns_high[5], columns_low[5])
    collide_flow(flow, post_f.at[0], speeds.at[0], beyond)
    collide_heat(heat, post_g.at[0], speeds.at[0], beyond)
    heat_halo = send_heat(0)
    flow_halo = send_flow(0)
    round_second(near_late, got_late, 2)

    settle(quick_halo)
    rest_rows = []
    for x in range(4):
        post = lambda q, at=x: post_g[0, at + 1, q, 0:1, here]
        total = post(0) + (post_g[0, x, 1, 0:1, here] if x else got_quick[2])
        total = total + (post_g[0, x + 2, 2, 0:1, here] if x < 3 else got_quick[3])
        total = total + jnp.where(row_lane == 0, turn(got_quick[0], 128 - x, 1), turn(post(3), 1, 1))
        total = total + jnp.where(row_lane == 127, turn(got_quick[1], 127 - x, 1), turn(post(4), 127, 1))
        wall_post = post(6)
        total = total + jnp.where(covered_ref[x, 0:1, here] > 0.5, -wall_post, wall_post)
        rest_rows.append(total + post_g[0, x + 1, 6, 1:2, here])
    a2_col = at_wall(rest_rows)
    slots(third, 0, a2_col, 0.0)
    fill(third, 1, as_row(a2_col))
    round_first(third, near_third, 4, True)

    for x in range(4):
        covered_ref[x, :, beyond] = jnp.where(jnp.broadcast_to(named_beyond[x : x + 1], (8, 128)) > 0.5, 1.0, 0.0)
    halo_lanes = (126, 127, 0, 1)
    halo_cells = [
        jnp.sum(
            jnp.where(lane_8 == jnp.where(sub_8 < 4, halo_lanes[n], halo_lanes[n + 1]), named_beyond, 0.0),
            axis=1,
            keepdims=True,
        )
        - 1.0
        for n in (0, 2)
    ]
    rows_col = jnp.concatenate([cell_col] + halo_cells, axis=0)
    cell_ref[0:144] = jnp.broadcast_to(rows_col, (144, 128))
    rows_cell = cell_ref[0:144].astype(jnp.int32)
    above = (sub_8 & 3) >= 2
    halo_column = jnp.where(above, (sub_8 & 3) - 2, 126 + (sub_8 & 3))
    cell_ref[144:152] = (
        (j + jnp.where(above, 1, -1)) * 256 + 128 * (sub_8 >> 2) + halo_column
    ).astype(F32)
    lane_144 = lane_of((144, 128))
    face_hit = jnp.where(lane_144 == (rows_cell & 127), 1.0, 0.0)
    rows_place = ((rows_cell >> 8) & 31) + 32 * ((rows_cell >> 7) & 1)
    pick = jnp.where(lane_144 == rows_place, 1.0, 0.0)[:, 0:64]

    def put_heat(q, value):
        heat[q] = value

    def put_flow(q, value):
        flow[q] = value

    settle(solid_x_halo)
    k = [solid_k[6 + x] for x in range(2)]
    field_0 = [solid_k[x] for x in range(2)]
    p1 = conduct(field_0, 0, k, whole, gates_y)

    got_bytes(got_early, ny - 4, 1)

    def slot_columns(value, field):
        return [
            jnp.broadcast_to(
                jnp.sum(jnp.where(lane_32 == 8 * field + c, value, 0.0), axis=1, keepdims=True), (32, 128)
            )
            for c in range(CAP)
        ]

    def mine(ref, n):
        return pltpu.roll(ref[:, n, :], lax.rem(128 - 16 * y, 128), 1)

    first_slots = mine(got_early, 2)
    faces = slot_columns(first_slots, 1)

    def own_sums(fields):
        result = []
        for x in range(2):
            place = (lane_32 + (128 * x + 1)).astype(F32)
            totals = [jnp.zeros((32, 128), F32) for _ in fields]
            for c in range(CAP):
                hit = faces[c] == place
                for n, field in enumerate(fields):
                    totals[n] = totals[n] + jnp.where(hit, 1.0 if field is None else field[c], 0.0)
            result.append([jnp.sum(total, axis=0, keepdims=True) for total in totals])
        return result

    def halo_sums(cols):
        result = []
        for x in range(2):
            rows = [jnp.zeros((1, 128), F32) for _ in cols]
            for n, col in enumerate(cols):
                for m, at in enumerate(halo_lanes):
                    rows[n] = jnp.where(row_lane == at, col[144 + 4 * x + m : 145 + 4 * x + m], rows[n])
            result.append(rows)
        return result

    def joined(own, halo):
        return [
            [jnp.concatenate([a, b], axis=1) for a, b in zip(own[x], halo[x])] for x in range(2)
        ]

    top_256 = sub_of((8, 256)) == 7

    def on_top(value, row):
        return value + jnp.where(top_256, jnp.broadcast_to(row, (8, 256)), 0.0)

    def same_cell(ref, n, count, many_rows):
        cells = cell_ref[0:many_rows]

        def body(b, carry):
            hit = cells == got_early[b, 0:1, :]
            total = carry[0] + jnp.where(hit, ref[b, n : n + 1, :], 0.0)
            if count:
                return total, carry[1] + jnp.where(hit, 1.0, 0.0)
            return (total,)

        zero = jnp.zeros((many_rows, 128), F32)
        return lax.fori_loop(0, ny, body, (zero, zero) if count else (zero,))

    total_1, number = same_cell(got_early, 1, True, 152)
    number_col = jnp.sum(number, axis=1, keepdims=True)
    total_1_col = jnp.sum(total_1, axis=1, keepdims=True)
    sums = joined(own_sums([slot_columns(first_slots, 0), None]), halo_sums([total_1_col, number_col]))
    many = [sums[x][1] for x in range(2)]
    solid_1 = [on_top(p1[x], DT * (sums[x][0] - many[x] * field_0[x][7:8])) for x in range(2)]
    for x in range(2):
        solid_k[2 + x] = solid_1[x]
    solid_halo = send_solid(1, whole)

    edge_k = got_early[:, 3, :]
    crossing = []
    for x in range(2):
        inside = got_early[:, 4 + x, :]
        inside_k = edge_k if x == 0 else jnp.where(lane_32 == 0, turn(edge_k, 127, 1), turn(edge_k, 1, 1))
        outside, outside_k = (turn(turn(part, 31, 0), 127, 1) for part in (inside, inside_k))
        c, cb = conduct_of(inside, inside_k), conduct_of(outside, outside_k)
        rise = 2.0 * c * cb / (c + cb) * (outside - inside)
        rise = jnp.where((lane_32 == 127) & (sub_32 != ny - 1), rise, 0.0)
        crossing.append(DT * (rise - turn(turn(rise, 1, 0), 1, 1)))

    settle(heat_halo)
    stream(post_g.at[0], HEAT_PLACES, covered_ref[...], put_heat)
    settle(flow_halo)
    stream(post_f.at[0], FLOW_PLACES, None, put_flow)
    collide_flow(flow, post_f.at[1], speeds.at[1], whole)
    flow_halo = send_flow(1)

    round_second(near_third, got_third, 4)
    got_bytes(got_late, ny - 4, 3)
    surfaces = jnp.concatenate(
        [
            jnp.concatenate([got_late[:, x, :] + crossing[x] for x in range(2)], axis=0),
            jnp.concatenate([got_early[:, 4 + x, :] for x in range(2)], axis=0),
        ],
        axis=1,
    )
    picked = pick_rows(pick, surfaces)
    w1_col = jnp.sum(
        face_hit * (picked[:, 0:128] - DT * number_col[0:144] * picked[:, 128:256]), axis=1, keepdims=True
    )
    w1_col = w1_col + DT * total_1_col[0:144]

    def warm_wall(col):
        rows = on_wall(col[0:128])
        for x in range(4):
            outer = jnp.zeros((1, 128), F32)
            for n, at in enumerate(halo_lanes):
                outer = jnp.where(row_lane == at, col[128 + 4 * n + x : 129 + 4 * n + x], outer)
            outer = jnp.where(covered_ref[x, 0:1, beyond] > 0.5, outer, 0.0)
            heat[5, x, 0:1, here] = heat[5, x, 0:1, here] + 0.25 * rows[x]
            heat[5, x, 0:1, beyond] = heat[5, x, 0:1, beyond] + 0.25 * outer

    warm_wall(w1_col)
    heat_halo = []
    collide_heat(heat, post_g.at[1], speeds.at[1], whole, lambda: heat_halo.extend(send_heat(1)))

    settle(solid_halo)
    p2 = conduct(solid_1, 1, k, whole, gates_y)
    p2 = [on_top(p2[x], (-0.75 * DT) * many[x] * solid_1[x][7:8]) for x in range(2)]
    for x in range(2):
        fill(mid, 2 + x, p2[x][7:8, 0:128])

    settle(heat_halo)
    post = post_g.at[1]
    warmth = post[1:5, 0, 0:1] + post[0:4, 1, 0:1] + post[2:6, 2, 0:1]
    warmth = warmth + turn(post[1:5, 3, 0:1], 1, 2) + turn(post[1:5, 4, 0:1], -1, 2)
    bounce = post[1:5, 6, 0:1]
    warmth = warmth + jnp.where(covered_ref[:, 0:1] > 0.5, -bounce, bounce) + post[1:5, 6, 1:2]
    a3_col = at_wall([warmth[x, :, 0:128] for x in range(4)])
    fill(mid, 0, as_row(a3_col))
    to_owner = jnp.where(jnp.broadcast_to(owner_row, (32, 128)) == sub_32.astype(F32), 1.0, 0.0)
    mid[:, 1, :] = pick_rows(to_owner, jnp.where(lane_f == rank_col, a3_col * live_col, 0.0))
    to_all(mid, got_mid, 6)
    stream(post_g.at[1], HEAT_PLACES, covered_ref[...], put_heat)

    got_bytes(got_third, ny - 4, 5)
    (total_2,) = same_cell(got_third, 1, False, 152)
    total_2_col = jnp.sum(total_2, axis=1, keepdims=True)
    rest = joined(own_sums([slot_columns(mine(got_third, 0), 0)]), halo_sums([total_2_col]))
    solid_2 = [on_top(p2[x], DT * rest[x][0]) for x in range(2)]
    for x in range(2):
        solid_k[4 + x] = solid_2[x]
    solid_halo = send_solid(2, whole)

    settle(flow_halo)
    stream(post_f.at[1], FLOW_PLACES, None, put_flow)
    collide_flow(flow, post_f.at[2], speeds.at[2], whole)
    flow_halo = send_flow(2)

    settle(solid_halo)
    p3 = conduct(solid_2, 2, k, whole, gates_y)
    p3 = [on_top(p3[x], (-0.75 * DT) * many[x] * solid_2[x][7:8])[:, 0:128] for x in range(2)]
    answer = jnp.zeros((32, 128), F32)
    for c in range(CAP):
        first = faces[c] == (lane_32 + 1).astype(F32)
        second = faces[c] == (lane_32 + 129).astype(F32)
        at_cell = jnp.where(first, p3[0][7:8], jnp.where(second, p3[1][7:8], 0.0))
        answer = jnp.where(lane_32 == c, jnp.sum(at_cell, axis=1, keepdims=True), answer)
    answer_out[:, 0, :] = answer
    to_all(answer_out, got_answer, 7)

    got_bytes(got_mid, ny - 1, 6)
    surfaces = jnp.concatenate([got_mid[:, 2 + x, :] for x in range(2)], axis=0)
    picked = pick_rows(pick, surfaces)
    w2_col = jnp.sum(face_hit * picked, axis=1, keepdims=True) + DT * total_2_col[0:144]
    warm_wall(w2_col)
    heat_halo = []
    collide_heat(heat, post_g.at[2], speeds.at[2], whole, lambda: heat_halo.extend(send_heat(2)))

    (total_3,) = same_cell(got_mid, 0, False, 128)
    last = own_sums([slot_columns(got_mid[:, 1, :], 0)])
    for x in range(2):
        s_out[pl.ds(x, 8, stride=2), :] = p3[x] + jnp.where(sub_8 == 7, DT * last[x][0], 0.0)

    settle(flow_halo)

    def write_flow(q, value):
        for x in range(4):
            f_out[q, pl.ds(x, 8, stride=4), :] = value[x, :, 0:128]

    stream(post_f.at[2], FLOW_PLACES, None, write_flow)

    got_bytes(got_answer, ny - 1, 7)
    pick_owner = jnp.where(lane_of((128, 32)).astype(F32) == owner_col, 1.0, 0.0)
    found = pick_rows(pick_owner, got_answer[:, 0, :])
    w3_col = jnp.sum(jnp.where(lane_f == rank_col, found, 0.0) + DT * total_3, axis=1, keepdims=True)
    w3_rows = on_wall(w3_col)

    settle(heat_halo)

    def write_heat(q, value):
        for x in range(4):
            row = value[x, :, 0:128]
            if q == 5:
                row = row + jnp.where(sub_8 == 0, 0.25 * w3_rows[x], 0.0)
            g_out[q, pl.ds(x, 8, stride=4), :] = row

    stream(post_g.at[2], HEAT_PLACES, covered_ref[...], write_heat)

    for n, target in enumerate((got_early, got_late, got_third)):
        sent_bytes(target, 3, 2 * n)
        sent_bytes(target, ny - 4, 2 * n + 1)
    sent_bytes(got_mid, ny - 1, 6)
    sent_bytes(got_answer, ny - 1, 7)
    for made, goes in sent:
        if goes is None:
            made.wait_send()
        else:
            pl.when(goes)(made.wait_send)


def finish(*refs):
    sources, targets, sems = refs[0:3], refs[3:6], refs[6]
    copies = [pltpu.make_async_copy(a, b, sems.at[n]) for n, (a, b) in enumerate(zip(sources, targets))]
    for made in copies:
        made.start()
    for made in copies:
        made.wait()


def on_device(nx, ny, flow, heat, solid, metal, owner, tally, wall, face):
    vmem = functools.partial(pltpu.VMEM, dtype=F32)
    tile, wide = (8, 128), (8, 256)
    copies = 40
    results = (
        jax.ShapeDtypeStruct((19, 32, 128), F32),
        jax.ShapeDtypeStruct((7, 32, 128), F32),
        jax.ShapeDtypeStruct((16, 128), F32),
    )
    out = pl.pallas_call(
        functools.partial(kernel, nx, ny),
        out_shape=tuple(pltpu.VMEM(result.shape, result.dtype) for result in results),
        in_specs=[pl.BlockSpec(memory_space=pltpu.HBM)] * 8,
        out_specs=[pl.BlockSpec(memory_space=pltpu.VMEM)] * 3,
        scratch_shapes=[
            vmem((19, 32, 128)),
            vmem((7, 32, 128)),
            vmem((16, 128)),
            pltpu.VMEM((16, 128), jnp.int32),
            pltpu.VMEM((1, 128), jnp.int32),
            pltpu.VMEM((1, 1), jnp.int32),
            pltpu.VMEM((1, 128), jnp.int32),
            pltpu.VMEM((1, 128), jnp.int32),
            vmem((19, 4) + wide),
            vmem((7, 4) + wide),
            vmem((STEPS, 6, 19) + wide),
            vmem((STEPS, 6, 7) + wide),
            vmem((STEPS, 3, 4) + wide),
            vmem((8,) + wide),
            vmem((4,) + wide),
            vmem((4,) + wide),
            vmem((2, 2) + tile),
            vmem((2, 2) + tile),
            vmem((6,) + tile),
            vmem((6,) + tile),
            vmem((6,) + tile),
            vmem((4, 1, 128)),
            vmem((4, 1, 128)),
            vmem((4, 128, 128)),
            vmem((4,) + wide),
            vmem((152, 128)),
            vmem((128, 128)),
            vmem((4, 6, 128)),
            vmem((4, 6, 128)),
            vmem((32, 6, 128)),
            vmem((1, 2, 128)),
            vmem((4, 2, 128)),
            vmem((32, 2, 128)),
            vmem((4, 2, 128)),
            vmem((4, 2, 128)),
            vmem((32, 2, 128)),
            vmem((32, 4, 128)),
            vmem((32, 4, 128)),
            vmem((32, 1, 128)),
            vmem((32, 1, 128)),
            pltpu.SemaphoreType.DMA((8,)),
            pltpu.SemaphoreType.DMA((copies,)),
            pltpu.SemaphoreType.DMA((copies,)),
            pltpu.SemaphoreType.DMA((8,)),
            pltpu.SemaphoreType.DMA((8,)),
        ],
        compiler_params=pltpu.CompilerParams(
            collective_id=0, has_side_effects=True, vmem_limit_bytes=ROOM
        ),
        name="coupled_steps",
    )(
        flow.reshape(19, 32, 128),
        heat.reshape(7, 32, 128),
        solid.reshape(16, 128),
        metal.reshape(16, 128),
        owner.reshape(1, 128),
        tally,
        wall,
        face,
    )
    out = pl.pallas_call(
        finish,
        out_shape=results,
        in_specs=[pl.BlockSpec(memory_space=pltpu.VMEM)] * 3,
        out_specs=[pl.BlockSpec(memory_space=pltpu.HBM)] * 3,
        scratch_shapes=[pltpu.SemaphoreType.DMA((3,))],
        compiler_params=pltpu.CompilerParams(vmem_limit_bytes=1024 * 1024),
        name="write_out",
    )(*out)
    return out[0].reshape(19, 8, 4, 128), out[1].reshape(7, 8, 4, 128), out[2].reshape(8, 2, 128)


def solution(mesh):
    placed = (
        P(None, None, "gx", "gy"),
        P(None, None, "gx", "gy"),
        P(None, "gx", "gy"),
        P(None, "gx", "gy"),
        P("gx", "gy", None),
        P("gx", "gy"),
        P("gx", "gy"),
        P("gx", "gy"),
    )
    return jax.shard_map(
        functools.partial(on_device, mesh.shape["gx"], mesh.shape["gy"]),
        mesh=mesh,
        in_specs=placed,
        out_specs=(P(None, None, "gx", "gy"), P(None, None, "gx", "gy"), P(None, "gx", "gy")),
        check_vma=False,
    )
```

```python
import functools

import jax
import jax.numpy as jnp
from jax import lax
from jax.experimental import pallas as pl
from jax.experimental.pallas import tpu as pltpu
from jax.sharding import PartitionSpec as P

MESH = pl.DeviceIdType.MESH
F32 = jnp.float32
STEPS = 3
CAP = 8

VELOCITY = [
    (0, 0, 0),
    (1, 0, 0),
    (-1, 0, 0),
    (0, 1, 0),
    (0, -1, 0),
    (0, 0, 1),
    (0, 0, -1),
    (1, 1, 0),
    (-1, -1, 0),
    (1, -1, 0),
    (-1, 1, 0),
    (1, 0, 1),
    (-1, 0, -1),
    (1, 0, -1),
    (-1, 0, 1),
    (0, 1, 1),
    (0, -1, -1),
    (0, 1, -1),
    (0, -1, 1),
]
OPPOSITE = [VELOCITY.index((-a, -b, -c)) for a, b, c in VELOCITY]
ORDER = [1, 7, 9, 11, 13, 2, 8, 10, 12, 14, 0, 3, 4, 5, 6, 15, 16, 17, 18]
PLACE = {q: n for n, q in enumerate(ORDER)}
DT = 0.04
ROOM = 63 * 1024 * 1024


def lane_of(shape):
    return lax.broadcasted_iota(jnp.int32, shape, len(shape) - 1)


def sub_of(shape):
    return lax.broadcasted_iota(jnp.int32, shape, len(shape) - 2)


def turn(value, amount, axis):
    size = value.shape[axis]
    amount = amount % size
    return value if amount == 0 else pltpu.roll(value, amount, axis)


def collide_flow(state, post, velocity, span):
    total, moved = None, [None, None, None]
    for q in range(19):
        value = state[q, :, :, span]
        total = value if total is None else total + value
        for axis in range(3):
            if VELOCITY[q][axis] == 1:
                moved[axis] = value if moved[axis] is None else moved[axis] + value
            elif VELOCITY[q][axis] == -1:
                moved[axis] = -value if moved[axis] is None else moved[axis] - value
    inverse = 1.0 / total
    speed = [part * inverse for part in moved]
    for axis in range(3):
        velocity[axis, :, :, span] = speed[axis]
    base = 1.0 - 1.5 * (speed[0] * speed[0] + speed[1] * speed[1] + speed[2] * speed[2])
    post[1:5, PLACE[0], :, span] = (1.25 / 3.0) * total * base - 0.25 * state[0, :, :, span]
    axial = (1.25 / 18.0) * total
    diagonal = (1.25 / 36.0) * total
    for q in range(1, 19):
        p = OPPOSITE[q]
        if p < q:
            continue
        along = None
        for axis in range(3):
            c = VELOCITY[q][axis]
            if c:
                term = speed[axis] if c == 1 else -speed[axis]
                along = term if along is None else along + term
        even = base + 4.5 * along * along
        odd = 3.0 * along
        scale = axial if q < 7 else diagonal
        post[1:5, PLACE[q], :, span] = scale * (even + odd) - 0.25 * state[q, :, :, span]
        post[1:5, PLACE[p], :, span] = scale * (even - odd) - 0.25 * state[p, :, :, span]


def collide_heat(state, post, velocity, span, x_done=None):
    keep = 1.0 - 1.0 / 0.7
    warmth = state[0, :, :, span]
    for q in range(1, 7):
        warmth = warmth + state[q, :, :, span]
    part = (0.125 / 0.7) * warmth
    for axis in range(3):
        tilt = part * (4.0 * velocity[axis, :, :, span])
        for q in (1 + 2 * axis, 2 + 2 * axis):
            sign = tilt if q == 1 + 2 * axis else -tilt
            post[1:5, q, :, span] = keep * state[q, :, :, span] + (part + sign)
        if axis == 0 and x_done is not None:
            x_done()
    post[1:5, 0, :, span] = keep * state[0, :, :, span] + (0.25 / 0.7) * warmth


def pick_rows(pick, value):
    parts, rest = [], value
    for _ in range(3):
        parts.append(rest.astype(jnp.bfloat16))
        rest = rest - parts[-1].astype(F32)
    found = jnp.dot(
        pick.astype(jnp.bfloat16), jnp.concatenate(parts, axis=1), preferred_element_type=F32
    )
    width = value.shape[1]
    return found[:, 0:width] + (found[:, width : 2 * width] + found[:, 2 * width :])


def lifted(value, cz, bounce):
    if cz == 0:
        return value
    layer = sub_of(value.shape)
    if cz == 1:
        return jnp.where(layer == 0, bounce, turn(value, 1, 1))
    return jnp.where(layer == 7, bounce, turn(value, 7, 1))


def stream(post, places, covered, put):
    for q, place in enumerate(places):
        cx, cy, cz = VELOCITY[q]
        value = turn(post[1 - cx : 5 - cx, place], cy, 2)
        bounce = None
        if cz:
            bounce = post[1:5, places[OPPOSITE[q]]]
            if covered is not None and q == 5:
                bounce = jnp.where(covered > 0.5, -bounce, bounce)
        put(q, lifted(value, cz, bounce))


FLOW_PLACES = [PLACE[q] for q in range(19)]
HEAT_PLACES = list(range(7))


def conduct_of(warmth, k):
    return k * (1.0 + 0.5 * warmth)


def fluxes(field, k, low_x, low_xk, high_x, high_xk, gates):
    gate_low_x, gate_high_x, gate_low_y, gate_high_y = gates
    shape = field[0].shape
    lane, layer = lane_of(shape), sub_of(shape)
    cond = [conduct_of(field[x], k[x]) for x in range(2)]
    result = []

    def face(a, ca, b, cb):
        return 2.0 * ca * cb / (ca + cb) * (b - a)

    inner = face(field[0], cond[0], field[1], cond[1])
    for x in range(2):
        here, c = field[x], cond[x]
        if x == 0:
            total = inner + gate_low_x * face(here, c, low_x, conduct_of(low_x, low_xk))
        else:
            total = gate_high_x * face(here, c, high_x, conduct_of(high_x, high_xk)) - inner
        above = face(here, c, turn(here, -1, 1), turn(c, -1, 1))
        below = -turn(above, 1, 1)
        total = total + jnp.where(lane == 127, gate_high_y, 1.0) * above
        total = total + jnp.where(lane == 0, gate_low_y, 1.0) * below
        up = face(here, c, turn(here, 7, 0), turn(c, 7, 0))
        down = -turn(up, 1, 0)
        total = total + jnp.where(layer == 0, 0.0, down) + jnp.where(layer == 7, 0.0, up)
        result.append(total)
    return result


def kernel(
    nx,
    ny,
    f_hbm,
    g_hbm,
    s_hbm,
    m_hbm,
    owner_hbm,
    tally_hbm,
    wall_hbm,
    face_hbm,
    f_out,
    g_out,
    s_out,
    f_in,
    g_in,
    s_in,
    m_in,
    owner_in,
    tally_in,
    wall_in,
    face_in,
    flow,
    heat,
    post_f,
    post_g,
    speeds,
    solid_k,
    solid_low_x,
    solid_high_x,
    solid_low_y,
    solid_high_y,
    columns,
    columns_low,
    columns_high,
    quick,
    got_quick,
    wall_mask,
    covered_ref,
    cell_ref,
    slot_key,
    early,
    near_early,
    got_early,
    late,
    near_late,
    got_late,
    third,
    near_third,
    got_third,
    mid,
    got_mid,
    answer_out,
    got_answer,
    i_sem,
    n_send,
    n_recv,
    g_send,
    g_recv,
):
    arrivals = []
    for n, (source, target) in enumerate(
        (
            (g_hbm, g_in),
            (f_hbm, f_in),
            (s_hbm, s_in),
            (m_hbm, m_in),
            (owner_hbm, owner_in),
            (tally_hbm, tally_in),
            (wall_hbm, wall_in),
            (face_hbm, face_in),
        )
    ):
        made = pltpu.make_async_copy(source, target, i_sem.at[n])
        made.start()
        arrivals.append(made)

    i, j = lax.axis_index("gx"), lax.axis_index("gy")
    right, left = lax.rem(i + 1, nx), lax.rem(i + nx - 1, nx)
    upper, lower = lax.rem(j + 1, ny), lax.rem(j + ny - 1, ny)
    along = ny // 4
    y = lax.rem(j // 2, along)
    corner = j // (2 * along) * 2 + lax.rem(j, 2)

    def seat(corner_there, y_there):
        return corner_there // 2 * (2 * along) + 2 * y_there + lax.rem(corner_there, 2)

    barrier = pltpu.get_barrier_semaphore()
    greeted = [(i, seat(lax.rem(corner + d, 4), y)) for d in (2, 3, 1)]
    greeted += [(i, seat(corner, lax.rem(y + d, along))) for d in (4, 3, 5, 2, 6, 1, 7)]
    greeted += [(right, j), (left, j), (i, upper), (i, lower)]
    for device in greeted:
        pl.semaphore_signal(barrier, inc=1, device_id=device, device_id_type=MESH)

    sent = []

    def copy(source, target, device, goes=None, comes=None):
        n = len(sent)
        made = pltpu.make_async_remote_copy(
            src_ref=source,
            dst_ref=target,
            send_sem=n_send.at[n],
            recv_sem=n_recv.at[n],
            device_id=device,
            device_id_type=MESH,
        )
        if goes is None:
            made.start()
        else:
            pl.when(goes)(made.start)
        sent.append((made, goes))
        return made, comes

    def settle(copies):
        for made, comes in copies:
            if comes is None:
                made.wait_recv()
            else:
                pl.when(comes)(made.wait_recv)

    def to_right(source, target):
        return copy(source, target, (right, j), i < nx - 1, i > 0)

    def to_left(source, target):
        return copy(source, target, (left, j), i > 0, i < nx - 1)

    def send_flow(t):
        return [
            copy(post_f.at[t, 4, pl.ds(0, 5)], post_f.at[t, 0, pl.ds(0, 5)], (right, j)),
            copy(post_f.at[t, 1, pl.ds(5, 5)], post_f.at[t, 5, pl.ds(5, 5)], (left, j)),
        ]

    def send_heat(t):
        return [
            copy(post_g.at[t, 4, 1], post_g.at[t, 0, 1], (right, j)),
            copy(post_g.at[t, 1, 2], post_g.at[t, 5, 2], (left, j)),
        ]

    def send_solid(r, lanes):
        return [
            to_right(solid_k.at[2 * r + 1, :, lanes], solid_low_x.at[r, :, lanes]),
            to_left(solid_k.at[2 * r, :, lanes], solid_high_x.at[r, :, lanes]),
        ]

    def round_first(source, near, pair, personal):
        for d in (2, 3, 1):
            there = lax.rem(corner + d, 4)
            pltpu.make_async_remote_copy(
                src_ref=source.at[there] if personal else source.at[0],
                dst_ref=near.at[corner],
                send_sem=g_send.at[pair],
                recv_sem=g_recv.at[pair],
                device_id=(i, seat(there, y)),
                device_id_type=MESH,
            ).start()
        near[corner] = source[corner] if personal else source[0]

    def round_second(near, target, pair):
        got_bytes(target, 3, pair)
        for d in (4, 3, 5, 2, 6, 1, 7):
            for half in range(2):
                pltpu.make_async_remote_copy(
                    src_ref=near.at[pl.ds(2 * half, 2)],
                    dst_ref=target.at[pl.ds(2 * along * half + 2 * y, 2)],
                    send_sem=g_send.at[pair + 1],
                    recv_sem=g_recv.at[pair + 1],
                    device_id=(i, seat(corner, lax.rem(y + d, along))),
                    device_id_type=MESH,
                ).start()
        for half in range(2):
            for c in range(2):
                target[2 * along * half + 2 * y + c] = near[2 * half + c]

    def to_all(source, target, pair):
        @pl.loop(0, ny - 1)
        def _(o):
            there = lax.rem(j + 1 + lax.rem(o + ny // 2 - 1, ny - 1), ny)
            pltpu.make_async_remote_copy(
                src_ref=source.at[there],
                dst_ref=target.at[j],
                send_sem=g_send.at[pair],
                recv_sem=g_recv.at[pair],
                device_id=(i, there),
                device_id_type=MESH,
            ).start()

        target[j] = source[j]

    def got_bytes(target, blocks, pair):
        span = pl.ds(0, blocks)
        pltpu.make_async_copy(target.at[span], target.at[span], g_recv.at[pair]).wait()

    def sent_bytes(target, blocks, pair):
        span = pl.ds(0, blocks)
        pltpu.make_async_copy(target.at[span], target.at[span], g_send.at[pair]).wait()

    here, beyond, whole = pl.ds(0, 128), pl.ds(128, 128), pl.ds(0, 256)

    lane_8, sub_8 = lane_of((8, 128)), sub_of((8, 128))
    arrivals[0].wait()
    for q in range(7):
        for x in range(4):
            heat[q, x, :, here] = g_in[q, pl.ds(x, 8, stride=4), :]
    arrivals[1].wait()
    for q in range(19):
        for x in range(4):
            flow[q, x, :, here] = f_in[q, pl.ds(x, 8, stride=4), :]
    units = [(flow, q, x) for q in range(19) for x in range(4)] + [(heat, q, x) for q in range(7) for x in range(4)]
    for tile in range(5):
        packed = jnp.zeros((8, 128), F32)
        for n, (ref, q, x) in enumerate(units[21 * tile : 21 * tile + 21]):
            inside = (lane_8 >= 6 * n) & (lane_8 < 6 * n + 6)
            packed = jnp.where(inside, turn(ref[q, x, :, here], 6 * n + 3, 1), packed)
        columns[tile] = packed
    for n in (2, 3):
        arrivals[n].wait()
    for x in range(2):
        solid_k[x, :, here] = s_in[pl.ds(x, 8, stride=2), :]
        solid_k[6 + x, :, here] = 0.2 + 0.8 * m_in[pl.ds(x, 8, stride=2), :].astype(F32)
    solid_0 = [solid_k[x, :, here] for x in range(2)]
    k_here = [solid_k[6 + x, :, here] for x in range(2)]

    square = (128, 128)
    lane, sub = lane_of(square), sub_of(square)
    lane_32, sub_32 = lane_of((32, 128)), sub_of((32, 128))
    row_lane = lane_of((1, 128))
    diagonal = lane == sub

    def as_row(col):
        return jnp.sum(jnp.where(diagonal, jnp.broadcast_to(col, square), 0.0), axis=0, keepdims=True)

    for n in (4, 5, 6, 7):
        arrivals[n].wait()
    owner = owner_in[...]
    face_index = face_in[...]
    wall = wall_in[...]
    live = lane_of((1, 128)) < jnp.broadcast_to(tally_in[...], (1, 128))
    owner_y = (owner >> 1) & (along - 1)
    owner_corner = ((owner >> 1) // along) * 2 + (owner & 1)
    cell_row = jnp.where(live, owner * 256 + face_index, -1).astype(F32)
    small = [owner, owner_y, face_index >> 7, face_index & 127, wall >> 7, wall & 127]
    rows_8 = jnp.zeros((8, 128), F32)
    for n, row in enumerate([value.astype(F32) for value in small] + [jnp.where(live, 1.0, 0.0)]):
        rows_8 = jnp.where(sub_8 == n, row, rows_8)
    turned = lax.dot_general(
        jnp.where(diagonal, 1.0, 0.0).astype(jnp.bfloat16),
        rows_8.astype(jnp.bfloat16),
        (((1,), (1,)), ((), ())),
        preferred_element_type=F32,
    )
    owner_col, owner_y_col, face_x_col, face_y_col, wall_x_col, wall_y_col, live_col = (
        jnp.sum(jnp.where(lane_of((128, 8)) == n, turned, 0.0), axis=1, keepdims=True) for n in range(7)
    )
    owner_row = owner.astype(F32)
    face_col = 128.0 * face_x_col + face_y_col
    cell_col = jnp.where(live_col > 0.5, 256.0 * owner_col + face_col, -1.0)
    rank_col = jnp.sum(
        jnp.where((jnp.broadcast_to(owner_row, square) == owner_col) & (lane < sub), 1.0, 0.0),
        axis=1,
        keepdims=True,
    )
    lane_f = lane.astype(F32)
    wall_hit = jnp.where(lane_f == wall_y_col, live_col, 0.0)
    for x in range(4):
        wall_mask[x] = jnp.where(wall_x_col == float(x), wall_hit, 0.0)
    slot_key[...] = jnp.where(
        ((lane >> 4).astype(F32) == owner_y_col) & ((lane & 7).astype(F32) == rank_col),
        jnp.broadcast_to(live_col, square),
        0.0,
    )
    to_corner = jnp.where(jnp.broadcast_to(owner_corner, (8, 128)) == sub_8, 1.0, 0.0)

    def at_wall(rows):
        total = wall_mask[0] * rows[0]
        for x in range(1, 4):
            total = total + wall_mask[x] * rows[x]
        return jnp.sum(total, axis=1, keepdims=True)

    def on_wall(col):
        return [jnp.sum(wall_mask[x] * col, axis=0, keepdims=True) for x in range(4)]

    def slots(buffer, n, first, second):
        fields = jnp.where((lane & 8) == 0, first, second)
        value = pick_rows(to_corner, fields * slot_key[...])
        for there in range(4):
            buffer[there, n : n + 1, :] = value[there : there + 1]

    def fill(buffer, n, value):
        buffer[:, n, :] = jnp.broadcast_to(value, (buffer.shape[0], 128))

    warmth = heat[0, :, 0:1, here]
    for q in range(1, 7):
        warmth = warmth + heat[q, :, 0:1, here]
    t1_col = at_wall([warmth[x] for x in range(4)])
    fill(early, 0, cell_row)
    fill(early, 1, as_row(t1_col))
    slots(early, 2, t1_col, face_col + 1.0)
    k_top = [k_here[x][7:8] for x in range(2)]
    k_inner = jnp.where(row_lane == 1, turn(k_top[1], 1, 1), turn(k_top[1], 127, 1))
    fill(early, 3, jnp.where((row_lane == 0) | (row_lane == 127), k_top[0], k_inner))
    for x in range(2):
        fill(early, 4 + x, solid_0[x][7:8])

    named = on_wall(cell_col + 1.0)
    named_8 = jnp.zeros((8, 128), F32)
    for x in range(4):
        named_8 = jnp.where((sub_8 & 3) == x, named[x], named_8)
    columns[5] = named_8
    collide_flow(flow, post_f.at[0], speeds.at[0], here)
    collide_heat(heat, post_g.at[0], speeds.at[0], here)
    up = down = jnp.zeros((1, 128), F32)
    for x in range(4):
        up = jnp.where(row_lane == x, turn(post_g[0, x + 1, 3, 0:1, here], x + 1, 1), up)
        down = jnp.where(row_lane == x, turn(post_g[0, x + 1, 4, 0:1, here], x, 1), down)
    quick[0], quick[1] = up, down
    quick[2], quick[3] = post_g[0, 4, 1, 0:1, here], post_g[0, 1, 2, 0:1, here]
    for x in range(4):
        covered_ref[x, :, here] = jnp.broadcast_to(jnp.sum(wall_mask[x], axis=0, keepdims=True), (8, 128))

    pl.semaphore_wait(barrier, len(greeted))
    solid_x_halo = send_solid(0, here) + send_solid(3, here)
    round_first(early, near_early, 0, True)
    column_halo = [copy(columns, columns_low, (i, upper)), copy(columns, columns_high, (i, lower))]
    quick_halo = [
        copy(quick.at[0], got_quick.at[0], (i, upper)),
        copy(quick.at[1], got_quick.at[1], (i, lower)),
        copy(quick.at[2], got_quick.at[2], (right, j)),
        copy(quick.at[3], got_quick.at[3], (left, j)),
    ]
    both = [solid_k.at[pl.ds(0, 2), :, here], solid_k.at[pl.ds(6, 2), :, here]]
    solid_y_halo = [
        made
        for n, part in enumerate(both)
        for made in (copy(part, solid_low_y.at[n], (i, upper)), copy(part, solid_high_y.at[n], (i, lower)))
    ]

    gates_x = (jnp.where(i == 0, 0.0, 1.0), jnp.where(i == nx - 1, 0.0, 1.0))
    gates_y = (jnp.where(j == 0, 0.0, 1.0), jnp.where(j == ny - 1, 0.0, 1.0))

    def conduct(field, r, k, span, y_gates):
        change = fluxes(
            field,
            k,
            jnp.where(i > 0, solid_low_x[r, :, span], field[0]),
            jnp.where(i > 0, solid_low_x[3, :, span], k[0]),
            jnp.where(i < nx - 1, solid_high_x[r, :, span], field[1]),
            jnp.where(i < nx - 1, solid_high_x[3, :, span], k[1]),
            gates_x + y_gates,
        )
        return [field[x] + DT * change[x] for x in range(2)]

    settle(solid_x_halo)
    inner_1 = conduct(solid_0, 0, k_here, here, (0.0, 0.0))
    for x in range(2):
        late[0, x : x + 1, :] = inner_1[x][7:8]
    round_first(late, near_late, 2, False)

    round_second(near_early, got_early, 0)
    settle(solid_y_halo)
    for x in range(2):
        for n, at in ((0, 0), (1, 6)):
            solid_k[at + x, :, beyond] = jnp.where(lane_8 < 64, solid_high_y[n, x], solid_low_y[n, x])
    solid_x_halo = send_solid(0, beyond) + send_solid(3, beyond)
    settle(column_halo)
    for tile in range(5):
        low, high = columns_low[tile], columns_high[tile]
        for n, (ref, q, x) in enumerate(units[21 * tile : 21 * tile + 21]):
            ref[q, x, :, beyond] = jnp.where(lane_8 < 64, turn(high, 125 - 6 * n, 1), turn(low, 125 - 6 * n, 1))
    named_beyond = jnp.where(lane_8 < 64, columns_high[5], columns_low[5])
    collide_flow(flow, post_f.at[0], speeds.at[0], beyond)
    collide_heat(heat, post_g.at[0], speeds.at[0], beyond)
    heat_halo = send_heat(0)
    flow_halo = send_flow(0)
    round_second(near_late, got_late, 2)

    settle(quick_halo)
    rest_rows = []
    for x in range(4):
        post = lambda q, at=x: post_g[0, at + 1, q, 0:1, here]
        total = post(0) + (post_g[0, x, 1, 0:1, here] if x else got_quick[2])
        total = total + (post_g[0, x + 2, 2, 0:1, here] if x < 3 else got_quick[3])
        total = total + jnp.where(row_lane == 0, turn(got_quick[0], 128 - x, 1), turn(post(3), 1, 1))
        total = total + jnp.where(row_lane == 127, turn(got_quick[1], 127 - x, 1), turn(post(4), 127, 1))
        wall_post = post(6)
        total = total + jnp.where(covered_ref[x, 0:1, here] > 0.5, -wall_post, wall_post)
        rest_rows.append(total + post_g[0, x + 1, 6, 1:2, here])
    a2_col = at_wall(rest_rows)
    slots(third, 0, a2_col, 0.0)
    fill(third, 1, as_row(a2_col))
    round_first(third, near_third, 4, True)

    for x in range(4):
        covered_ref[x, :, beyond] = jnp.where(jnp.broadcast_to(named_beyond[x : x + 1], (8, 128)) > 0.5, 1.0, 0.0)
    halo_lanes = (126, 127, 0, 1)
    halo_cells = [
        jnp.sum(
            jnp.where(lane_8 == jnp.where(sub_8 < 4, halo_lanes[n], halo_lanes[n + 1]), named_beyond, 0.0),
            axis=1,
            keepdims=True,
        )
        - 1.0
        for n in (0, 2)
    ]
    rows_col = jnp.concatenate([cell_col] + halo_cells, axis=0)
    cell_ref[0:144] = jnp.broadcast_to(rows_col, (144, 128))
    rows_cell = cell_ref[0:144].astype(jnp.int32)
    above = (sub_8 & 3) >= 2
    halo_column = jnp.where(above, (sub_8 & 3) - 2, 126 + (sub_8 & 3))
    cell_ref[144:152] = (
        (j + jnp.where(above, 1, -1)) * 256 + 128 * (sub_8 >> 2) + halo_column
    ).astype(F32)
    lane_144 = lane_of((144, 128))
    face_hit = jnp.where(lane_144 == (rows_cell & 127), 1.0, 0.0)
    rows_place = ((rows_cell >> 8) & 31) + 32 * ((rows_cell >> 7) & 1)
    pick = jnp.where(lane_144 == rows_place, 1.0, 0.0)[:, 0:64]

    def put_heat(q, value):
        heat[q] = value

    def put_flow(q, value):
        flow[q] = value

    settle(heat_halo)
    stream(post_g.at[0], HEAT_PLACES, covered_ref[...], put_heat)
    settle(flow_halo)
    stream(post_f.at[0], FLOW_PLACES, None, put_flow)
    collide_flow(flow, post_f.at[1], speeds.at[1], whole)
    flow_halo = send_flow(1)

    settle(solid_x_halo)
    k = [solid_k[6 + x] for x in range(2)]
    field_0 = [solid_k[x] for x in range(2)]
    p1 = conduct(field_0, 0, k, whole, gates_y)

    got_bytes(got_early, ny - 4, 1)

    def slot_columns(value, field):
        return [
            jnp.broadcast_to(
                jnp.sum(jnp.where(lane_32 == 8 * field + c, value, 0.0), axis=1, keepdims=True), (32, 128)
            )
            for c in range(CAP)
        ]

    def mine(ref, n):
        return pltpu.roll(ref[:, n, :], lax.rem(128 - 16 * y, 128), 1)

    first_slots = mine(got_early, 2)
    faces = slot_columns(first_slots, 1)

    def own_sums(fields):
        result = []
        for x in range(2):
            place = (lane_32 + (128 * x + 1)).astype(F32)
            totals = [jnp.zeros((32, 128), F32) for _ in fields]
            for c in range(CAP):
                hit = faces[c] == place
                for n, field in enumerate(fields):
                    totals[n] = totals[n] + jnp.where(hit, 1.0 if field is None else field[c], 0.0)
            result.append([jnp.sum(total, axis=0, keepdims=True) for total in totals])
        return result

    def halo_sums(cols):
        result = []
        for x in range(2):
            rows = [jnp.zeros((1, 128), F32) for _ in cols]
            for n, col in enumerate(cols):
                for m, at in enumerate(halo_lanes):
                    rows[n] = jnp.where(row_lane == at, col[144 + 4 * x + m : 145 + 4 * x + m], rows[n])
            result.append(rows)
        return result

    def joined(own, halo):
        return [
            [jnp.concatenate([a, b], axis=1) for a, b in zip(own[x], halo[x])] for x in range(2)
        ]

    top_256 = sub_of((8, 256)) == 7

    def on_top(value, row):
        return value + jnp.where(top_256, jnp.broadcast_to(row, (8, 256)), 0.0)

    def same_cell(ref, n, count, many_rows):
        halves = []
        for first, last in ((0, 80), (80, many_rows)):
            cells = cell_ref[first:last]

            def body(b, carry, cells=cells):
                hit = cells == got_early[b, 0:1, :]
                total = carry[0] + jnp.where(hit, ref[b, n : n + 1, :], 0.0)
                if count:
                    return total, carry[1] + jnp.where(hit, 1.0, 0.0)
                return (total,)

            zero = jnp.zeros((last - first, 128), F32)
            halves.append(lax.fori_loop(0, ny, body, (zero, zero) if count else (zero,), unroll=2))
        return [jnp.concatenate(parts, axis=0) for parts in zip(*halves)]

    total_1, number = same_cell(got_early, 1, True, 152)
    number_col = jnp.sum(number, axis=1, keepdims=True)
    total_1_col = jnp.sum(total_1, axis=1, keepdims=True)
    sums = joined(own_sums([slot_columns(first_slots, 0), None]), halo_sums([total_1_col, number_col]))
    many = [sums[x][1] for x in range(2)]
    solid_1 = [on_top(p1[x], DT * (sums[x][0] - many[x] * field_0[x][7:8])) for x in range(2)]
    for x in range(2):
        solid_k[2 + x] = solid_1[x]
    solid_halo = send_solid(1, whole)

    edge_k = got_early[:, 3, :]
    crossing = []
    for x in range(2):
        inside = got_early[:, 4 + x, :]
        inside_k = edge_k if x == 0 else jnp.where(lane_32 == 0, turn(edge_k, 127, 1), turn(edge_k, 1, 1))
        outside, outside_k = (turn(turn(part, 31, 0), 127, 1) for part in (inside, inside_k))
        c, cb = conduct_of(inside, inside_k), conduct_of(outside, outside_k)
        rise = 2.0 * c * cb / (c + cb) * (outside - inside)
        rise = jnp.where((lane_32 == 127) & (sub_32 != ny - 1), rise, 0.0)
        crossing.append(DT * (rise - turn(turn(rise, 1, 0), 1, 1)))

    round_second(near_third, got_third, 4)
    got_bytes(got_late, ny - 4, 3)
    surfaces = jnp.concatenate(
        [
            jnp.concatenate([got_late[:, x, :] + crossing[x] for x in range(2)], axis=0),
            jnp.concatenate([got_early[:, 4 + x, :] for x in range(2)], axis=0),
        ],
        axis=1,
    )
    picked = pick_rows(pick, surfaces)
    w1_col = jnp.sum(
        face_hit * (picked[:, 0:128] - DT * number_col[0:144] * picked[:, 128:256]), axis=1, keepdims=True
    )
    w1_col = w1_col + DT * total_1_col[0:144]

    def warm_wall(col):
        rows = on_wall(col[0:128])
        for x in range(4):
            outer = jnp.zeros((1, 128), F32)
            for n, at in enumerate(halo_lanes):
                outer = jnp.where(row_lane == at, col[128 + 4 * n + x : 129 + 4 * n + x], outer)
            outer = jnp.where(covered_ref[x, 0:1, beyond] > 0.5, outer, 0.0)
            heat[5, x, 0:1, here] = heat[5, x, 0:1, here] + 0.25 * rows[x]
            heat[5, x, 0:1, beyond] = heat[5, x, 0:1, beyond] + 0.25 * outer

    warm_wall(w1_col)
    heat_halo = []
    collide_heat(heat, post_g.at[1], speeds.at[1], whole, lambda: heat_halo.extend(send_heat(1)))

    settle(solid_halo)
    p2 = conduct(solid_1, 1, k, whole, gates_y)
    p2 = [on_top(p2[x], (-0.75 * DT) * many[x] * solid_1[x][7:8]) for x in range(2)]
    for x in range(2):
        fill(mid, 2 + x, p2[x][7:8, 0:128])

    settle(heat_halo)
    post = post_g.at[1]
    warmth = post[1:5, 0, 0:1] + post[0:4, 1, 0:1] + post[2:6, 2, 0:1]
    warmth = warmth + turn(post[1:5, 3, 0:1], 1, 2) + turn(post[1:5, 4, 0:1], -1, 2)
    bounce = post[1:5, 6, 0:1]
    warmth = warmth + jnp.where(covered_ref[:, 0:1] > 0.5, -bounce, bounce) + post[1:5, 6, 1:2]
    a3_col = at_wall([warmth[x, :, 0:128] for x in range(4)])
    fill(mid, 0, as_row(a3_col))
    to_owner = jnp.where(jnp.broadcast_to(owner_row, (32, 128)) == sub_32.astype(F32), 1.0, 0.0)
    mid[:, 1, :] = pick_rows(to_owner, jnp.where(lane_f == rank_col, a3_col * live_col, 0.0))
    to_all(mid, got_mid, 6)
    stream(post_g.at[1], HEAT_PLACES, covered_ref[...], put_heat)

    got_bytes(got_third, ny - 4, 5)
    (total_2,) = same_cell(got_third, 1, False, 152)
    total_2_col = jnp.sum(total_2, axis=1, keepdims=True)
    rest = joined(own_sums([slot_columns(mine(got_third, 0), 0)]), halo_sums([total_2_col]))
    solid_2 = [on_top(p2[x], DT * rest[x][0]) for x in range(2)]
    for x in range(2):
        solid_k[4 + x] = solid_2[x]
    solid_halo = send_solid(2, whole)

    settle(flow_halo)
    stream(post_f.at[1], FLOW_PLACES, None, put_flow)
    collide_flow(flow, post_f.at[2], speeds.at[2], whole)
    flow_halo = send_flow(2)

    settle(solid_halo)
    p3 = conduct(solid_2, 2, k, whole, gates_y)
    p3 = [on_top(p3[x], (-0.75 * DT) * many[x] * solid_2[x][7:8])[:, 0:128] for x in range(2)]
    answer = jnp.zeros((32, 128), F32)
    for c in range(CAP):
        first = faces[c] == (lane_32 + 1).astype(F32)
        second = faces[c] == (lane_32 + 129).astype(F32)
        at_cell = jnp.where(first, p3[0][7:8], jnp.where(second, p3[1][7:8], 0.0))
        answer = jnp.where(lane_32 == c, jnp.sum(at_cell, axis=1, keepdims=True), answer)
    answer_out[:, 0, :] = answer
    to_all(answer_out, got_answer, 7)

    got_bytes(got_mid, ny - 1, 6)
    surfaces = jnp.concatenate([got_mid[:, 2 + x, :] for x in range(2)], axis=0)
    picked = pick_rows(pick, surfaces)
    w2_col = jnp.sum(face_hit * picked, axis=1, keepdims=True) + DT * total_2_col[0:144]
    warm_wall(w2_col)
    heat_halo = []
    collide_heat(heat, post_g.at[2], speeds.at[2], whole, lambda: heat_halo.extend(send_heat(2)))

    (total_3,) = same_cell(got_mid, 0, False, 128)
    last = own_sums([slot_columns(got_mid[:, 1, :], 0)])
    for x in range(2):
        s_out[pl.ds(x, 8, stride=2), :] = p3[x] + jnp.where(sub_8 == 7, DT * last[x][0], 0.0)

    settle(flow_halo)

    def write_flow(q, value):
        for x in range(4):
            f_out[q, pl.ds(x, 8, stride=4), :] = value[x, :, 0:128]

    stream(post_f.at[2], FLOW_PLACES, None, write_flow)

    got_bytes(got_answer, ny - 1, 7)
    pick_owner = jnp.where(lane_of((128, 32)).astype(F32) == owner_col, 1.0, 0.0)
    found = pick_rows(pick_owner, got_answer[:, 0, :])
    w3_col = jnp.sum(jnp.where(lane_f == rank_col, found, 0.0) + DT * total_3, axis=1, keepdims=True)
    w3_rows = on_wall(w3_col)

    settle(heat_halo)

    def write_heat(q, value):
        for x in range(4):
            row = value[x, :, 0:128]
            if q == 5:
                row = row + jnp.where(sub_8 == 0, 0.25 * w3_rows[x], 0.0)
            g_out[q, pl.ds(x, 8, stride=4), :] = row

    stream(post_g.at[2], HEAT_PLACES, covered_ref[...], write_heat)

    for n, target in enumerate((got_early, got_late, got_third)):
        sent_bytes(target, 3, 2 * n)
        sent_bytes(target, ny - 4, 2 * n + 1)
    sent_bytes(got_mid, ny - 1, 6)
    sent_bytes(got_answer, ny - 1, 7)
    for made, goes in sent:
        if goes is None:
            made.wait_send()
        else:
            pl.when(goes)(made.wait_send)


def finish(*refs):
    sources, targets, sems = refs[0:3], refs[3:6], refs[6]
    copies = [pltpu.make_async_copy(a, b, sems.at[n]) for n, (a, b) in enumerate(zip(sources, targets))]
    for made in copies:
        made.start()
    for made in copies:
        made.wait()


def on_device(nx, ny, flow, heat, solid, metal, owner, tally, wall, face):
    vmem = functools.partial(pltpu.VMEM, dtype=F32)
    tile, wide = (8, 128), (8, 256)
    copies = 40
    results = (
        jax.ShapeDtypeStruct((19, 32, 128), F32),
        jax.ShapeDtypeStruct((7, 32, 128), F32),
        jax.ShapeDtypeStruct((16, 128), F32),
    )
    out = pl.pallas_call(
        functools.partial(kernel, nx, ny),
        out_shape=tuple(pltpu.VMEM(result.shape, result.dtype) for result in results),
        in_specs=[pl.BlockSpec(memory_space=pltpu.HBM)] * 8,
        out_specs=[pl.BlockSpec(memory_space=pltpu.VMEM)] * 3,
        scratch_shapes=[
            vmem((19, 32, 128)),
            vmem((7, 32, 128)),
            vmem((16, 128)),
            pltpu.VMEM((16, 128), jnp.int32),
            pltpu.VMEM((1, 128), jnp.int32),
            pltpu.VMEM((1, 1), jnp.int32),
            pltpu.VMEM((1, 128), jnp.int32),
            pltpu.VMEM((1, 128), jnp.int32),
            vmem((19, 4) + wide),
            vmem((7, 4) + wide),
            vmem((STEPS, 6, 19) + wide),
            vmem((STEPS, 6, 7) + wide),
            vmem((STEPS, 3, 4) + wide),
            vmem((8,) + wide),
            vmem((4,) + wide),
            vmem((4,) + wide),
            vmem((2, 2) + tile),
            vmem((2, 2) + tile),
            vmem((6,) + tile),
            vmem((6,) + tile),
            vmem((6,) + tile),
            vmem((4, 1, 128)),
            vmem((4, 1, 128)),
            vmem((4, 128, 128)),
            vmem((4,) + wide),
            vmem((152, 128)),
            vmem((128, 128)),
            vmem((4, 6, 128)),
            vmem((4, 6, 128)),
            vmem((32, 6, 128)),
            vmem((1, 2, 128)),
            vmem((4, 2, 128)),
            vmem((32, 2, 128)),
            vmem((4, 2, 128)),
            vmem((4, 2, 128)),
            vmem((32, 2, 128)),
            vmem((32, 4, 128)),
            vmem((32, 4, 128)),
            vmem((32, 1, 128)),
            vmem((32, 1, 128)),
            pltpu.SemaphoreType.DMA((8,)),
            pltpu.SemaphoreType.DMA((copies,)),
            pltpu.SemaphoreType.DMA((copies,)),
            pltpu.SemaphoreType.DMA((8,)),
            pltpu.SemaphoreType.DMA((8,)),
        ],
        compiler_params=pltpu.CompilerParams(
            collective_id=0, has_side_effects=True, vmem_limit_bytes=ROOM
        ),
        name="coupled_steps",
    )(
        flow.reshape(19, 32, 128),
        heat.reshape(7, 32, 128),
        solid.reshape(16, 128),
        metal.reshape(16, 128),
        owner.reshape(1, 128),
        tally,
        wall,
        face,
    )
    out = pl.pallas_call(
        finish,
        out_shape=results,
        in_specs=[pl.BlockSpec(memory_space=pltpu.VMEM)] * 3,
        out_specs=[pl.BlockSpec(memory_space=pltpu.HBM)] * 3,
        scratch_shapes=[pltpu.SemaphoreType.DMA((3,))],
        compiler_params=pltpu.CompilerParams(vmem_limit_bytes=1024 * 1024),
        name="write_out",
    )(*out)
    return out[0].reshape(19, 8, 4, 128), out[1].reshape(7, 8, 4, 128), out[2].reshape(8, 2, 128)


def solution(mesh):
    placed = (
        P(None, None, "gx", "gy"),
        P(None, None, "gx", "gy"),
        P(None, "gx", "gy"),
        P(None, "gx", "gy"),
        P("gx", "gy", None),
        P("gx", "gy"),
        P("gx", "gy"),
        P("gx", "gy"),
    )
    return jax.shard_map(
        functools.partial(on_device, mesh.shape["gx"], mesh.shape["gy"]),
        mesh=mesh,
        in_specs=placed,
        out_specs=(P(None, None, "gx", "gy"), P(None, None, "gx", "gy"), P(None, "gx", "gy")),
        check_vma=False,
    )
```

```python
import functools

import jax
import jax.numpy as jnp
from jax import lax
from jax.experimental import pallas as pl
from jax.experimental.pallas import tpu as pltpu
from jax.sharding import PartitionSpec as P

MESH = pl.DeviceIdType.MESH
F32 = jnp.float32
STEPS = 3
CAP = 8

VELOCITY = [
    (0, 0, 0),
    (1, 0, 0),
    (-1, 0, 0),
    (0, 1, 0),
    (0, -1, 0),
    (0, 0, 1),
    (0, 0, -1),
    (1, 1, 0),
    (-1, -1, 0),
    (1, -1, 0),
    (-1, 1, 0),
    (1, 0, 1),
    (-1, 0, -1),
    (1, 0, -1),
    (-1, 0, 1),
    (0, 1, 1),
    (0, -1, -1),
    (0, 1, -1),
    (0, -1, 1),
]
OPPOSITE = [VELOCITY.index((-a, -b, -c)) for a, b, c in VELOCITY]
ORDER = [1, 7, 9, 11, 13, 2, 8, 10, 12, 14, 0, 3, 4, 5, 6, 15, 16, 17, 18]
PLACE = {q: n for n, q in enumerate(ORDER)}
DT = 0.04
ROOM = 63 * 1024 * 1024


def lane_of(shape):
    return lax.broadcasted_iota(jnp.int32, shape, len(shape) - 1)


def sub_of(shape):
    return lax.broadcasted_iota(jnp.int32, shape, len(shape) - 2)


def turn(value, amount, axis):
    size = value.shape[axis]
    amount = amount % size
    return value if amount == 0 else pltpu.roll(value, amount, axis)


def collide_flow(state, post, velocity, span):
    total, moved = None, [None, None, None]
    for q in range(19):
        value = state[q, :, :, span]
        total = value if total is None else total + value
        for axis in range(3):
            if VELOCITY[q][axis] == 1:
                moved[axis] = value if moved[axis] is None else moved[axis] + value
            elif VELOCITY[q][axis] == -1:
                moved[axis] = -value if moved[axis] is None else moved[axis] - value
    inverse = 1.0 / total
    speed = [part * inverse for part in moved]
    for axis in range(3):
        velocity[axis, :, :, span] = speed[axis]
    base = 1.0 - 1.5 * (speed[0] * speed[0] + speed[1] * speed[1] + speed[2] * speed[2])
    post[1:5, PLACE[0], :, span] = (1.25 / 3.0) * total * base - 0.25 * state[0, :, :, span]
    axial = (1.25 / 18.0) * total
    diagonal = (1.25 / 36.0) * total
    for q in range(1, 19):
        p = OPPOSITE[q]
        if p < q:
            continue
        along = None
        for axis in range(3):
            c = VELOCITY[q][axis]
            if c:
                term = speed[axis] if c == 1 else -speed[axis]
                along = term if along is None else along + term
        even = base + 4.5 * along * along
        odd = 3.0 * along
        scale = axial if q < 7 else diagonal
        post[1:5, PLACE[q], :, span] = scale * (even + odd) - 0.25 * state[q, :, :, span]
        post[1:5, PLACE[p], :, span] = scale * (even - odd) - 0.25 * state[p, :, :, span]


def collide_heat(state, post, velocity, span, x_done=None):
    keep = 1.0 - 1.0 / 0.7
    warmth = state[0, :, :, span]
    for q in range(1, 7):
        warmth = warmth + state[q, :, :, span]
    part = (0.125 / 0.7) * warmth
    for axis in range(3):
        tilt = part * (4.0 * velocity[axis, :, :, span])
        for q in (1 + 2 * axis, 2 + 2 * axis):
            sign = tilt if q == 1 + 2 * axis else -tilt
            post[1:5, q, :, span] = keep * state[q, :, :, span] + (part + sign)
        if axis == 0 and x_done is not None:
            x_done()
    post[1:5, 0, :, span] = keep * state[0, :, :, span] + (0.25 / 0.7) * warmth


def pick_rows(pick, value):
    parts, rest = [], value
    for _ in range(3):
        parts.append(rest.astype(jnp.bfloat16))
        rest = rest - parts[-1].astype(F32)
    found = jnp.dot(
        pick.astype(jnp.bfloat16), jnp.concatenate(parts, axis=1), preferred_element_type=F32
    )
    width = value.shape[1]
    return found[:, 0:width] + (found[:, width : 2 * width] + found[:, 2 * width :])


def lifted(value, cz, bounce):
    if cz == 0:
        return value
    layer = sub_of(value.shape)
    if cz == 1:
        return jnp.where(layer == 0, bounce, turn(value, 1, 1))
    return jnp.where(layer == 7, bounce, turn(value, 7, 1))


def stream(post, places, covered, put):
    for q, place in enumerate(places):
        cx, cy, cz = VELOCITY[q]
        value = turn(post[1 - cx : 5 - cx, place], cy, 2)
        bounce = None
        if cz:
            bounce = post[1:5, places[OPPOSITE[q]]]
            if covered is not None and q == 5:
                bounce = jnp.where(covered > 0.5, -bounce, bounce)
        put(q, lifted(value, cz, bounce))


FLOW_PLACES = [PLACE[q] for q in range(19)]
HEAT_PLACES = list(range(7))


def conduct_of(warmth, k):
    return k * (1.0 + 0.5 * warmth)


def fluxes(field, k, low_x, low_xk, high_x, high_xk, gates):
    gate_low_x, gate_high_x, gate_low_y, gate_high_y = gates
    shape = field[0].shape
    lane, layer = lane_of(shape), sub_of(shape)
    cond = [conduct_of(field[x], k[x]) for x in range(2)]
    result = []

    def face(a, ca, b, cb):
        return 2.0 * ca * cb / (ca + cb) * (b - a)

    inner = face(field[0], cond[0], field[1], cond[1])
    for x in range(2):
        here, c = field[x], cond[x]
        if x == 0:
            total = inner + gate_low_x * face(here, c, low_x, conduct_of(low_x, low_xk))
        else:
            total = gate_high_x * face(here, c, high_x, conduct_of(high_x, high_xk)) - inner
        above = face(here, c, turn(here, -1, 1), turn(c, -1, 1))
        below = -turn(above, 1, 1)
        total = total + jnp.where(lane == 127, gate_high_y, 1.0) * above
        total = total + jnp.where(lane == 0, gate_low_y, 1.0) * below
        up = face(here, c, turn(here, 7, 0), turn(c, 7, 0))
        down = -turn(up, 1, 0)
        total = total + jnp.where(layer == 0, 0.0, down) + jnp.where(layer == 7, 0.0, up)
        result.append(total)
    return result


def kernel(
    nx,
    ny,
    f_hbm,
    g_hbm,
    s_hbm,
    m_hbm,
    owner_hbm,
    tally_hbm,
    wall_hbm,
    face_hbm,
    f_out,
    g_out,
    s_out,
    f_in,
    g_in,
    s_in,
    m_in,
    owner_in,
    tally_in,
    wall_in,
    face_in,
    flow,
    heat,
    post_f,
    post_g,
    speeds,
    solid_k,
    solid_low_x,
    solid_high_x,
    solid_low_y,
    solid_high_y,
    columns,
    columns_low,
    columns_high,
    quick,
    got_quick,
    wall_mask,
    covered_ref,
    cell_ref,
    slot_key,
    early,
    near_early,
    got_early,
    late,
    near_late,
    got_late,
    third,
    near_third,
    got_third,
    surface,
    got_surface,
    mid,
    got_mid,
    answer_out,
    got_answer,
    i_sem,
    n_send,
    n_recv,
    g_send,
    g_recv,
):
    arrivals = []
    for n, (source, target) in enumerate(
        (
            (g_hbm, g_in),
            (f_hbm, f_in),
            (s_hbm, s_in),
            (m_hbm, m_in),
            (owner_hbm, owner_in),
            (tally_hbm, tally_in),
            (wall_hbm, wall_in),
            (face_hbm, face_in),
        )
    ):
        made = pltpu.make_async_copy(source, target, i_sem.at[n])
        made.start()
        arrivals.append(made)

    i, j = lax.axis_index("gx"), lax.axis_index("gy")
    right, left = lax.rem(i + 1, nx), lax.rem(i + nx - 1, nx)
    upper, lower = lax.rem(j + 1, ny), lax.rem(j + ny - 1, ny)
    along = ny // 4
    y = lax.rem(j // 2, along)
    corner = j // (2 * along) * 2 + lax.rem(j, 2)

    def seat(corner_there, y_there):
        return corner_there // 2 * (2 * along) + 2 * y_there + lax.rem(corner_there, 2)

    barrier = pltpu.get_barrier_semaphore()
    greeted = [(i, seat(lax.rem(corner + d, 4), y)) for d in (2, 3, 1)]
    greeted += [(i, seat(corner, lax.rem(y + d, along))) for d in (4, 3, 5, 2, 6, 1, 7)]
    greeted += [(right, j), (left, j), (i, upper), (i, lower)]
    for device in greeted:
        pl.semaphore_signal(barrier, inc=1, device_id=device, device_id_type=MESH)

    sent = []

    def copy(source, target, device, goes=None, comes=None):
        n = len(sent)
        made = pltpu.make_async_remote_copy(
            src_ref=source,
            dst_ref=target,
            send_sem=n_send.at[n],
            recv_sem=n_recv.at[n],
            device_id=device,
            device_id_type=MESH,
        )
        if goes is None:
            made.start()
        else:
            pl.when(goes)(made.start)
        sent.append((made, goes))
        return made, comes

    def settle(copies):
        for made, comes in copies:
            if comes is None:
                made.wait_recv()
            else:
                pl.when(comes)(made.wait_recv)

    def to_right(source, target):
        return copy(source, target, (right, j), i < nx - 1, i > 0)

    def to_left(source, target):
        return copy(source, target, (left, j), i > 0, i < nx - 1)

    def send_flow(t):
        return [
            copy(post_f.at[t, 4, pl.ds(0, 5)], post_f.at[t, 0, pl.ds(0, 5)], (right, j)),
            copy(post_f.at[t, 1, pl.ds(5, 5)], post_f.at[t, 5, pl.ds(5, 5)], (left, j)),
        ]

    def send_heat(t):
        return [
            copy(post_g.at[t, 4, 1], post_g.at[t, 0, 1], (right, j)),
            copy(post_g.at[t, 1, 2], post_g.at[t, 5, 2], (left, j)),
        ]

    def send_solid(r, lanes):
        return [
            to_right(solid_k.at[2 * r + 1, :, lanes], solid_low_x.at[r, :, lanes]),
            to_left(solid_k.at[2 * r, :, lanes], solid_high_x.at[r, :, lanes]),
        ]

    def round_first(source, near, pair, personal):
        for d in (2, 3, 1):
            there = lax.rem(corner + d, 4)
            pltpu.make_async_remote_copy(
                src_ref=source.at[there] if personal else source.at[0],
                dst_ref=near.at[corner],
                send_sem=g_send.at[pair],
                recv_sem=g_recv.at[pair],
                device_id=(i, seat(there, y)),
                device_id_type=MESH,
            ).start()
        near[corner] = source[corner] if personal else source[0]

    def round_second(near, target, pair):
        got_bytes(target, 3, pair)
        for d in (4, 3, 5, 2, 6, 1, 7):
            for half in range(2):
                pltpu.make_async_remote_copy(
                    src_ref=near.at[pl.ds(2 * half, 2)],
                    dst_ref=target.at[pl.ds(2 * along * half + 2 * y, 2)],
                    send_sem=g_send.at[pair + 1],
                    recv_sem=g_recv.at[pair + 1],
                    device_id=(i, seat(corner, lax.rem(y + d, along))),
                    device_id_type=MESH,
                ).start()
        for half in range(2):
            for c in range(2):
                target[2 * along * half + 2 * y + c] = near[2 * half + c]

    def to_all(source, target, pair):
        @pl.loop(0, ny - 1)
        def _(o):
            there = lax.rem(j + 1 + lax.rem(o + ny // 2 - 1, ny - 1), ny)
            pltpu.make_async_remote_copy(
                src_ref=source.at[there],
                dst_ref=target.at[j],
                send_sem=g_send.at[pair],
                recv_sem=g_recv.at[pair],
                device_id=(i, there),
                device_id_type=MESH,
            ).start()

        target[j] = source[j]

    def got_bytes(target, blocks, pair):
        span = pl.ds(0, blocks)
        pltpu.make_async_copy(target.at[span], target.at[span], g_recv.at[pair]).wait()

    def sent_bytes(target, blocks, pair):
        span = pl.ds(0, blocks)
        pltpu.make_async_copy(target.at[span], target.at[span], g_send.at[pair]).wait()

    here, beyond, whole = pl.ds(0, 128), pl.ds(128, 128), pl.ds(0, 256)

    lane_8, sub_8 = lane_of((8, 128)), sub_of((8, 128))
    arrivals[0].wait()
    for q in range(7):
        for x in range(4):
            heat[q, x, :, here] = g_in[q, pl.ds(x, 8, stride=4), :]
    arrivals[1].wait()
    for q in range(19):
        for x in range(4):
            flow[q, x, :, here] = f_in[q, pl.ds(x, 8, stride=4), :]
    units = [(flow, q, x) for q in range(19) for x in range(4)] + [(heat, q, x) for q in range(7) for x in range(4)]
    for tile in range(5):
        packed = jnp.zeros((8, 128), F32)
        for n, (ref, q, x) in enumerate(units[21 * tile : 21 * tile + 21]):
            inside = (lane_8 >= 6 * n) & (lane_8 < 6 * n + 6)
            packed = jnp.where(inside, turn(ref[q, x, :, here], 6 * n + 3, 1), packed)
        columns[tile] = packed
    for n in (2, 3):
        arrivals[n].wait()
    for x in range(2):
        solid_k[x, :, here] = s_in[pl.ds(x, 8, stride=2), :]
        solid_k[6 + x, :, here] = 0.2 + 0.8 * m_in[pl.ds(x, 8, stride=2), :].astype(F32)
    solid_0 = [solid_k[x, :, here] for x in range(2)]
    k_here = [solid_k[6 + x, :, here] for x in range(2)]

    square = (128, 128)
    lane, sub = lane_of(square), sub_of(square)
    lane_32, sub_32 = lane_of((32, 128)), sub_of((32, 128))
    row_lane = lane_of((1, 128))
    diagonal = lane == sub

    def as_row(col):
        return jnp.sum(jnp.where(diagonal, jnp.broadcast_to(col, square), 0.0), axis=0, keepdims=True)

    for n in (4, 5, 6, 7):
        arrivals[n].wait()
    owner = owner_in[...]
    face_index = face_in[...]
    wall = wall_in[...]
    live = lane_of((1, 128)) < jnp.broadcast_to(tally_in[...], (1, 128))
    owner_y = (owner >> 1) & (along - 1)
    owner_corner = ((owner >> 1) // along) * 2 + (owner & 1)
    cell_row = jnp.where(live, owner * 256 + face_index, -1).astype(F32)
    small = [owner, owner_y, face_index >> 7, face_index & 127, wall >> 7, wall & 127]
    rows_8 = jnp.zeros((8, 128), F32)
    for n, row in enumerate([value.astype(F32) for value in small] + [jnp.where(live, 1.0, 0.0)]):
        rows_8 = jnp.where(sub_8 == n, row, rows_8)
    turned = lax.dot_general(
        jnp.where(diagonal, 1.0, 0.0).astype(jnp.bfloat16),
        rows_8.astype(jnp.bfloat16),
        (((1,), (1,)), ((), ())),
        preferred_element_type=F32,
    )
    owner_col, owner_y_col, face_x_col, face_y_col, wall_x_col, wall_y_col, live_col = (
        jnp.sum(jnp.where(lane_of((128, 8)) == n, turned, 0.0), axis=1, keepdims=True) for n in range(7)
    )
    owner_row = owner.astype(F32)
    face_col = 128.0 * face_x_col + face_y_col
    cell_col = jnp.where(live_col > 0.5, 256.0 * owner_col + face_col, -1.0)
    rank_col = jnp.sum(
        jnp.where((jnp.broadcast_to(owner_row, square) == owner_col) & (lane < sub), 1.0, 0.0),
        axis=1,
        keepdims=True,
    )
    lane_f = lane.astype(F32)
    wall_hit = jnp.where(lane_f == wall_y_col, live_col, 0.0)
    for x in range(4):
        wall_mask[x] = jnp.where(wall_x_col == float(x), wall_hit, 0.0)
    slot_key[...] = jnp.where(
        ((lane >> 4).astype(F32) == owner_y_col) & ((lane & 7).astype(F32) == rank_col),
        jnp.broadcast_to(live_col, square),
        0.0,
    )
    to_corner = jnp.where(jnp.broadcast_to(owner_corner, (8, 128)) == sub_8, 1.0, 0.0)

    def at_wall(rows):
        total = wall_mask[0] * rows[0]
        for x in range(1, 4):
            total = total + wall_mask[x] * rows[x]
        return jnp.sum(total, axis=1, keepdims=True)

    def on_wall(col):
        return [jnp.sum(wall_mask[x] * col, axis=0, keepdims=True) for x in range(4)]

    def slots(buffer, n, first, second):
        fields = jnp.where((lane & 8) == 0, first, second)
        value = pick_rows(to_corner, fields * slot_key[...])
        for there in range(4):
            buffer[there, n : n + 1, :] = value[there : there + 1]

    def fill(buffer, n, value):
        buffer[:, n, :] = jnp.broadcast_to(value, (buffer.shape[0], 128))

    warmth = heat[0, :, 0:1, here]
    for q in range(1, 7):
        warmth = warmth + heat[q, :, 0:1, here]
    t1_col = at_wall([warmth[x] for x in range(4)])
    fill(early, 0, cell_row)
    fill(early, 1, as_row(t1_col))
    slots(early, 2, t1_col, face_col + 1.0)
    k_top = [k_here[x][7:8] for x in range(2)]
    k_inner = jnp.where(row_lane == 1, turn(k_top[1], 1, 1), turn(k_top[1], 127, 1))
    fill(early, 3, jnp.where((row_lane == 0) | (row_lane == 127), k_top[0], k_inner))
    for x in range(2):
        fill(early, 4 + x, solid_0[x][7:8])

    named = on_wall(cell_col + 1.0)
    named_8 = jnp.zeros((8, 128), F32)
    for x in range(4):
        named_8 = jnp.where((sub_8 & 3) == x, named[x], named_8)
    columns[5] = named_8
    collide_flow(flow, post_f.at[0], speeds.at[0], here)
    collide_heat(heat, post_g.at[0], speeds.at[0], here)
    up = down = jnp.zeros((1, 128), F32)
    for x in range(4):
        up = jnp.where(row_lane == x, turn(post_g[0, x + 1, 3, 0:1, here], x + 1, 1), up)
        down = jnp.where(row_lane == x, turn(post_g[0, x + 1, 4, 0:1, here], x, 1), down)
    quick[0], quick[1] = up, down
    quick[2], quick[3] = post_g[0, 4, 1, 0:1, here], post_g[0, 1, 2, 0:1, here]
    for x in range(4):
        covered_ref[x, :, here] = jnp.broadcast_to(jnp.sum(wall_mask[x], axis=0, keepdims=True), (8, 128))

    pl.semaphore_wait(barrier, len(greeted))
    solid_x_halo = send_solid(0, here) + send_solid(3, here)
    round_first(early, near_early, 0, True)
    column_halo = [copy(columns, columns_low, (i, upper)), copy(columns, columns_high, (i, lower))]
    quick_halo = [
        copy(quick.at[0], got_quick.at[0], (i, upper)),
        copy(quick.at[1], got_quick.at[1], (i, lower)),
        copy(quick.at[2], got_quick.at[2], (right, j)),
        copy(quick.at[3], got_quick.at[3], (left, j)),
    ]
    both = [solid_k.at[pl.ds(0, 2), :, here], solid_k.at[pl.ds(6, 2), :, here]]
    solid_y_halo = [
        made
        for n, part in enumerate(both)
        for made in (copy(part, solid_low_y.at[n], (i, upper)), copy(part, solid_high_y.at[n], (i, lower)))
    ]

    gates_x = (jnp.where(i == 0, 0.0, 1.0), jnp.where(i == nx - 1, 0.0, 1.0))
    gates_y = (jnp.where(j == 0, 0.0, 1.0), jnp.where(j == ny - 1, 0.0, 1.0))

    def conduct(field, r, k, span, y_gates):
        change = fluxes(
            field,
            k,
            jnp.where(i > 0, solid_low_x[r, :, span], field[0]),
            jnp.where(i > 0, solid_low_x[3, :, span], k[0]),
            jnp.where(i < nx - 1, solid_high_x[r, :, span], field[1]),
            jnp.where(i < nx - 1, solid_high_x[3, :, span], k[1]),
            gates_x + y_gates,
        )
        return [field[x] + DT * change[x] for x in range(2)]

    settle(solid_x_halo)
    inner_1 = conduct(solid_0, 0, k_here, here, (0.0, 0.0))
    for x in range(2):
        late[0, x : x + 1, :] = inner_1[x][7:8]
    round_first(late, near_late, 2, False)

    round_second(near_early, got_early, 0)
    settle(quick_halo)
    rest_rows = []
    for x in range(4):
        post = lambda q, at=x: post_g[0, at + 1, q, 0:1, here]
        total = post(0) + (post_g[0, x, 1, 0:1, here] if x else got_quick[2])
        total = total + (post_g[0, x + 2, 2, 0:1, here] if x < 3 else got_quick[3])
        total = total + jnp.where(row_lane == 0, turn(got_quick[0], 128 - x, 1), turn(post(3), 1, 1))
        total = total + jnp.where(row_lane == 127, turn(got_quick[1], 127 - x, 1), turn(post(4), 127, 1))
        wall_post = post(6)
        total = total + jnp.where(covered_ref[x, 0:1, here] > 0.5, -wall_post, wall_post)
        rest_rows.append(total + post_g[0, x + 1, 6, 1:2, here])
    a2_col = at_wall(rest_rows)
    slots(third, 0, a2_col, 0.0)
    fill(third, 1, as_row(a2_col))
    round_first(third, near_third, 4, True)

    settle(solid_y_halo)
    for x in range(2):
        for n, at in ((0, 0), (1, 6)):
            solid_k[at + x, :, beyond] = jnp.where(lane_8 < 64, solid_high_y[n, x], solid_low_y[n, x])
    solid_x_halo = send_solid(0, beyond) + send_solid(3, beyond)
    settle(column_halo)
    for tile in range(5):
        low, high = columns_low[tile], columns_high[tile]
        for n, (ref, q, x) in enumerate(units[21 * tile : 21 * tile + 21]):
            ref[q, x, :, beyond] = jnp.where(lane_8 < 64, turn(high, 125 - 6 * n, 1), turn(low, 125 - 6 * n, 1))
    named_beyond = jnp.where(lane_8 < 64, columns_high[5], columns_low[5])
    collide_flow(flow, post_f.at[0], speeds.at[0], beyond)
    collide_heat(heat, post_g.at[0], speeds.at[0], beyond)
    heat_halo = send_heat(0)
    flow_halo = send_flow(0)
    round_second(near_late, got_late, 2)

    for x in range(4):
        covered_ref[x, :, beyond] = jnp.where(jnp.broadcast_to(named_beyond[x : x + 1], (8, 128)) > 0.5, 1.0, 0.0)
    halo_lanes = (126, 127, 0, 1)
    halo_cells = [
        jnp.sum(
            jnp.where(lane_8 == jnp.where(sub_8 < 4, halo_lanes[n], halo_lanes[n + 1]), named_beyond, 0.0),
            axis=1,
            keepdims=True,
        )
        - 1.0
        for n in (0, 2)
    ]
    rows_col = jnp.concatenate([cell_col] + halo_cells, axis=0)
    cell_ref[0:144] = jnp.broadcast_to(rows_col, (144, 128))
    rows_cell = cell_ref[0:144].astype(jnp.int32)
    above = (sub_8 & 3) >= 2
    halo_column = jnp.where(above, (sub_8 & 3) - 2, 126 + (sub_8 & 3))
    cell_ref[144:152] = (
        (j + jnp.where(above, 1, -1)) * 256 + 128 * (sub_8 >> 2) + halo_column
    ).astype(F32)
    lane_144 = lane_of((144, 128))
    face_hit = jnp.where(lane_144 == (rows_cell & 127), 1.0, 0.0)
    rows_place = ((rows_cell >> 8) & 31) + 32 * ((rows_cell >> 7) & 1)
    pick = jnp.where(lane_144 == rows_place, 1.0, 0.0)[:, 0:64]

    def put_heat(q, value):
        heat[q] = value

    def put_flow(q, value):
        flow[q] = value

    settle(heat_halo)
    stream(post_g.at[0], HEAT_PLACES, covered_ref[...], put_heat)
    settle(flow_halo)
    stream(post_f.at[0], FLOW_PLACES, None, put_flow)
    collide_flow(flow, post_f.at[1], speeds.at[1], whole)
    flow_halo = send_flow(1)

    settle(solid_x_halo)
    k = [solid_k[6 + x] for x in range(2)]
    field_0 = [solid_k[x] for x in range(2)]
    p1 = conduct(field_0, 0, k, whole, gates_y)

    got_bytes(got_early, ny - 4, 1)

    def slot_columns(value, field):
        return [
            jnp.broadcast_to(
                jnp.sum(jnp.where(lane_32 == 8 * field + c, value, 0.0), axis=1, keepdims=True), (32, 128)
            )
            for c in range(CAP)
        ]

    def mine(ref, n):
        return pltpu.roll(ref[:, n, :], lax.rem(128 - 16 * y, 128), 1)

    first_slots = mine(got_early, 2)
    faces = slot_columns(first_slots, 1)

    def own_sums(fields):
        result = []
        for x in range(2):
            place = (lane_32 + (128 * x + 1)).astype(F32)
            totals = [jnp.zeros((32, 128), F32) for _ in fields]
            for c in range(CAP):
                hit = faces[c] == place
                for n, field in enumerate(fields):
                    totals[n] = totals[n] + jnp.where(hit, 1.0 if field is None else field[c], 0.0)
            result.append([jnp.sum(total, axis=0, keepdims=True) for total in totals])
        return result

    def halo_sums(cols):
        result = []
        for x in range(2):
            rows = [jnp.zeros((1, 128), F32) for _ in cols]
            for n, col in enumerate(cols):
                for m, at in enumerate(halo_lanes):
                    rows[n] = jnp.where(row_lane == at, col[144 + 4 * x + m : 145 + 4 * x + m], rows[n])
            result.append(rows)
        return result

    def joined(own, halo):
        return [
            [jnp.concatenate([a, b], axis=1) for a, b in zip(own[x], halo[x])] for x in range(2)
        ]

    top_256 = sub_of((8, 256)) == 7

    def on_top(value, row):
        return value + jnp.where(top_256, jnp.broadcast_to(row, (8, 256)), 0.0)

    def same_cell(ref, n, count, many_rows):
        halves = []
        for first, last in ((0, 80), (80, many_rows)):
            cells = cell_ref[first:last]

            def body(b, carry, cells=cells):
                hit = cells == got_early[b, 0:1, :]
                total = carry[0] + jnp.where(hit, ref[b, n : n + 1, :], 0.0)
                if count:
                    return total, carry[1] + jnp.where(hit, 1.0, 0.0)
                return (total,)

            zero = jnp.zeros((last - first, 128), F32)
            halves.append(lax.fori_loop(0, ny, body, (zero, zero) if count else (zero,), unroll=2))
        return [jnp.concatenate(parts, axis=0) for parts in zip(*halves)]

    total_1, number = same_cell(got_early, 1, True, 152)
    number_col = jnp.sum(number, axis=1, keepdims=True)
    total_1_col = jnp.sum(total_1, axis=1, keepdims=True)
    sums = joined(own_sums([slot_columns(first_slots, 0), None]), halo_sums([total_1_col, number_col]))
    many = [sums[x][1] for x in range(2)]
    solid_1 = [on_top(p1[x], DT * (sums[x][0] - many[x] * field_0[x][7:8])) for x in range(2)]
    for x in range(2):
        solid_k[2 + x] = solid_1[x]
    solid_halo = send_solid(1, whole)

    edge_k = got_early[:, 3, :]
    crossing = []
    for x in range(2):
        inside = got_early[:, 4 + x, :]
        inside_k = edge_k if x == 0 else jnp.where(lane_32 == 0, turn(edge_k, 127, 1), turn(edge_k, 1, 1))
        outside, outside_k = (turn(turn(part, 31, 0), 127, 1) for part in (inside, inside_k))
        c, cb = conduct_of(inside, inside_k), conduct_of(outside, outside_k)
        rise = 2.0 * c * cb / (c + cb) * (outside - inside)
        rise = jnp.where((lane_32 == 127) & (sub_32 != ny - 1), rise, 0.0)
        crossing.append(DT * (rise - turn(turn(rise, 1, 0), 1, 1)))

    known = jnp.concatenate(
        [jnp.concatenate(crossing, axis=0), jnp.concatenate([got_early[:, 4 + x, :] for x in range(2)], axis=0)],
        axis=1,
    )
    known = pick_rows(pick, known)
    known = face_hit * (known[:, 0:128] - DT * number_col[0:144] * known[:, 128:256])
    known_col = jnp.sum(known, axis=1, keepdims=True) + DT * total_1_col[0:144]
    round_second(near_third, got_third, 4)

    def surface_at_rows(ref):
        surface = jnp.concatenate([ref[:, x, :] for x in range(2)], axis=0)
        return jnp.sum(face_hit * pick_rows(pick, surface), axis=1, keepdims=True)

    got_bytes(got_late, ny - 4, 3)
    w1_col = known_col + surface_at_rows(got_late)

    def warm_wall(col):
        rows = on_wall(col[0:128])
        for x in range(4):
            outer = jnp.zeros((1, 128), F32)
            for n, at in enumerate(halo_lanes):
                outer = jnp.where(row_lane == at, col[128 + 4 * n + x : 129 + 4 * n + x], outer)
            outer = jnp.where(covered_ref[x, 0:1, beyond] > 0.5, outer, 0.0)
            heat[5, x, 0:1, here] = heat[5, x, 0:1, here] + 0.25 * rows[x]
            heat[5, x, 0:1, beyond] = heat[5, x, 0:1, beyond] + 0.25 * outer

    warm_wall(w1_col)
    heat_halo = []
    collide_heat(heat, post_g.at[1], speeds.at[1], whole, lambda: heat_halo.extend(send_heat(1)))

    settle(solid_halo)
    p2 = conduct(solid_1, 1, k, whole, gates_y)
    p2 = [on_top(p2[x], (-0.75 * DT) * many[x] * solid_1[x][7:8]) for x in range(2)]
    for x in range(2):
        fill(surface, x, p2[x][7:8, 0:128])
    to_all(surface, got_surface, 8)

    settle(heat_halo)
    post = post_g.at[1]
    warmth = post[1:5, 0, 0:1] + post[0:4, 1, 0:1] + post[2:6, 2, 0:1]
    warmth = warmth + turn(post[1:5, 3, 0:1], 1, 2) + turn(post[1:5, 4, 0:1], -1, 2)
    bounce = post[1:5, 6, 0:1]
    warmth = warmth + jnp.where(covered_ref[:, 0:1] > 0.5, -bounce, bounce) + post[1:5, 6, 1:2]
    a3_col = at_wall([warmth[x, :, 0:128] for x in range(4)])
    fill(mid, 0, as_row(a3_col))
    to_owner = jnp.where(jnp.broadcast_to(owner_row, (32, 128)) == sub_32.astype(F32), 1.0, 0.0)
    mid[:, 1, :] = pick_rows(to_owner, jnp.where(lane_f == rank_col, a3_col * live_col, 0.0))
    to_all(mid, got_mid, 6)
    stream(post_g.at[1], HEAT_PLACES, covered_ref[...], put_heat)

    got_bytes(got_third, ny - 4, 5)
    (total_2,) = same_cell(got_third, 1, False, 152)
    total_2_col = jnp.sum(total_2, axis=1, keepdims=True)
    rest = joined(own_sums([slot_columns(mine(got_third, 0), 0)]), halo_sums([total_2_col]))
    solid_2 = [on_top(p2[x], DT * rest[x][0]) for x in range(2)]
    for x in range(2):
        solid_k[4 + x] = solid_2[x]
    solid_halo = send_solid(2, whole)

    settle(flow_halo)
    stream(post_f.at[1], FLOW_PLACES, None, put_flow)
    collide_flow(flow, post_f.at[2], speeds.at[2], whole)
    flow_halo = send_flow(2)

    settle(solid_halo)
    p3 = conduct(solid_2, 2, k, whole, gates_y)
    p3 = [on_top(p3[x], (-0.75 * DT) * many[x] * solid_2[x][7:8])[:, 0:128] for x in range(2)]
    answer = jnp.zeros((32, 128), F32)
    for c in range(CAP):
        first = faces[c] == (lane_32 + 1).astype(F32)
        second = faces[c] == (lane_32 + 129).astype(F32)
        at_cell = jnp.where(first, p3[0][7:8], jnp.where(second, p3[1][7:8], 0.0))
        answer = jnp.where(lane_32 == c, jnp.sum(at_cell, axis=1, keepdims=True), answer)
    answer_out[:, 0, :] = answer
    to_all(answer_out, got_answer, 7)

    got_bytes(got_surface, ny - 1, 8)
    w2_col = surface_at_rows(got_surface) + DT * total_2_col[0:144]
    warm_wall(w2_col)
    heat_halo = []
    collide_heat(heat, post_g.at[2], speeds.at[2], whole, lambda: heat_halo.extend(send_heat(2)))

    got_bytes(got_mid, ny - 1, 6)
    (total_3,) = same_cell(got_mid, 0, False, 128)
    last = own_sums([slot_columns(got_mid[:, 1, :], 0)])
    for x in range(2):
        s_out[pl.ds(x, 8, stride=2), :] = p3[x] + jnp.where(sub_8 == 7, DT * last[x][0], 0.0)

    settle(flow_halo)

    def write_flow(q, value):
        for x in range(4):
            f_out[q, pl.ds(x, 8, stride=4), :] = value[x, :, 0:128]

    stream(post_f.at[2], FLOW_PLACES, None, write_flow)

    got_bytes(got_answer, ny - 1, 7)
    pick_owner = jnp.where(lane_of((128, 32)).astype(F32) == owner_col, 1.0, 0.0)
    found = pick_rows(pick_owner, got_answer[:, 0, :])
    w3_col = jnp.sum(jnp.where(lane_f == rank_col, found, 0.0) + DT * total_3, axis=1, keepdims=True)
    w3_rows = on_wall(w3_col)

    settle(heat_halo)

    def write_heat(q, value):
        for x in range(4):
            row = value[x, :, 0:128]
            if q == 5:
                row = row + jnp.where(sub_8 == 0, 0.25 * w3_rows[x], 0.0)
            g_out[q, pl.ds(x, 8, stride=4), :] = row

    stream(post_g.at[2], HEAT_PLACES, covered_ref[...], write_heat)

    for n, target in enumerate((got_early, got_late, got_third)):
        sent_bytes(target, 3, 2 * n)
        sent_bytes(target, ny - 4, 2 * n + 1)
    sent_bytes(got_mid, ny - 1, 6)
    sent_bytes(got_answer, ny - 1, 7)
    sent_bytes(got_surface, ny - 1, 8)
    for made, goes in sent:
        if goes is None:
            made.wait_send()
        else:
            pl.when(goes)(made.wait_send)


def finish(*refs):
    sources, targets, sems = refs[0:3], refs[3:6], refs[6]
    copies = [pltpu.make_async_copy(a, b, sems.at[n]) for n, (a, b) in enumerate(zip(sources, targets))]
    for made in copies:
        made.start()
    for made in copies:
        made.wait()


def on_device(nx, ny, flow, heat, solid, metal, owner, tally, wall, face):
    vmem = functools.partial(pltpu.VMEM, dtype=F32)
    tile, wide = (8, 128), (8, 256)
    copies = 40
    results = (
        jax.ShapeDtypeStruct((19, 32, 128), F32),
        jax.ShapeDtypeStruct((7, 32, 128), F32),
        jax.ShapeDtypeStruct((16, 128), F32),
    )
    out = pl.pallas_call(
        functools.partial(kernel, nx, ny),
        out_shape=tuple(pltpu.VMEM(result.shape, result.dtype) for result in results),
        in_specs=[pl.BlockSpec(memory_space=pltpu.HBM)] * 8,
        out_specs=[pl.BlockSpec(memory_space=pltpu.VMEM)] * 3,
        scratch_shapes=[
            vmem((19, 32, 128)),
            vmem((7, 32, 128)),
            vmem((16, 128)),
            pltpu.VMEM((16, 128), jnp.int32),
            pltpu.VMEM((1, 128), jnp.int32),
            pltpu.VMEM((1, 1), jnp.int32),
            pltpu.VMEM((1, 128), jnp.int32),
            pltpu.VMEM((1, 128), jnp.int32),
            vmem((19, 4) + wide),
            vmem((7, 4) + wide),
            vmem((STEPS, 6, 19) + wide),
            vmem((STEPS, 6, 7) + wide),
            vmem((STEPS, 3, 4) + wide),
            vmem((8,) + wide),
            vmem((4,) + wide),
            vmem((4,) + wide),
            vmem((2, 2) + tile),
            vmem((2, 2) + tile),
            vmem((6,) + tile),
            vmem((6,) + tile),
            vmem((6,) + tile),
            vmem((4, 1, 128)),
            vmem((4, 1, 128)),
            vmem((4, 128, 128)),
            vmem((4,) + wide),
            vmem((152, 128)),
            vmem((128, 128)),
            vmem((4, 6, 128)),
            vmem((4, 6, 128)),
            vmem((32, 6, 128)),
            vmem((1, 2, 128)),
            vmem((4, 2, 128)),
            vmem((32, 2, 128)),
            vmem((4, 2, 128)),
            vmem((4, 2, 128)),
            vmem((32, 2, 128)),
            vmem((32, 2, 128)),
            vmem((32, 2, 128)),
            vmem((32, 2, 128)),
            vmem((32, 2, 128)),
            vmem((32, 1, 128)),
            vmem((32, 1, 128)),
            pltpu.SemaphoreType.DMA((8,)),
            pltpu.SemaphoreType.DMA((copies,)),
            pltpu.SemaphoreType.DMA((copies,)),
            pltpu.SemaphoreType.DMA((9,)),
            pltpu.SemaphoreType.DMA((9,)),
        ],
        compiler_params=pltpu.CompilerParams(
            collective_id=0, has_side_effects=True, vmem_limit_bytes=ROOM
        ),
        name="coupled_steps",
    )(
        flow.reshape(19, 32, 128),
        heat.reshape(7, 32, 128),
        solid.reshape(16, 128),
        metal.reshape(16, 128),
        owner.reshape(1, 128),
        tally,
        wall,
        face,
    )
    out = pl.pallas_call(
        finish,
        out_shape=results,
        in_specs=[pl.BlockSpec(memory_space=pltpu.VMEM)] * 3,
        out_specs=[pl.BlockSpec(memory_space=pltpu.HBM)] * 3,
        scratch_shapes=[pltpu.SemaphoreType.DMA((3,))],
        compiler_params=pltpu.CompilerParams(vmem_limit_bytes=1024 * 1024),
        name="write_out",
    )(*out)
    return out[0].reshape(19, 8, 4, 128), out[1].reshape(7, 8, 4, 128), out[2].reshape(8, 2, 128)


def solution(mesh):
    placed = (
        P(None, None, "gx", "gy"),
        P(None, None, "gx", "gy"),
        P(None, "gx", "gy"),
        P(None, "gx", "gy"),
        P("gx", "gy", None),
        P("gx", "gy"),
        P("gx", "gy"),
        P("gx", "gy"),
    )
    return jax.shard_map(
        functools.partial(on_device, mesh.shape["gx"], mesh.shape["gy"]),
        mesh=mesh,
        in_specs=placed,
        out_specs=(P(None, None, "gx", "gy"), P(None, None, "gx", "gy"), P(None, "gx", "gy")),
        check_vma=False,
    )
```

```python
import functools

import jax
import jax.numpy as jnp
from jax import lax
from jax.experimental import pallas as pl
from jax.experimental.pallas import tpu as pltpu
from jax.sharding import PartitionSpec as P

MESH = pl.DeviceIdType.MESH
F32 = jnp.float32
STEPS = 3
CAP = 8

VELOCITY = [
    (0, 0, 0),
    (1, 0, 0),
    (-1, 0, 0),
    (0, 1, 0),
    (0, -1, 0),
    (0, 0, 1),
    (0, 0, -1),
    (1, 1, 0),
    (-1, -1, 0),
    (1, -1, 0),
    (-1, 1, 0),
    (1, 0, 1),
    (-1, 0, -1),
    (1, 0, -1),
    (-1, 0, 1),
    (0, 1, 1),
    (0, -1, -1),
    (0, 1, -1),
    (0, -1, 1),
]
OPPOSITE = [VELOCITY.index((-a, -b, -c)) for a, b, c in VELOCITY]
ORDER = [1, 7, 9, 11, 13, 2, 8, 10, 12, 14, 0, 3, 4, 5, 6, 15, 16, 17, 18]
PLACE = {q: n for n, q in enumerate(ORDER)}
DT = 0.04
ROOM = 63 * 1024 * 1024


def lane_of(shape):
    return lax.broadcasted_iota(jnp.int32, shape, len(shape) - 1)


def sub_of(shape):
    return lax.broadcasted_iota(jnp.int32, shape, len(shape) - 2)


def turn(value, amount, axis):
    size = value.shape[axis]
    amount = amount % size
    return value if amount == 0 else pltpu.roll(value, amount, axis)


def collide_flow(state, post, velocity, span):
    total, moved = None, [None, None, None]
    for q in range(19):
        value = state[q, :, :, span]
        total = value if total is None else total + value
        for axis in range(3):
            if VELOCITY[q][axis] == 1:
                moved[axis] = value if moved[axis] is None else moved[axis] + value
            elif VELOCITY[q][axis] == -1:
                moved[axis] = -value if moved[axis] is None else moved[axis] - value
    inverse = 1.0 / total
    speed = [part * inverse for part in moved]
    for axis in range(3):
        velocity[axis, :, :, span] = speed[axis]
    base = 1.0 - 1.5 * (speed[0] * speed[0] + speed[1] * speed[1] + speed[2] * speed[2])
    post[1:5, PLACE[0], :, span] = (1.25 / 3.0) * total * base - 0.25 * state[0, :, :, span]
    axial = (1.25 / 18.0) * total
    diagonal = (1.25 / 36.0) * total
    for q in range(1, 19):
        p = OPPOSITE[q]
        if p < q:
            continue
        along = None
        for axis in range(3):
            c = VELOCITY[q][axis]
            if c:
                term = speed[axis] if c == 1 else -speed[axis]
                along = term if along is None else along + term
        even = base + 4.5 * along * along
        odd = 3.0 * along
        scale = axial if q < 7 else diagonal
        post[1:5, PLACE[q], :, span] = scale * (even + odd) - 0.25 * state[q, :, :, span]
        post[1:5, PLACE[p], :, span] = scale * (even - odd) - 0.25 * state[p, :, :, span]


def collide_heat(state, post, velocity, span, x_done=None):
    keep = 1.0 - 1.0 / 0.7
    warmth = state[0, :, :, span]
    for q in range(1, 7):
        warmth = warmth + state[q, :, :, span]
    part = (0.125 / 0.7) * warmth
    for axis in range(3):
        tilt = part * (4.0 * velocity[axis, :, :, span])
        for q in (1 + 2 * axis, 2 + 2 * axis):
            sign = tilt if q == 1 + 2 * axis else -tilt
            post[1:5, q, :, span] = keep * state[q, :, :, span] + (part + sign)
        if axis == 0 and x_done is not None:
            x_done()
    post[1:5, 0, :, span] = keep * state[0, :, :, span] + (0.25 / 0.7) * warmth


def pick_rows(pick, value):
    parts, rest = [], value
    for _ in range(3):
        parts.append(rest.astype(jnp.bfloat16))
        rest = rest - parts[-1].astype(F32)
    found = jnp.dot(
        pick.astype(jnp.bfloat16), jnp.concatenate(parts, axis=1), preferred_element_type=F32
    )
    width = value.shape[1]
    return found[:, 0:width] + (found[:, width : 2 * width] + found[:, 2 * width :])


def lifted(value, cz, bounce):
    if cz == 0:
        return value
    layer = sub_of(value.shape)
    if cz == 1:
        return jnp.where(layer == 0, bounce, turn(value, 1, 1))
    return jnp.where(layer == 7, bounce, turn(value, 7, 1))


def stream(post, places, covered, put):
    for q, place in enumerate(places):
        cx, cy, cz = VELOCITY[q]
        value = turn(post[1 - cx : 5 - cx, place], cy, 2)
        bounce = None
        if cz:
            bounce = post[1:5, places[OPPOSITE[q]]]
            if covered is not None and q == 5:
                bounce = jnp.where(covered > 0.5, -bounce, bounce)
        put(q, lifted(value, cz, bounce))


FLOW_PLACES = [PLACE[q] for q in range(19)]
HEAT_PLACES = list(range(7))


def conduct_of(warmth, k):
    return k * (1.0 + 0.5 * warmth)


def fluxes(field, k, low_x, low_xk, high_x, high_xk, gates):
    gate_low_x, gate_high_x, gate_low_y, gate_high_y = gates
    shape = field[0].shape
    lane, layer = lane_of(shape), sub_of(shape)
    cond = [conduct_of(field[x], k[x]) for x in range(2)]
    result = []

    def face(a, ca, b, cb):
        return 2.0 * ca * cb / (ca + cb) * (b - a)

    inner = face(field[0], cond[0], field[1], cond[1])
    for x in range(2):
        here, c = field[x], cond[x]
        if x == 0:
            total = inner + gate_low_x * face(here, c, low_x, conduct_of(low_x, low_xk))
        else:
            total = gate_high_x * face(here, c, high_x, conduct_of(high_x, high_xk)) - inner
        above = face(here, c, turn(here, -1, 1), turn(c, -1, 1))
        below = -turn(above, 1, 1)
        total = total + jnp.where(lane == 127, gate_high_y, 1.0) * above
        total = total + jnp.where(lane == 0, gate_low_y, 1.0) * below
        up = face(here, c, turn(here, 7, 0), turn(c, 7, 0))
        down = -turn(up, 1, 0)
        total = total + jnp.where(layer == 0, 0.0, down) + jnp.where(layer == 7, 0.0, up)
        result.append(total)
    return result


def kernel(
    nx,
    ny,
    f_hbm,
    g_hbm,
    s_hbm,
    m_hbm,
    owner_hbm,
    tally_hbm,
    wall_hbm,
    face_hbm,
    f_out,
    g_out,
    s_out,
    f_in,
    g_in,
    s_in,
    m_in,
    owner_in,
    tally_in,
    wall_in,
    face_in,
    flow,
    heat,
    post_f,
    post_g,
    speeds,
    solid_k,
    solid_low_x,
    solid_high_x,
    solid_low_y,
    solid_high_y,
    columns,
    columns_low,
    columns_high,
    quick,
    got_quick,
    wall_mask,
    covered_ref,
    cell_ref,
    slot_key,
    early,
    near_early,
    got_early,
    late,
    near_late,
    got_late,
    third,
    near_third,
    got_third,
    surface,
    got_surface,
    mid,
    got_mid,
    answer_out,
    got_answer,
    i_sem,
    n_send,
    n_recv,
    g_send,
    g_recv,
):
    i, j = lax.axis_index("gx"), lax.axis_index("gy")
    right, left = lax.rem(i + 1, nx), lax.rem(i + nx - 1, nx)
    upper, lower = lax.rem(j + 1, ny), lax.rem(j + ny - 1, ny)
    along = ny // 4
    y = lax.rem(j // 2, along)
    corner = j // (2 * along) * 2 + lax.rem(j, 2)

    def seat(corner_there, y_there):
        return corner_there // 2 * (2 * along) + 2 * y_there + lax.rem(corner_there, 2)

    barrier = pltpu.get_barrier_semaphore()
    greeted = [(i, seat(lax.rem(corner + d, 4), y)) for d in (2, 3, 1)]
    greeted += [(i, seat(corner, lax.rem(y + d, along))) for d in (4, 3, 5, 2, 6, 1, 7)]
    greeted += [(right, j), (left, j), (i, upper), (i, lower)]
    for device in greeted:
        pl.semaphore_signal(barrier, inc=1, device_id=device, device_id_type=MESH)

    arrivals = []
    for n, (source, target) in enumerate(
        (
            (g_hbm, g_in),
            (f_hbm, f_in),
            (s_hbm, s_in),
            (m_hbm, m_in),
            (owner_hbm, owner_in),
            (tally_hbm, tally_in),
            (wall_hbm, wall_in),
            (face_hbm, face_in),
        )
    ):
        made = pltpu.make_async_copy(source, target, i_sem.at[n])
        made.start()
        arrivals.append(made)

    sent = []

    def copy(source, target, device, goes=None, comes=None):
        n = len(sent)
        made = pltpu.make_async_remote_copy(
            src_ref=source,
            dst_ref=target,
            send_sem=n_send.at[n],
            recv_sem=n_recv.at[n],
            device_id=device,
            device_id_type=MESH,
        )
        if goes is None:
            made.start()
        else:
            pl.when(goes)(made.start)
        sent.append((made, goes))
        return made, comes

    def settle(copies):
        for made, comes in copies:
            if comes is None:
                made.wait_recv()
            else:
                pl.when(comes)(made.wait_recv)

    def to_right(source, target):
        return copy(source, target, (right, j), i < nx - 1, i > 0)

    def to_left(source, target):
        return copy(source, target, (left, j), i > 0, i < nx - 1)

    def send_flow(t):
        return [
            copy(post_f.at[t, 4, pl.ds(0, 5)], post_f.at[t, 0, pl.ds(0, 5)], (right, j)),
            copy(post_f.at[t, 1, pl.ds(5, 5)], post_f.at[t, 5, pl.ds(5, 5)], (left, j)),
        ]

    def send_heat(t):
        return [
            copy(post_g.at[t, 4, 1], post_g.at[t, 0, 1], (right, j)),
            copy(post_g.at[t, 1, 2], post_g.at[t, 5, 2], (left, j)),
        ]

    def send_solid(r, lanes):
        return [
            to_right(solid_k.at[2 * r + 1, :, lanes], solid_low_x.at[r, :, lanes]),
            to_left(solid_k.at[2 * r, :, lanes], solid_high_x.at[r, :, lanes]),
        ]

    def round_first(source, near, pair, personal):
        for d in (2, 3, 1):
            there = lax.rem(corner + d, 4)
            pltpu.make_async_remote_copy(
                src_ref=source.at[there] if personal else source.at[0],
                dst_ref=near.at[corner // 2, lax.rem(corner, 2)],
                send_sem=g_send.at[pair],
                recv_sem=g_recv.at[pair],
                device_id=(i, seat(there, y)),
                device_id_type=MESH,
            ).start()
        near[corner // 2, lax.rem(corner, 2)] = source[corner] if personal else source[0]

    def round_second(near, target, pair):
        few = target.at[0, pl.ds(0, 3)]
        pltpu.make_async_copy(few, few, g_recv.at[pair]).wait()
        for d in (4, 3, 5, 2, 6, 1, 7):
            pltpu.make_async_remote_copy(
                src_ref=near,
                dst_ref=target.at[:, pl.ds(2 * y, 2)],
                send_sem=g_send.at[pair + 1],
                recv_sem=g_recv.at[pair + 1],
                device_id=(i, seat(corner, lax.rem(y + d, along))),
                device_id_type=MESH,
            ).start()
        for half in range(2):
            for c in range(2):
                target[half, 2 * y + c] = near[half, c]

    def second_wait(target, sems):
        most = target.at[:, pl.ds(0, ny // 2 - 2)]
        pltpu.make_async_copy(most, most, sems).wait()

    def rows_of(ref, n):
        return jnp.concatenate([ref[half, :, n, :] for half in range(2)], axis=0)

    def to_all(source, target, pair):
        @pl.loop(0, ny - 1)
        def _(o):
            there = lax.rem(j + 1 + lax.rem(o + ny // 2 - 1, ny - 1), ny)
            pltpu.make_async_remote_copy(
                src_ref=source.at[there],
                dst_ref=target.at[j],
                send_sem=g_send.at[pair],
                recv_sem=g_recv.at[pair],
                device_id=(i, there),
                device_id_type=MESH,
            ).start()

        target[j] = source[j]

    def got_bytes(target, blocks, pair):
        span = pl.ds(0, blocks)
        pltpu.make_async_copy(target.at[span], target.at[span], g_recv.at[pair]).wait()

    def sent_bytes(target, blocks, pair):
        span = pl.ds(0, blocks)
        pltpu.make_async_copy(target.at[span], target.at[span], g_send.at[pair]).wait()

    here, beyond, whole = pl.ds(0, 128), pl.ds(128, 128), pl.ds(0, 256)

    lane_8, sub_8 = lane_of((8, 128)), sub_of((8, 128))
    arrivals[0].wait()
    for q in range(7):
        for x in range(4):
            heat[q, x, :, here] = g_in[q, pl.ds(x, 8, stride=4), :]
    arrivals[1].wait()
    for q in range(19):
        for x in range(4):
            flow[q, x, :, here] = f_in[q, pl.ds(x, 8, stride=4), :]
    units = [(flow, q, x) for q in range(19) for x in range(4)] + [(heat, q, x) for q in range(7) for x in range(4)]
    for tile in range(5):
        packed = jnp.zeros((8, 128), F32)
        for n, (ref, q, x) in enumerate(units[21 * tile : 21 * tile + 21]):
            inside = (lane_8 >= 6 * n) & (lane_8 < 6 * n + 6)
            packed = jnp.where(inside, turn(ref[q, x, :, here], 6 * n + 3, 1), packed)
        columns[tile] = packed
    for n in (2, 3):
        arrivals[n].wait()
    for x in range(2):
        solid_k[x, :, here] = s_in[pl.ds(x, 8, stride=2), :]
        solid_k[6 + x, :, here] = 0.2 + 0.8 * m_in[pl.ds(x, 8, stride=2), :].astype(F32)
    solid_0 = [solid_k[x, :, here] for x in range(2)]
    k_here = [solid_k[6 + x, :, here] for x in range(2)]

    square = (128, 128)
    lane, sub = lane_of(square), sub_of(square)
    lane_32, sub_32 = lane_of((32, 128)), sub_of((32, 128))
    row_lane = lane_of((1, 128))
    diagonal = lane == sub

    def as_row(col):
        return jnp.sum(jnp.where(diagonal, jnp.broadcast_to(col, square), 0.0), axis=0, keepdims=True)

    for n in (4, 5, 6, 7):
        arrivals[n].wait()
    owner = owner_in[...]
    face_index = face_in[...]
    wall = wall_in[...]
    live = lane_of((1, 128)) < jnp.broadcast_to(tally_in[...], (1, 128))
    owner_y = (owner >> 1) & (along - 1)
    owner_corner = ((owner >> 1) // along) * 2 + (owner & 1)
    cell_row = jnp.where(live, owner * 256 + face_index, -1).astype(F32)
    small = [owner, owner_y, face_index >> 7, face_index & 127, wall >> 7, wall & 127]
    rows_8 = jnp.zeros((8, 128), F32)
    for n, row in enumerate([value.astype(F32) for value in small] + [jnp.where(live, 1.0, 0.0)]):
        rows_8 = jnp.where(sub_8 == n, row, rows_8)
    turned = lax.dot_general(
        jnp.where(diagonal, 1.0, 0.0).astype(jnp.bfloat16),
        rows_8.astype(jnp.bfloat16),
        (((1,), (1,)), ((), ())),
        preferred_element_type=F32,
    )
    owner_col, owner_y_col, face_x_col, face_y_col, wall_x_col, wall_y_col, live_col = (
        jnp.sum(jnp.where(lane_of((128, 8)) == n, turned, 0.0), axis=1, keepdims=True) for n in range(7)
    )
    owner_row = owner.astype(F32)
    face_col = 128.0 * face_x_col + face_y_col
    cell_col = jnp.where(live_col > 0.5, 256.0 * owner_col + face_col, -1.0)
    rank_col = jnp.sum(
        jnp.where((jnp.broadcast_to(owner_row, square) == owner_col) & (lane < sub), 1.0, 0.0),
        axis=1,
        keepdims=True,
    )
    lane_f = lane.astype(F32)
    wall_hit = jnp.where(lane_f == wall_y_col, live_col, 0.0)
    for x in range(4):
        wall_mask[x] = jnp.where(wall_x_col == float(x), wall_hit, 0.0)
    slot_key[...] = jnp.where(
        ((lane >> 4).astype(F32) == owner_y_col) & ((lane & 7).astype(F32) == rank_col),
        jnp.broadcast_to(live_col, square),
        0.0,
    )
    to_corner = jnp.where(jnp.broadcast_to(owner_corner, (8, 128)) == sub_8, 1.0, 0.0)

    def at_wall(rows):
        total = wall_mask[0] * rows[0]
        for x in range(1, 4):
            total = total + wall_mask[x] * rows[x]
        return jnp.sum(total, axis=1, keepdims=True)

    def on_wall(col):
        return [jnp.sum(wall_mask[x] * col, axis=0, keepdims=True) for x in range(4)]

    def slots(buffer, n, first, second):
        fields = jnp.where((lane & 8) == 0, first, second)
        value = pick_rows(to_corner, fields * slot_key[...])
        for there in range(4):
            buffer[there, n : n + 1, :] = value[there : there + 1]

    def fill(buffer, n, value):
        buffer[:, n, :] = jnp.broadcast_to(value, (buffer.shape[0], 128))

    warmth = heat[0, :, 0:1, here]
    for q in range(1, 7):
        warmth = warmth + heat[q, :, 0:1, here]
    t1_col = at_wall([warmth[x] for x in range(4)])
    fill(early, 0, cell_row)
    fill(early, 1, as_row(t1_col))
    slots(early, 2, t1_col, face_col + 1.0)
    k_top = [k_here[x][7:8] for x in range(2)]
    k_inner = jnp.where(row_lane == 1, turn(k_top[1], 1, 1), turn(k_top[1], 127, 1))
    fill(early, 3, jnp.where((row_lane == 0) | (row_lane == 127), k_top[0], k_inner))
    for x in range(2):
        fill(early, 4 + x, solid_0[x][7:8])

    named = on_wall(cell_col + 1.0)
    named_8 = jnp.zeros((8, 128), F32)
    for x in range(4):
        named_8 = jnp.where((sub_8 & 3) == x, named[x], named_8)
    columns[5] = named_8
    collide_flow(flow, post_f.at[0], speeds.at[0], here)
    collide_heat(heat, post_g.at[0], speeds.at[0], here)
    up = down = jnp.zeros((1, 128), F32)
    for x in range(4):
        up = jnp.where(row_lane == x, turn(post_g[0, x + 1, 3, 0:1, here], x + 1, 1), up)
        down = jnp.where(row_lane == x, turn(post_g[0, x + 1, 4, 0:1, here], x, 1), down)
    quick[0], quick[1] = up, down
    quick[2], quick[3] = post_g[0, 4, 1, 0:1, here], post_g[0, 1, 2, 0:1, here]
    for x in range(4):
        covered_ref[x, :, here] = jnp.broadcast_to(jnp.sum(wall_mask[x], axis=0, keepdims=True), (8, 128))

    pl.semaphore_wait(barrier, len(greeted))
    solid_x_halo = send_solid(0, here) + send_solid(3, here)
    round_first(early, near_early, 0, True)
    column_halo = [copy(columns, columns_low, (i, upper)), copy(columns, columns_high, (i, lower))]
    quick_halo = [
        copy(quick.at[0], got_quick.at[0], (i, upper)),
        copy(quick.at[1], got_quick.at[1], (i, lower)),
        copy(quick.at[2], got_quick.at[2], (right, j)),
        copy(quick.at[3], got_quick.at[3], (left, j)),
    ]
    both = [solid_k.at[pl.ds(0, 2), :, here], solid_k.at[pl.ds(6, 2), :, here]]
    solid_y_halo = [
        made
        for n, part in enumerate(both)
        for made in (copy(part, solid_low_y.at[n], (i, upper)), copy(part, solid_high_y.at[n], (i, lower)))
    ]

    gates_x = (jnp.where(i == 0, 0.0, 1.0), jnp.where(i == nx - 1, 0.0, 1.0))
    gates_y = (jnp.where(j == 0, 0.0, 1.0), jnp.where(j == ny - 1, 0.0, 1.0))

    def conduct(field, r, k, span, y_gates):
        change = fluxes(
            field,
            k,
            jnp.where(i > 0, solid_low_x[r, :, span], field[0]),
            jnp.where(i > 0, solid_low_x[3, :, span], k[0]),
            jnp.where(i < nx - 1, solid_high_x[r, :, span], field[1]),
            jnp.where(i < nx - 1, solid_high_x[3, :, span], k[1]),
            gates_x + y_gates,
        )
        return [field[x] + DT * change[x] for x in range(2)]

    settle(solid_x_halo)
    inner_1 = conduct(solid_0, 0, k_here, here, (0.0, 0.0))
    for x in range(2):
        late[0, x : x + 1, :] = inner_1[x][7:8]
    round_first(late, near_late, 2, False)

    round_second(near_early, got_early, 0)
    settle(quick_halo)
    rest_rows = []
    for x in range(4):
        post = lambda q, at=x: post_g[0, at + 1, q, 0:1, here]
        total = post(0) + (post_g[0, x, 1, 0:1, here] if x else got_quick[2])
        total = total + (post_g[0, x + 2, 2, 0:1, here] if x < 3 else got_quick[3])
        total = total + jnp.where(row_lane == 0, turn(got_quick[0], 128 - x, 1), turn(post(3), 1, 1))
        total = total + jnp.where(row_lane == 127, turn(got_quick[1], 127 - x, 1), turn(post(4), 127, 1))
        wall_post = post(6)
        total = total + jnp.where(covered_ref[x, 0:1, here] > 0.5, -wall_post, wall_post)
        rest_rows.append(total + post_g[0, x + 1, 6, 1:2, here])
    a2_col = at_wall(rest_rows)
    slots(third, 0, a2_col, 0.0)
    fill(third, 1, as_row(a2_col))
    round_first(third, near_third, 4, True)

    settle(solid_y_halo)
    for x in range(2):
        for n, at in ((0, 0), (1, 6)):
            solid_k[at + x, :, beyond] = jnp.where(lane_8 < 64, solid_high_y[n, x], solid_low_y[n, x])
    solid_x_halo = send_solid(0, beyond) + send_solid(3, beyond)
    settle(column_halo)
    for tile in range(5):
        low, high = columns_low[tile], columns_high[tile]
        for n, (ref, q, x) in enumerate(units[21 * tile : 21 * tile + 21]):
            ref[q, x, :, beyond] = jnp.where(lane_8 < 64, turn(high, 125 - 6 * n, 1), turn(low, 125 - 6 * n, 1))
    named_beyond = jnp.where(lane_8 < 64, columns_high[5], columns_low[5])
    collide_flow(flow, post_f.at[0], speeds.at[0], beyond)
    collide_heat(heat, post_g.at[0], speeds.at[0], beyond)
    heat_halo = send_heat(0)
    flow_halo = send_flow(0)
    round_second(near_late, got_late, 2)

    for x in range(4):
        covered_ref[x, :, beyond] = jnp.where(jnp.broadcast_to(named_beyond[x : x + 1], (8, 128)) > 0.5, 1.0, 0.0)
    halo_lanes = (126, 127, 0, 1)
    halo_cells = [
        jnp.sum(
            jnp.where(lane_8 == jnp.where(sub_8 < 4, halo_lanes[n], halo_lanes[n + 1]), named_beyond, 0.0),
            axis=1,
            keepdims=True,
        )
        - 1.0
        for n in (0, 2)
    ]
    rows_col = jnp.concatenate([cell_col] + halo_cells, axis=0)
    cell_ref[0:144] = jnp.broadcast_to(rows_col, (144, 128))
    rows_cell = cell_ref[0:144].astype(jnp.int32)
    above = (sub_8 & 3) >= 2
    halo_column = jnp.where(above, (sub_8 & 3) - 2, 126 + (sub_8 & 3))
    cell_ref[144:152] = (
        (j + jnp.where(above, 1, -1)) * 256 + 128 * (sub_8 >> 2) + halo_column
    ).astype(F32)
    lane_144 = lane_of((144, 128))
    face_hit = jnp.where(lane_144 == (rows_cell & 127), 1.0, 0.0)
    rows_place = ((rows_cell >> 8) & 31) + 32 * ((rows_cell >> 7) & 1)
    pick = jnp.where(lane_144 == rows_place, 1.0, 0.0)[:, 0:64]

    def put_heat(q, value):
        heat[q] = value

    def put_flow(q, value):
        flow[q] = value

    settle(heat_halo)
    stream(post_g.at[0], HEAT_PLACES, covered_ref[...], put_heat)
    settle(flow_halo)
    stream(post_f.at[0], FLOW_PLACES, None, put_flow)
    collide_flow(flow, post_f.at[1], speeds.at[1], whole)
    flow_halo = send_flow(1)

    settle(solid_x_halo)
    k = [solid_k[6 + x] for x in range(2)]
    field_0 = [solid_k[x] for x in range(2)]
    p1 = conduct(field_0, 0, k, whole, gates_y)

    second_wait(got_early, g_recv.at[1])

    def slot_columns(value, field):
        return [
            jnp.broadcast_to(
                jnp.sum(jnp.where(lane_32 == 8 * field + c, value, 0.0), axis=1, keepdims=True), (32, 128)
            )
            for c in range(CAP)
        ]

    def mine(ref, n):
        return pltpu.roll(rows_of(ref, n), lax.rem(128 - 16 * y, 128), 1)

    first_slots = mine(got_early, 2)
    faces = slot_columns(first_slots, 1)

    def own_sums(fields):
        result = []
        for x in range(2):
            place = (lane_32 + (128 * x + 1)).astype(F32)
            totals = [jnp.zeros((32, 128), F32) for _ in fields]
            for c in range(CAP):
                hit = faces[c] == place
                for n, field in enumerate(fields):
                    totals[n] = totals[n] + jnp.where(hit, 1.0 if field is None else field[c], 0.0)
            result.append([jnp.sum(total, axis=0, keepdims=True) for total in totals])
        return result

    def halo_sums(cols):
        result = []
        for x in range(2):
            rows = [jnp.zeros((1, 128), F32) for _ in cols]
            for n, col in enumerate(cols):
                for m, at in enumerate(halo_lanes):
                    rows[n] = jnp.where(row_lane == at, col[144 + 4 * x + m : 145 + 4 * x + m], rows[n])
            result.append(rows)
        return result

    def joined(own, halo):
        return [
            [jnp.concatenate([a, b], axis=1) for a, b in zip(own[x], halo[x])] for x in range(2)
        ]

    top_256 = sub_of((8, 256)) == 7

    def on_top(value, row):
        return value + jnp.where(top_256, jnp.broadcast_to(row, (8, 256)), 0.0)

    def same_cell(value_of, count, many_rows):
        halves = []
        for first, last in ((0, 80), (80, many_rows)):
            cells = cell_ref[first:last]

            def body(b, carry, cells=cells):
                hit = cells == got_early[b // 16, lax.rem(b, 16), 0:1, :]
                total = carry[0] + jnp.where(hit, value_of(b), 0.0)
                if count:
                    return total, carry[1] + jnp.where(hit, 1.0, 0.0)
                return (total,)

            zero = jnp.zeros((last - first, 128), F32)
            halves.append(lax.fori_loop(0, ny, body, (zero, zero) if count else (zero,), unroll=2))
        return [jnp.concatenate(parts, axis=0) for parts in zip(*halves)]

    total_1, number = same_cell(lambda b: got_early[b // 16, lax.rem(b, 16), 1:2, :], True, 152)
    number_col = jnp.sum(number, axis=1, keepdims=True)
    total_1_col = jnp.sum(total_1, axis=1, keepdims=True)
    sums = joined(own_sums([slot_columns(first_slots, 0), None]), halo_sums([total_1_col, number_col]))
    many = [sums[x][1] for x in range(2)]
    solid_1 = [on_top(p1[x], DT * (sums[x][0] - many[x] * field_0[x][7:8])) for x in range(2)]
    for x in range(2):
        solid_k[2 + x] = solid_1[x]
    solid_halo = send_solid(1, whole)

    edge_k = rows_of(got_early, 3)
    crossing = []
    for x in range(2):
        inside = rows_of(got_early, 4 + x)
        inside_k = edge_k if x == 0 else jnp.where(lane_32 == 0, turn(edge_k, 127, 1), turn(edge_k, 1, 1))
        outside, outside_k = (turn(turn(part, 31, 0), 127, 1) for part in (inside, inside_k))
        c, cb = conduct_of(inside, inside_k), conduct_of(outside, outside_k)
        rise = 2.0 * c * cb / (c + cb) * (outside - inside)
        rise = jnp.where((lane_32 == 127) & (sub_32 != ny - 1), rise, 0.0)
        crossing.append(DT * (rise - turn(turn(rise, 1, 0), 1, 1)))

    known = jnp.concatenate(
        [jnp.concatenate(crossing, axis=0), jnp.concatenate([rows_of(got_early, 4 + x) for x in range(2)], axis=0)],
        axis=1,
    )
    known = pick_rows(pick, known)
    known = face_hit * (known[:, 0:128] - DT * number_col[0:144] * known[:, 128:256])
    known_col = jnp.sum(known, axis=1, keepdims=True) + DT * total_1_col[0:144]
    round_second(near_third, got_third, 4)

    def surface_at_rows(rows):
        return jnp.sum(face_hit * pick_rows(pick, jnp.concatenate(rows, axis=0)), axis=1, keepdims=True)

    second_wait(got_late, g_recv.at[3])
    w1_col = known_col + surface_at_rows([rows_of(got_late, x) for x in range(2)])

    def warm_wall(col):
        rows = on_wall(col[0:128])
        for x in range(4):
            outer = jnp.zeros((1, 128), F32)
            for n, at in enumerate(halo_lanes):
                outer = jnp.where(row_lane == at, col[128 + 4 * n + x : 129 + 4 * n + x], outer)
            outer = jnp.where(covered_ref[x, 0:1, beyond] > 0.5, outer, 0.0)
            heat[5, x, 0:1, here] = heat[5, x, 0:1, here] + 0.25 * rows[x]
            heat[5, x, 0:1, beyond] = heat[5, x, 0:1, beyond] + 0.25 * outer

    warm_wall(w1_col)
    heat_halo = []
    collide_heat(heat, post_g.at[1], speeds.at[1], whole, lambda: heat_halo.extend(send_heat(1)))

    settle(solid_halo)
    p2 = conduct(solid_1, 1, k, whole, gates_y)
    p2 = [on_top(p2[x], (-0.75 * DT) * many[x] * solid_1[x][7:8]) for x in range(2)]
    for x in range(2):
        fill(surface, x, p2[x][7:8, 0:128])
    to_all(surface, got_surface, 8)

    settle(heat_halo)
    post = post_g.at[1]
    warmth = post[1:5, 0, 0:1] + post[0:4, 1, 0:1] + post[2:6, 2, 0:1]
    warmth = warmth + turn(post[1:5, 3, 0:1], 1, 2) + turn(post[1:5, 4, 0:1], -1, 2)
    bounce = post[1:5, 6, 0:1]
    warmth = warmth + jnp.where(covered_ref[:, 0:1] > 0.5, -bounce, bounce) + post[1:5, 6, 1:2]
    a3_col = at_wall([warmth[x, :, 0:128] for x in range(4)])
    fill(mid, 0, as_row(a3_col))
    to_all(mid, got_mid, 6)
    to_owner = jnp.where(jnp.broadcast_to(owner_row, (32, 128)) == sub_32.astype(F32), 1.0, 0.0)
    answer_out[:, 1, :] = pick_rows(to_owner, jnp.where(lane_f == rank_col, a3_col * live_col, 0.0))
    stream(post_g.at[1], HEAT_PLACES, covered_ref[...], put_heat)

    second_wait(got_third, g_recv.at[5])
    (total_2,) = same_cell(lambda b: got_third[b // 16, lax.rem(b, 16), 1:2, :], False, 152)
    total_2_col = jnp.sum(total_2, axis=1, keepdims=True)
    rest = joined(own_sums([slot_columns(mine(got_third, 0), 0)]), halo_sums([total_2_col]))
    solid_2 = [on_top(p2[x], DT * rest[x][0]) for x in range(2)]
    for x in range(2):
        solid_k[4 + x] = solid_2[x]
    solid_halo = send_solid(2, whole)

    settle(flow_halo)
    stream(post_f.at[1], FLOW_PLACES, None, put_flow)
    collide_flow(flow, post_f.at[2], speeds.at[2], whole)
    flow_halo = send_flow(2)

    settle(solid_halo)
    p3 = conduct(solid_2, 2, k, whole, gates_y)
    p3 = [on_top(p3[x], (-0.75 * DT) * many[x] * solid_2[x][7:8])[:, 0:128] for x in range(2)]
    answer = jnp.zeros((32, 128), F32)
    for c in range(CAP):
        first = faces[c] == (lane_32 + 1).astype(F32)
        second = faces[c] == (lane_32 + 129).astype(F32)
        at_cell = jnp.where(first, p3[0][7:8], jnp.where(second, p3[1][7:8], 0.0))
        answer = jnp.where(lane_32 == c, jnp.sum(at_cell, axis=1, keepdims=True), answer)
    answer_out[:, 0, :] = answer
    to_all(answer_out, got_answer, 7)

    got_bytes(got_surface, ny - 1, 8)
    w2_col = surface_at_rows([got_surface[:, x, :] for x in range(2)]) + DT * total_2_col[0:144]
    warm_wall(w2_col)
    heat_halo = []
    collide_heat(heat, post_g.at[2], speeds.at[2], whole, lambda: heat_halo.extend(send_heat(2)))

    settle(flow_halo)

    def write_flow(q, value):
        for x in range(4):
            f_out[q, pl.ds(x, 8, stride=4), :] = value[x, :, 0:128]

    stream(post_f.at[2], FLOW_PLACES, None, write_flow)

    got_bytes(got_mid, ny - 1, 6)
    (total_3,) = same_cell(lambda b: got_mid[b], False, 128)
    got_bytes(got_answer, ny - 1, 7)
    pick_owner = jnp.where(lane_of((128, 32)).astype(F32) == owner_col, 1.0, 0.0)
    found = pick_rows(pick_owner, got_answer[:, 0, :])
    w3_col = jnp.sum(jnp.where(lane_f == rank_col, found, 0.0) + DT * total_3, axis=1, keepdims=True)
    w3_rows = on_wall(w3_col)
    last = own_sums([slot_columns(got_answer[:, 1, :], 0)])
    for x in range(2):
        s_out[pl.ds(x, 8, stride=2), :] = p3[x] + jnp.where(sub_8 == 7, DT * last[x][0], 0.0)


    settle(heat_halo)

    def write_heat(q, value):
        for x in range(4):
            row = value[x, :, 0:128]
            if q == 5:
                row = row + jnp.where(sub_8 == 0, 0.25 * w3_rows[x], 0.0)
            g_out[q, pl.ds(x, 8, stride=4), :] = row

    stream(post_g.at[2], HEAT_PLACES, covered_ref[...], write_heat)

    for n, target in enumerate((got_early, got_late, got_third)):
        few = target.at[0, pl.ds(0, 3)]
        pltpu.make_async_copy(few, few, g_send.at[2 * n]).wait()
        second_wait(target, g_send.at[2 * n + 1])
    sent_bytes(got_mid, ny - 1, 6)
    sent_bytes(got_answer, ny - 1, 7)
    sent_bytes(got_surface, ny - 1, 8)
    for made, goes in sent:
        if goes is None:
            made.wait_send()
        else:
            pl.when(goes)(made.wait_send)


def finish(*refs):
    sources, targets, sems = refs[0:3], refs[3:6], refs[6]
    copies = [pltpu.make_async_copy(a, b, sems.at[n]) for n, (a, b) in enumerate(zip(sources, targets))]
    for made in copies:
        made.start()
    for made in copies:
        made.wait()


def on_device(nx, ny, flow, heat, solid, metal, owner, tally, wall, face):
    vmem = functools.partial(pltpu.VMEM, dtype=F32)
    tile, wide = (8, 128), (8, 256)
    copies = 40
    results = (
        jax.ShapeDtypeStruct((19, 32, 128), F32),
        jax.ShapeDtypeStruct((7, 32, 128), F32),
        jax.ShapeDtypeStruct((16, 128), F32),
    )
    out = pl.pallas_call(
        functools.partial(kernel, nx, ny),
        out_shape=tuple(pltpu.VMEM(result.shape, result.dtype) for result in results),
        in_specs=[pl.BlockSpec(memory_space=pltpu.HBM)] * 8,
        out_specs=[pl.BlockSpec(memory_space=pltpu.VMEM)] * 3,
        scratch_shapes=[
            vmem((19, 32, 128)),
            vmem((7, 32, 128)),
            vmem((16, 128)),
            pltpu.VMEM((16, 128), jnp.int32),
            pltpu.VMEM((1, 128), jnp.int32),
            pltpu.VMEM((1, 1), jnp.int32),
            pltpu.VMEM((1, 128), jnp.int32),
            pltpu.VMEM((1, 128), jnp.int32),
            vmem((19, 4) + wide),
            vmem((7, 4) + wide),
            vmem((STEPS, 6, 19) + wide),
            vmem((STEPS, 6, 7) + wide),
            vmem((STEPS, 3, 4) + wide),
            vmem((8,) + wide),
            vmem((4,) + wide),
            vmem((4,) + wide),
            vmem((2, 2) + tile),
            vmem((2, 2) + tile),
            vmem((6,) + tile),
            vmem((6,) + tile),
            vmem((6,) + tile),
            vmem((4, 1, 128)),
            vmem((4, 1, 128)),
            vmem((4, 128, 128)),
            vmem((4,) + wide),
            vmem((152, 128)),
            vmem((128, 128)),
            vmem((4, 6, 128)),
            vmem((2, 2, 6, 128)),
            vmem((2, 16, 6, 128)),
            vmem((1, 2, 128)),
            vmem((2, 2, 2, 128)),
            vmem((2, 16, 2, 128)),
            vmem((4, 2, 128)),
            vmem((2, 2, 2, 128)),
            vmem((2, 16, 2, 128)),
            vmem((32, 2, 128)),
            vmem((32, 2, 128)),
            vmem((32, 1, 128)),
            vmem((32, 1, 128)),
            vmem((32, 2, 128)),
            vmem((32, 2, 128)),
            pltpu.SemaphoreType.DMA((8,)),
            pltpu.SemaphoreType.DMA((copies,)),
            pltpu.SemaphoreType.DMA((copies,)),
            pltpu.SemaphoreType.DMA((9,)),
            pltpu.SemaphoreType.DMA((9,)),
        ],
        compiler_params=pltpu.CompilerParams(
            collective_id=0, has_side_effects=True, vmem_limit_bytes=ROOM
        ),
        name="coupled_steps",
    )(
        flow.reshape(19, 32, 128),
        heat.reshape(7, 32, 128),
        solid.reshape(16, 128),
        metal.reshape(16, 128),
        owner.reshape(1, 128),
        tally,
        wall,
        face,
    )
    out = pl.pallas_call(
        finish,
        out_shape=results,
        in_specs=[pl.BlockSpec(memory_space=pltpu.VMEM)] * 3,
        out_specs=[pl.BlockSpec(memory_space=pltpu.HBM)] * 3,
        scratch_shapes=[pltpu.SemaphoreType.DMA((3,))],
        compiler_params=pltpu.CompilerParams(vmem_limit_bytes=1024 * 1024),
        name="write_out",
    )(*out)
    return out[0].reshape(19, 8, 4, 128), out[1].reshape(7, 8, 4, 128), out[2].reshape(8, 2, 128)


def solution(mesh):
    placed = (
        P(None, None, "gx", "gy"),
        P(None, None, "gx", "gy"),
        P(None, "gx", "gy"),
        P(None, "gx", "gy"),
        P("gx", "gy", None),
        P("gx", "gy"),
        P("gx", "gy"),
        P("gx", "gy"),
    )
    return jax.shard_map(
        functools.partial(on_device, mesh.shape["gx"], mesh.shape["gy"]),
        mesh=mesh,
        in_specs=placed,
        out_specs=(P(None, None, "gx", "gy"), P(None, None, "gx", "gy"), P(None, "gx", "gy")),
        check_vma=False,
    )
```

```python
import functools

import jax
import jax.numpy as jnp
from jax import lax
from jax.experimental import pallas as pl
from jax.experimental.pallas import tpu as pltpu
from jax.sharding import PartitionSpec as P

MESH = pl.DeviceIdType.MESH
F32 = jnp.float32
STEPS = 3
CAP = 8

VELOCITY = [
    (0, 0, 0),
    (1, 0, 0),
    (-1, 0, 0),
    (0, 1, 0),
    (0, -1, 0),
    (0, 0, 1),
    (0, 0, -1),
    (1, 1, 0),
    (-1, -1, 0),
    (1, -1, 0),
    (-1, 1, 0),
    (1, 0, 1),
    (-1, 0, -1),
    (1, 0, -1),
    (-1, 0, 1),
    (0, 1, 1),
    (0, -1, -1),
    (0, 1, -1),
    (0, -1, 1),
]
OPPOSITE = [VELOCITY.index((-a, -b, -c)) for a, b, c in VELOCITY]
ORDER = [1, 7, 9, 11, 13, 2, 8, 10, 12, 14, 0, 3, 4, 5, 6, 15, 16, 17, 18]
PLACE = {q: n for n, q in enumerate(ORDER)}
DT = 0.04
ROOM = 63 * 1024 * 1024


def lane_of(shape):
    return lax.broadcasted_iota(jnp.int32, shape, len(shape) - 1)


def sub_of(shape):
    return lax.broadcasted_iota(jnp.int32, shape, len(shape) - 2)


def turn(value, amount, axis):
    size = value.shape[axis]
    amount = amount % size
    return value if amount == 0 else pltpu.roll(value, amount, axis)


def collide_flow(state, post, velocity, span):
    total, moved = None, [None, None, None]
    for q in range(19):
        value = state[q, :, :, span]
        total = value if total is None else total + value
        for axis in range(3):
            if VELOCITY[q][axis] == 1:
                moved[axis] = value if moved[axis] is None else moved[axis] + value
            elif VELOCITY[q][axis] == -1:
                moved[axis] = -value if moved[axis] is None else moved[axis] - value
    inverse = 1.0 / total
    speed = [part * inverse for part in moved]
    for axis in range(3):
        velocity[axis, :, :, span] = speed[axis]
    base = 1.0 - 1.5 * (speed[0] * speed[0] + speed[1] * speed[1] + speed[2] * speed[2])
    post[1:5, PLACE[0], :, span] = (1.25 / 3.0) * total * base - 0.25 * state[0, :, :, span]
    axial = (1.25 / 18.0) * total
    diagonal = (1.25 / 36.0) * total
    for q in range(1, 19):
        p = OPPOSITE[q]
        if p < q:
            continue
        along = None
        for axis in range(3):
            c = VELOCITY[q][axis]
            if c:
                term = speed[axis] if c == 1 else -speed[axis]
                along = term if along is None else along + term
        even = base + 4.5 * along * along
        odd = 3.0 * along
        scale = axial if q < 7 else diagonal
        post[1:5, PLACE[q], :, span] = scale * (even + odd) - 0.25 * state[q, :, :, span]
        post[1:5, PLACE[p], :, span] = scale * (even - odd) - 0.25 * state[p, :, :, span]


def collide_heat(state, post, velocity, span, x_done=None):
    keep = 1.0 - 1.0 / 0.7
    warmth = state[0, :, :, span]
    for q in range(1, 7):
        warmth = warmth + state[q, :, :, span]
    part = (0.125 / 0.7) * warmth
    for axis in range(3):
        tilt = part * (4.0 * velocity[axis, :, :, span])
        for q in (1 + 2 * axis, 2 + 2 * axis):
            sign = tilt if q == 1 + 2 * axis else -tilt
            post[1:5, q, :, span] = keep * state[q, :, :, span] + (part + sign)
        if axis == 0 and x_done is not None:
            x_done()
    post[1:5, 0, :, span] = keep * state[0, :, :, span] + (0.25 / 0.7) * warmth


def pick_rows(pick, value):
    parts, rest = [], value
    for _ in range(3):
        parts.append(rest.astype(jnp.bfloat16))
        rest = rest - parts[-1].astype(F32)
    found = jnp.dot(
        pick.astype(jnp.bfloat16), jnp.concatenate(parts, axis=1), preferred_element_type=F32
    )
    width = value.shape[1]
    return found[:, 0:width] + (found[:, width : 2 * width] + found[:, 2 * width :])


def lifted(value, cz, bounce):
    if cz == 0:
        return value
    layer = sub_of(value.shape)
    if cz == 1:
        return jnp.where(layer == 0, bounce, turn(value, 1, 1))
    return jnp.where(layer == 7, bounce, turn(value, 7, 1))


def stream(post, places, covered, put):
    for q, place in enumerate(places):
        cx, cy, cz = VELOCITY[q]
        value = turn(post[1 - cx : 5 - cx, place], cy, 2)
        bounce = None
        if cz:
            bounce = post[1:5, places[OPPOSITE[q]]]
            if covered is not None and q == 5:
                bounce = jnp.where(covered > 0.5, -bounce, bounce)
        put(q, lifted(value, cz, bounce))


FLOW_PLACES = [PLACE[q] for q in range(19)]
HEAT_PLACES = list(range(7))


def conduct_of(warmth, k):
    return k * (1.0 + 0.5 * warmth)


def fluxes(field, k, low_x, low_xk, high_x, high_xk, gates):
    gate_low_x, gate_high_x, gate_low_y, gate_high_y = gates
    shape = field[0].shape
    lane, layer = lane_of(shape), sub_of(shape)
    cond = [conduct_of(field[x], k[x]) for x in range(2)]
    result = []

    def face(a, ca, b, cb):
        return 2.0 * ca * cb / (ca + cb) * (b - a)

    inner = face(field[0], cond[0], field[1], cond[1])
    for x in range(2):
        here, c = field[x], cond[x]
        if x == 0:
            total = inner + gate_low_x * face(here, c, low_x, conduct_of(low_x, low_xk))
        else:
            total = gate_high_x * face(here, c, high_x, conduct_of(high_x, high_xk)) - inner
        above = face(here, c, turn(here, -1, 1), turn(c, -1, 1))
        below = -turn(above, 1, 1)
        total = total + jnp.where(lane == 127, gate_high_y, 1.0) * above
        total = total + jnp.where(lane == 0, gate_low_y, 1.0) * below
        up = face(here, c, turn(here, 7, 0), turn(c, 7, 0))
        down = -turn(up, 1, 0)
        total = total + jnp.where(layer == 0, 0.0, down) + jnp.where(layer == 7, 0.0, up)
        result.append(total)
    return result


def kernel(
    nx,
    ny,
    f_hbm,
    g_hbm,
    s_hbm,
    m_hbm,
    owner_hbm,
    tally_hbm,
    wall_hbm,
    face_hbm,
    f_out,
    g_out,
    s_out,
    f_in,
    g_in,
    s_in,
    m_in,
    owner_in,
    tally_in,
    wall_in,
    face_in,
    flow,
    heat,
    post_f,
    post_g,
    speeds,
    solid_k,
    solid_low_x,
    solid_high_x,
    solid_low_y,
    solid_high_y,
    columns,
    columns_low,
    columns_high,
    quick,
    got_quick,
    wall_mask,
    covered_ref,
    cell_ref,
    early,
    near_early,
    got_early,
    late,
    near_late,
    got_late,
    third,
    near_third,
    got_third,
    surface,
    got_surface,
    mid,
    got_mid,
    answer_out,
    got_answer,
    i_sem,
    n_send,
    n_recv,
    g_send,
    g_recv,
):
    i, j = lax.axis_index("gx"), lax.axis_index("gy")
    right, left = lax.rem(i + 1, nx), lax.rem(i + nx - 1, nx)
    upper, lower = lax.rem(j + 1, ny), lax.rem(j + ny - 1, ny)
    along = ny // 4
    y = lax.rem(j // 2, along)
    corner = j // (2 * along) * 2 + lax.rem(j, 2)

    def seat(corner_there, y_there):
        return corner_there // 2 * (2 * along) + 2 * y_there + lax.rem(corner_there, 2)

    barrier = pltpu.get_barrier_semaphore()
    greeted = [(i, seat(lax.rem(corner + d, 4), y)) for d in (2, 3, 1)]
    greeted += [(i, seat(corner, lax.rem(y + d, along))) for d in (4, 3, 5, 2, 6, 1, 7)]
    greeted += [(right, j), (left, j), (i, upper), (i, lower)]
    for device in greeted:
        pl.semaphore_signal(barrier, inc=1, device_id=device, device_id_type=MESH)

    arrivals = []
    for n, (source, target) in enumerate(
        (
            (g_hbm, g_in),
            (f_hbm, f_in),
            (s_hbm, s_in),
            (m_hbm, m_in),
            (owner_hbm, owner_in),
            (tally_hbm, tally_in),
            (wall_hbm, wall_in),
            (face_hbm, face_in),
        )
    ):
        made = pltpu.make_async_copy(source, target, i_sem.at[n])
        made.start()
        arrivals.append(made)

    sent = []

    def copy(source, target, device, goes=None, comes=None):
        n = len(sent)
        made = pltpu.make_async_remote_copy(
            src_ref=source,
            dst_ref=target,
            send_sem=n_send.at[n],
            recv_sem=n_recv.at[n],
            device_id=device,
            device_id_type=MESH,
        )
        if goes is None:
            made.start()
        else:
            pl.when(goes)(made.start)
        sent.append((made, goes))
        return made, comes

    def settle(copies):
        for made, comes in copies:
            if comes is None:
                made.wait_recv()
            else:
                pl.when(comes)(made.wait_recv)

    def to_right(source, target):
        return copy(source, target, (right, j), i < nx - 1, i > 0)

    def to_left(source, target):
        return copy(source, target, (left, j), i > 0, i < nx - 1)

    def send_flow(t):
        return [
            copy(post_f.at[t, 4, pl.ds(0, 5)], post_f.at[t, 0, pl.ds(0, 5)], (right, j)),
            copy(post_f.at[t, 1, pl.ds(5, 5)], post_f.at[t, 5, pl.ds(5, 5)], (left, j)),
        ]

    def send_heat(t):
        return [
            copy(post_g.at[t, 4, 1], post_g.at[t, 0, 1], (right, j)),
            copy(post_g.at[t, 1, 2], post_g.at[t, 5, 2], (left, j)),
        ]

    def send_solid(r, lanes):
        return [
            to_right(solid_k.at[2 * r + 1, :, lanes], solid_low_x.at[r, :, lanes]),
            to_left(solid_k.at[2 * r, :, lanes], solid_high_x.at[r, :, lanes]),
        ]

    def round_first(source, near, pair):
        for d in (2, 3, 1):
            there = lax.rem(corner + d, 4)
            pltpu.make_async_remote_copy(
                src_ref=source.at[0],
                dst_ref=near.at[corner // 2, lax.rem(corner, 2)],
                send_sem=g_send.at[pair],
                recv_sem=g_recv.at[pair],
                device_id=(i, seat(there, y)),
                device_id_type=MESH,
            ).start()
        near[corner // 2, lax.rem(corner, 2)] = source[0]

    def round_second(near, target, pair):
        few = target.at[0, pl.ds(0, 3)]
        pltpu.make_async_copy(few, few, g_recv.at[pair]).wait()
        for d in (4, 3, 5, 2, 6, 1, 7):
            pltpu.make_async_remote_copy(
                src_ref=near,
                dst_ref=target.at[:, pl.ds(2 * y, 2)],
                send_sem=g_send.at[pair + 1],
                recv_sem=g_recv.at[pair + 1],
                device_id=(i, seat(corner, lax.rem(y + d, along))),
                device_id_type=MESH,
            ).start()
        for half in range(2):
            for c in range(2):
                target[half, 2 * y + c] = near[half, c]

    def second_wait(target, sems):
        most = target.at[:, pl.ds(0, ny // 2 - 2)]
        pltpu.make_async_copy(most, most, sems).wait()

    def rows_of(ref, n):
        return jnp.concatenate([ref[half, :, n, :] for half in range(2)], axis=0)

    def to_all(source, target, pair):
        @pl.loop(0, ny - 1)
        def _(o):
            there = lax.rem(j + 1 + lax.rem(o + ny // 2 - 1, ny - 1), ny)
            pltpu.make_async_remote_copy(
                src_ref=source.at[there],
                dst_ref=target.at[j],
                send_sem=g_send.at[pair],
                recv_sem=g_recv.at[pair],
                device_id=(i, there),
                device_id_type=MESH,
            ).start()

        target[j] = source[j]

    def got_bytes(target, blocks, pair):
        span = pl.ds(0, blocks)
        pltpu.make_async_copy(target.at[span], target.at[span], g_recv.at[pair]).wait()

    def sent_bytes(target, blocks, pair):
        span = pl.ds(0, blocks)
        pltpu.make_async_copy(target.at[span], target.at[span], g_send.at[pair]).wait()

    here, beyond, whole = pl.ds(0, 128), pl.ds(128, 128), pl.ds(0, 256)

    lane_8, sub_8 = lane_of((8, 128)), sub_of((8, 128))
    arrivals[0].wait()
    for q in range(7):
        for x in range(4):
            heat[q, x, :, here] = g_in[q, pl.ds(x, 8, stride=4), :]
    for n in (2, 3):
        arrivals[n].wait()
    for x in range(2):
        solid_k[x, :, here] = s_in[pl.ds(x, 8, stride=2), :]
        solid_k[6 + x, :, here] = 0.2 + 0.8 * m_in[pl.ds(x, 8, stride=2), :].astype(F32)
    solid_0 = [solid_k[x, :, here] for x in range(2)]
    k_here = [solid_k[6 + x, :, here] for x in range(2)]

    square = (128, 128)
    lane, sub = lane_of(square), sub_of(square)
    lane_32, sub_32 = lane_of((32, 128)), sub_of((32, 128))
    row_lane = lane_of((1, 128))
    diagonal = lane == sub

    def as_row(col):
        return jnp.sum(jnp.where(diagonal, jnp.broadcast_to(col, square), 0.0), axis=0, keepdims=True)

    for n in (4, 5, 6, 7):
        arrivals[n].wait()
    owner = owner_in[...]
    face_index = face_in[...]
    wall = wall_in[...]
    live = lane_of((1, 128)) < jnp.broadcast_to(tally_in[...], (1, 128))
    cell_row = jnp.where(live, owner * 256 + face_index, -1).astype(F32)
    small = [owner, face_index >> 7, face_index & 127, wall >> 7, wall & 127]
    rows_8 = jnp.zeros((8, 128), F32)
    for n, row in enumerate([value.astype(F32) for value in small] + [jnp.where(live, 1.0, 0.0)]):
        rows_8 = jnp.where(sub_8 == n, row, rows_8)
    turned = lax.dot_general(
        jnp.where(diagonal, 1.0, 0.0).astype(jnp.bfloat16),
        rows_8.astype(jnp.bfloat16),
        (((1,), (1,)), ((), ())),
        preferred_element_type=F32,
    )
    owner_col, face_x_col, face_y_col, wall_x_col, wall_y_col, live_col = (
        jnp.sum(jnp.where(lane_of((128, 8)) == n, turned, 0.0), axis=1, keepdims=True) for n in range(6)
    )
    owner_row = owner.astype(F32)
    face_col = 128.0 * face_x_col + face_y_col
    cell_col = jnp.where(live_col > 0.5, 256.0 * owner_col + face_col, -1.0)
    rank_col = jnp.sum(
        jnp.where((jnp.broadcast_to(owner_row, square) == owner_col) & (lane < sub), 1.0, 0.0),
        axis=1,
        keepdims=True,
    )
    lane_f = lane.astype(F32)
    wall_hit = jnp.where(lane_f == wall_y_col, live_col, 0.0)
    for x in range(4):
        wall_mask[x] = jnp.where(wall_x_col == float(x), wall_hit, 0.0)
    def at_wall(rows):
        total = wall_mask[0] * rows[0]
        for x in range(1, 4):
            total = total + wall_mask[x] * rows[x]
        return jnp.sum(total, axis=1, keepdims=True)

    def on_wall(col):
        return [jnp.sum(wall_mask[x] * col, axis=0, keepdims=True) for x in range(4)]

    def fill(buffer, n, value):
        buffer[:, n, :] = jnp.broadcast_to(value, (buffer.shape[0], 128))

    warmth = heat[0, :, 0:1, here]
    for q in range(1, 7):
        warmth = warmth + heat[q, :, 0:1, here]
    t1_col = at_wall([warmth[x] for x in range(4)])
    fill(early, 0, cell_row)
    fill(early, 1, as_row(t1_col))
    k_top = [k_here[x][7:8] for x in range(2)]
    k_inner = jnp.where(row_lane == 1, turn(k_top[1], 1, 1), turn(k_top[1], 127, 1))
    fill(early, 2, jnp.where((row_lane == 0) | (row_lane == 127), k_top[0], k_inner))
    for x in range(2):
        fill(early, 3 + x, solid_0[x][7:8])

    named = on_wall(cell_col + 1.0)
    named_8 = jnp.zeros((8, 128), F32)
    for x in range(4):
        named_8 = jnp.where((sub_8 & 3) == x, named[x], named_8)
    columns[5] = named_8
    pl.semaphore_wait(barrier, len(greeted))
    solid_x_halo = send_solid(0, here) + send_solid(3, here)
    round_first(early, near_early, 0)

    arrivals[1].wait()
    for q in range(19):
        for x in range(4):
            flow[q, x, :, here] = f_in[q, pl.ds(x, 8, stride=4), :]
    units = [(flow, q, x) for q in range(19) for x in range(4)] + [(heat, q, x) for q in range(7) for x in range(4)]
    for tile in range(5):
        packed = jnp.zeros((8, 128), F32)
        for n, (ref, q, x) in enumerate(units[21 * tile : 21 * tile + 21]):
            inside = (lane_8 >= 6 * n) & (lane_8 < 6 * n + 6)
            packed = jnp.where(inside, turn(ref[q, x, :, here], 6 * n + 3, 1), packed)
        columns[tile] = packed
    column_halo = [copy(columns, columns_low, (i, upper)), copy(columns, columns_high, (i, lower))]
    both = [solid_k.at[pl.ds(0, 2), :, here], solid_k.at[pl.ds(6, 2), :, here]]
    solid_y_halo = [
        made
        for n, part in enumerate(both)
        for made in (copy(part, solid_low_y.at[n], (i, upper)), copy(part, solid_high_y.at[n], (i, lower)))
    ]

    collide_flow(flow, post_f.at[0], speeds.at[0], here)
    collide_heat(heat, post_g.at[0], speeds.at[0], here)
    up = down = jnp.zeros((1, 128), F32)
    for x in range(4):
        up = jnp.where(row_lane == x, turn(post_g[0, x + 1, 3, 0:1, here], x + 1, 1), up)
        down = jnp.where(row_lane == x, turn(post_g[0, x + 1, 4, 0:1, here], x, 1), down)
    quick[0], quick[1] = up, down
    quick[2], quick[3] = post_g[0, 4, 1, 0:1, here], post_g[0, 1, 2, 0:1, here]
    for x in range(4):
        covered_ref[x, :, here] = jnp.broadcast_to(jnp.sum(wall_mask[x], axis=0, keepdims=True), (8, 128))

    quick_halo = [
        copy(quick.at[0], got_quick.at[0], (i, upper)),
        copy(quick.at[1], got_quick.at[1], (i, lower)),
        copy(quick.at[2], got_quick.at[2], (right, j)),
        copy(quick.at[3], got_quick.at[3], (left, j)),
    ]

    gates_x = (jnp.where(i == 0, 0.0, 1.0), jnp.where(i == nx - 1, 0.0, 1.0))
    gates_y = (jnp.where(j == 0, 0.0, 1.0), jnp.where(j == ny - 1, 0.0, 1.0))

    def conduct(field, r, k, span, y_gates):
        change = fluxes(
            field,
            k,
            jnp.where(i > 0, solid_low_x[r, :, span], field[0]),
            jnp.where(i > 0, solid_low_x[3, :, span], k[0]),
            jnp.where(i < nx - 1, solid_high_x[r, :, span], field[1]),
            jnp.where(i < nx - 1, solid_high_x[3, :, span], k[1]),
            gates_x + y_gates,
        )
        return [field[x] + DT * change[x] for x in range(2)]

    settle(solid_x_halo)
    inner_1 = conduct(solid_0, 0, k_here, here, (0.0, 0.0))
    for x in range(2):
        late[0, x : x + 1, :] = inner_1[x][7:8]
    round_first(late, near_late, 2)

    round_second(near_early, got_early, 0)
    settle(quick_halo)
    rest_rows = []
    for x in range(4):
        post = lambda q, at=x: post_g[0, at + 1, q, 0:1, here]
        total = post(0) + (post_g[0, x, 1, 0:1, here] if x else got_quick[2])
        total = total + (post_g[0, x + 2, 2, 0:1, here] if x < 3 else got_quick[3])
        total = total + jnp.where(row_lane == 0, turn(got_quick[0], 128 - x, 1), turn(post(3), 1, 1))
        total = total + jnp.where(row_lane == 127, turn(got_quick[1], 127 - x, 1), turn(post(4), 127, 1))
        wall_post = post(6)
        total = total + jnp.where(covered_ref[x, 0:1, here] > 0.5, -wall_post, wall_post)
        rest_rows.append(total + post_g[0, x + 1, 6, 1:2, here])
    a2_col = at_wall(rest_rows)
    fill(third, 0, as_row(a2_col))
    round_first(third, near_third, 4)

    settle(solid_y_halo)
    for x in range(2):
        for n, at in ((0, 0), (1, 6)):
            solid_k[at + x, :, beyond] = jnp.where(lane_8 < 64, solid_high_y[n, x], solid_low_y[n, x])
    solid_x_halo = send_solid(0, beyond) + send_solid(3, beyond)
    settle(column_halo)
    for tile in range(5):
        low, high = columns_low[tile], columns_high[tile]
        for n, (ref, q, x) in enumerate(units[21 * tile : 21 * tile + 21]):
            ref[q, x, :, beyond] = jnp.where(lane_8 < 64, turn(high, 125 - 6 * n, 1), turn(low, 125 - 6 * n, 1))
    named_beyond = jnp.where(lane_8 < 64, columns_high[5], columns_low[5])
    collide_flow(flow, post_f.at[0], speeds.at[0], beyond)
    collide_heat(heat, post_g.at[0], speeds.at[0], beyond)
    heat_halo = send_heat(0)
    flow_halo = send_flow(0)
    round_second(near_late, got_late, 2)

    for x in range(4):
        covered_ref[x, :, beyond] = jnp.where(jnp.broadcast_to(named_beyond[x : x + 1], (8, 128)) > 0.5, 1.0, 0.0)
    halo_lanes = (126, 127, 0, 1)
    halo_cells = [
        jnp.sum(
            jnp.where(lane_8 == jnp.where(sub_8 < 4, halo_lanes[n], halo_lanes[n + 1]), named_beyond, 0.0),
            axis=1,
            keepdims=True,
        )
        - 1.0
        for n in (0, 2)
    ]
    rows_col = jnp.concatenate([cell_col] + halo_cells, axis=0)
    cell_ref[0:144] = jnp.broadcast_to(rows_col, (144, 128))
    rows_cell = cell_ref[0:144].astype(jnp.int32)
    above = (sub_8 & 3) >= 2
    halo_column = jnp.where(above, (sub_8 & 3) - 2, 126 + (sub_8 & 3))
    cell_ref[144:152] = (
        (j + jnp.where(above, 1, -1)) * 256 + 128 * (sub_8 >> 2) + halo_column
    ).astype(F32)
    lane_144 = lane_of((144, 128))
    face_hit = jnp.where(lane_144 == (rows_cell & 127), 1.0, 0.0)
    rows_place = ((rows_cell >> 8) & 31) + 32 * ((rows_cell >> 7) & 1)
    pick = jnp.where(lane_144 == rows_place, 1.0, 0.0)[:, 0:64]

    def put_heat(q, value):
        heat[q] = value

    def put_flow(q, value):
        flow[q] = value

    settle(heat_halo)
    stream(post_g.at[0], HEAT_PLACES, covered_ref[...], put_heat)
    settle(flow_halo)
    stream(post_f.at[0], FLOW_PLACES, None, put_flow)
    collide_flow(flow, post_f.at[1], speeds.at[1], whole)
    flow_halo = send_flow(1)

    settle(solid_x_halo)
    k = [solid_k[6 + x] for x in range(2)]
    field_0 = [solid_k[x] for x in range(2)]
    p1 = conduct(field_0, 0, k, whole, gates_y)

    second_wait(got_early, g_recv.at[1])

    cells = rows_of(got_early, 0).astype(jnp.int32)
    named_here = (cells >> 8) == j
    earlier = jnp.dot(
        jnp.where(named_here, 1.0, 0.0).astype(jnp.bfloat16),
        jnp.where(sub < lane, 1.0, 0.0).astype(jnp.bfloat16),
        preferred_element_type=F32,
    )
    slot = jnp.where(named_here, earlier, -1.0)

    def slot_columns(value):
        return [
            jnp.broadcast_to(
                jnp.sum(jnp.where(slot == float(c), value, 0.0), axis=1, keepdims=True), (32, 128)
            )
            for c in range(CAP)
        ]

    faces = slot_columns(((cells & 255) + 1).astype(F32))

    def own_sums(fields):
        result = []
        for x in range(2):
            place = (lane_32 + (128 * x + 1)).astype(F32)
            totals = [jnp.zeros((32, 128), F32) for _ in fields]
            for c in range(CAP):
                hit = faces[c] == place
                for n, field in enumerate(fields):
                    totals[n] = totals[n] + jnp.where(hit, 1.0 if field is None else field[c], 0.0)
            result.append([jnp.sum(total, axis=0, keepdims=True) for total in totals])
        return result

    def halo_sums(cols):
        result = []
        for x in range(2):
            rows = [jnp.zeros((1, 128), F32) for _ in cols]
            for n, col in enumerate(cols):
                for m, at in enumerate(halo_lanes):
                    rows[n] = jnp.where(row_lane == at, col[144 + 4 * x + m : 145 + 4 * x + m], rows[n])
            result.append(rows)
        return result

    def joined(own, halo):
        return [
            [jnp.concatenate([a, b], axis=1) for a, b in zip(own[x], halo[x])] for x in range(2)
        ]

    top_256 = sub_of((8, 256)) == 7

    def on_top(value, row):
        return value + jnp.where(top_256, jnp.broadcast_to(row, (8, 256)), 0.0)

    def same_cell(value_of, count, many_rows):
        halves = []
        for first, last in ((0, 80), (80, many_rows)):
            cells = cell_ref[first:last]

            def body(b, carry, cells=cells):
                hit = cells == got_early[b // 16, lax.rem(b, 16), 0:1, :]
                total = carry[0] + jnp.where(hit, value_of(b), 0.0)
                if count:
                    return total, carry[1] + jnp.where(hit, 1.0, 0.0)
                return (total,)

            zero = jnp.zeros((last - first, 128), F32)
            halves.append(lax.fori_loop(0, ny, body, (zero, zero) if count else (zero,), unroll=2))
        return [jnp.concatenate(parts, axis=0) for parts in zip(*halves)]

    total_1, number = same_cell(lambda b: got_early[b // 16, lax.rem(b, 16), 1:2, :], True, 152)
    number_col = jnp.sum(number, axis=1, keepdims=True)
    total_1_col = jnp.sum(total_1, axis=1, keepdims=True)
    sums = joined(own_sums([slot_columns(rows_of(got_early, 1)), None]), halo_sums([total_1_col, number_col]))
    many = [sums[x][1] for x in range(2)]
    solid_1 = [on_top(p1[x], DT * (sums[x][0] - many[x] * field_0[x][7:8])) for x in range(2)]
    for x in range(2):
        solid_k[2 + x] = solid_1[x]
    solid_halo = send_solid(1, whole)

    edge_k = rows_of(got_early, 2)
    crossing = []
    for x in range(2):
        inside = rows_of(got_early, 3 + x)
        inside_k = edge_k if x == 0 else jnp.where(lane_32 == 0, turn(edge_k, 127, 1), turn(edge_k, 1, 1))
        outside, outside_k = (turn(turn(part, 31, 0), 127, 1) for part in (inside, inside_k))
        c, cb = conduct_of(inside, inside_k), conduct_of(outside, outside_k)
        rise = 2.0 * c * cb / (c + cb) * (outside - inside)
        rise = jnp.where((lane_32 == 127) & (sub_32 != ny - 1), rise, 0.0)
        crossing.append(DT * (rise - turn(turn(rise, 1, 0), 1, 1)))

    known = jnp.concatenate(
        [jnp.concatenate(crossing, axis=0), jnp.concatenate([rows_of(got_early, 3 + x) for x in range(2)], axis=0)],
        axis=1,
    )
    known = pick_rows(pick, known)
    known = face_hit * (known[:, 0:128] - DT * number_col[0:144] * known[:, 128:256])
    known_col = jnp.sum(known, axis=1, keepdims=True) + DT * total_1_col[0:144]
    round_second(near_third, got_third, 4)

    def surface_at_rows(rows):
        return jnp.sum(face_hit * pick_rows(pick, jnp.concatenate(rows, axis=0)), axis=1, keepdims=True)

    second_wait(got_late, g_recv.at[3])
    w1_col = known_col + surface_at_rows([rows_of(got_late, x) for x in range(2)])

    def warm_wall(col):
        rows = on_wall(col[0:128])
        for x in range(4):
            outer = jnp.zeros((1, 128), F32)
            for n, at in enumerate(halo_lanes):
                outer = jnp.where(row_lane == at, col[128 + 4 * n + x : 129 + 4 * n + x], outer)
            outer = jnp.where(covered_ref[x, 0:1, beyond] > 0.5, outer, 0.0)
            heat[5, x, 0:1, here] = heat[5, x, 0:1, here] + 0.25 * rows[x]
            heat[5, x, 0:1, beyond] = heat[5, x, 0:1, beyond] + 0.25 * outer

    warm_wall(w1_col)
    heat_halo = []
    collide_heat(heat, post_g.at[1], speeds.at[1], whole, lambda: heat_halo.extend(send_heat(1)))

    settle(solid_halo)
    p2 = conduct(solid_1, 1, k, whole, gates_y)
    p2 = [on_top(p2[x], (-0.75 * DT) * many[x] * solid_1[x][7:8]) for x in range(2)]
    for x in range(2):
        fill(surface, x, p2[x][7:8, 0:128])
    to_all(surface, got_surface, 8)

    settle(heat_halo)
    post = post_g.at[1]
    warmth = post[1:5, 0, 0:1] + post[0:4, 1, 0:1] + post[2:6, 2, 0:1]
    warmth = warmth + turn(post[1:5, 3, 0:1], 1, 2) + turn(post[1:5, 4, 0:1], -1, 2)
    bounce = post[1:5, 6, 0:1]
    warmth = warmth + jnp.where(covered_ref[:, 0:1] > 0.5, -bounce, bounce) + post[1:5, 6, 1:2]
    a3_col = at_wall([warmth[x, :, 0:128] for x in range(4)])
    fill(mid, 0, as_row(a3_col))
    to_all(mid, got_mid, 6)
    stream(post_g.at[1], HEAT_PLACES, covered_ref[...], put_heat)

    second_wait(got_third, g_recv.at[5])
    (total_2,) = same_cell(lambda b: got_third[b // 16, lax.rem(b, 16)], False, 152)
    total_2_col = jnp.sum(total_2, axis=1, keepdims=True)
    rest = joined(own_sums([slot_columns(rows_of(got_third, 0))]), halo_sums([total_2_col]))
    solid_2 = [on_top(p2[x], DT * rest[x][0]) for x in range(2)]
    for x in range(2):
        solid_k[4 + x] = solid_2[x]
    solid_halo = send_solid(2, whole)

    settle(flow_halo)
    stream(post_f.at[1], FLOW_PLACES, None, put_flow)
    collide_flow(flow, post_f.at[2], speeds.at[2], whole)
    flow_halo = send_flow(2)

    settle(solid_halo)
    p3 = conduct(solid_2, 2, k, whole, gates_y)
    p3 = [on_top(p3[x], (-0.75 * DT) * many[x] * solid_2[x][7:8])[:, 0:128] for x in range(2)]
    answer = jnp.zeros((32, 128), F32)
    for c in range(CAP):
        first = faces[c] == (lane_32 + 1).astype(F32)
        second = faces[c] == (lane_32 + 129).astype(F32)
        at_cell = jnp.where(first, p3[0][7:8], jnp.where(second, p3[1][7:8], 0.0))
        answer = jnp.where(lane_32 == c, jnp.sum(at_cell, axis=1, keepdims=True), answer)
    answer_out[:, 0, :] = answer
    to_all(answer_out, got_answer, 7)

    got_bytes(got_surface, ny - 1, 8)
    w2_col = surface_at_rows([got_surface[:, x, :] for x in range(2)]) + DT * total_2_col[0:144]
    warm_wall(w2_col)
    heat_halo = []
    collide_heat(heat, post_g.at[2], speeds.at[2], whole, lambda: heat_halo.extend(send_heat(2)))

    settle(flow_halo)

    def write_flow(q, value):
        for x in range(4):
            f_out[q, pl.ds(x, 8, stride=4), :] = value[x, :, 0:128]

    stream(post_f.at[2], FLOW_PLACES, None, write_flow)

    got_bytes(got_mid, ny - 1, 6)
    (total_3,) = same_cell(lambda b: got_mid[b], False, 128)
    got_bytes(got_answer, ny - 1, 7)
    pick_owner = jnp.where(lane_of((128, 32)).astype(F32) == owner_col, 1.0, 0.0)
    found = pick_rows(pick_owner, got_answer[:, 0, :])
    w3_col = jnp.sum(jnp.where(lane_f == rank_col, found, 0.0) + DT * total_3, axis=1, keepdims=True)
    w3_rows = on_wall(w3_col)
    last = own_sums([slot_columns(got_mid[:, 0, :])])
    for x in range(2):
        s_out[pl.ds(x, 8, stride=2), :] = p3[x] + jnp.where(sub_8 == 7, DT * last[x][0], 0.0)


    settle(heat_halo)

    def write_heat(q, value):
        for x in range(4):
            row = value[x, :, 0:128]
            if q == 5:
                row = row + jnp.where(sub_8 == 0, 0.25 * w3_rows[x], 0.0)
            g_out[q, pl.ds(x, 8, stride=4), :] = row

    stream(post_g.at[2], HEAT_PLACES, covered_ref[...], write_heat)

    for n, target in enumerate((got_early, got_late, got_third)):
        few = target.at[0, pl.ds(0, 3)]
        pltpu.make_async_copy(few, few, g_send.at[2 * n]).wait()
        second_wait(target, g_send.at[2 * n + 1])
    sent_bytes(got_mid, ny - 1, 6)
    sent_bytes(got_answer, ny - 1, 7)
    sent_bytes(got_surface, ny - 1, 8)
    for made, goes in sent:
        if goes is None:
            made.wait_send()
        else:
            pl.when(goes)(made.wait_send)


def finish(*refs):
    sources, targets, sems = refs[0:3], refs[3:6], refs[6]
    copies = [pltpu.make_async_copy(a, b, sems.at[n]) for n, (a, b) in enumerate(zip(sources, targets))]
    for made in copies:
        made.start()
    for made in copies:
        made.wait()


def on_device(nx, ny, flow, heat, solid, metal, owner, tally, wall, face):
    vmem = functools.partial(pltpu.VMEM, dtype=F32)
    tile, wide = (8, 128), (8, 256)
    copies = 40
    results = (
        jax.ShapeDtypeStruct((19, 32, 128), F32),
        jax.ShapeDtypeStruct((7, 32, 128), F32),
        jax.ShapeDtypeStruct((16, 128), F32),
    )
    out = pl.pallas_call(
        functools.partial(kernel, nx, ny),
        out_shape=tuple(pltpu.VMEM(result.shape, result.dtype) for result in results),
        in_specs=[pl.BlockSpec(memory_space=pltpu.HBM)] * 8,
        out_specs=[pl.BlockSpec(memory_space=pltpu.VMEM)] * 3,
        scratch_shapes=[
            vmem((19, 32, 128)),
            vmem((7, 32, 128)),
            vmem((16, 128)),
            pltpu.VMEM((16, 128), jnp.int32),
            pltpu.VMEM((1, 128), jnp.int32),
            pltpu.VMEM((1, 1), jnp.int32),
            pltpu.VMEM((1, 128), jnp.int32),
            pltpu.VMEM((1, 128), jnp.int32),
            vmem((19, 4) + wide),
            vmem((7, 4) + wide),
            vmem((STEPS, 6, 19) + wide),
            vmem((STEPS, 6, 7) + wide),
            vmem((STEPS, 3, 4) + wide),
            vmem((8,) + wide),
            vmem((4,) + wide),
            vmem((4,) + wide),
            vmem((2, 2) + tile),
            vmem((2, 2) + tile),
            vmem((6,) + tile),
            vmem((6,) + tile),
            vmem((6,) + tile),
            vmem((4, 1, 128)),
            vmem((4, 1, 128)),
            vmem((4, 128, 128)),
            vmem((4,) + wide),
            vmem((152, 128)),
            vmem((1, 5, 128)),
            vmem((2, 2, 5, 128)),
            vmem((2, 16, 5, 128)),
            vmem((1, 2, 128)),
            vmem((2, 2, 2, 128)),
            vmem((2, 16, 2, 128)),
            vmem((1, 1, 128)),
            vmem((2, 2, 1, 128)),
            vmem((2, 16, 1, 128)),
            vmem((32, 2, 128)),
            vmem((32, 2, 128)),
            vmem((32, 1, 128)),
            vmem((32, 1, 128)),
            vmem((32, 1, 128)),
            vmem((32, 1, 128)),
            pltpu.SemaphoreType.DMA((8,)),
            pltpu.SemaphoreType.DMA((copies,)),
            pltpu.SemaphoreType.DMA((copies,)),
            pltpu.SemaphoreType.DMA((9,)),
            pltpu.SemaphoreType.DMA((9,)),
        ],
        compiler_params=pltpu.CompilerParams(
            collective_id=0, has_side_effects=True, vmem_limit_bytes=ROOM
        ),
        name="coupled_steps",
    )(
        flow.reshape(19, 32, 128),
        heat.reshape(7, 32, 128),
        solid.reshape(16, 128),
        metal.reshape(16, 128),
        owner.reshape(1, 128),
        tally,
        wall,
        face,
    )
    out = pl.pallas_call(
        finish,
        out_shape=results,
        in_specs=[pl.BlockSpec(memory_space=pltpu.VMEM)] * 3,
        out_specs=[pl.BlockSpec(memory_space=pltpu.HBM)] * 3,
        scratch_shapes=[pltpu.SemaphoreType.DMA((3,))],
        compiler_params=pltpu.CompilerParams(vmem_limit_bytes=1024 * 1024),
        name="write_out",
    )(*out)
    return out[0].reshape(19, 8, 4, 128), out[1].reshape(7, 8, 4, 128), out[2].reshape(8, 2, 128)


def solution(mesh):
    placed = (
        P(None, None, "gx", "gy"),
        P(None, None, "gx", "gy"),
        P(None, "gx", "gy"),
        P(None, "gx", "gy"),
        P("gx", "gy", None),
        P("gx", "gy"),
        P("gx", "gy"),
        P("gx", "gy"),
    )
    return jax.shard_map(
        functools.partial(on_device, mesh.shape["gx"], mesh.shape["gy"]),
        mesh=mesh,
        in_specs=placed,
        out_specs=(P(None, None, "gx", "gy"), P(None, None, "gx", "gy"), P(None, "gx", "gy")),
        check_vma=False,
    )
```

```python
import functools

import jax
import jax.numpy as jnp
from jax import lax
from jax.experimental import pallas as pl
from jax.experimental.pallas import tpu as pltpu
from jax.sharding import PartitionSpec as P

MESH = pl.DeviceIdType.MESH
F32 = jnp.float32
STEPS = 3
CAP = 8

VELOCITY = [
    (0, 0, 0),
    (1, 0, 0),
    (-1, 0, 0),
    (0, 1, 0),
    (0, -1, 0),
    (0, 0, 1),
    (0, 0, -1),
    (1, 1, 0),
    (-1, -1, 0),
    (1, -1, 0),
    (-1, 1, 0),
    (1, 0, 1),
    (-1, 0, -1),
    (1, 0, -1),
    (-1, 0, 1),
    (0, 1, 1),
    (0, -1, -1),
    (0, 1, -1),
    (0, -1, 1),
]
OPPOSITE = [VELOCITY.index((-a, -b, -c)) for a, b, c in VELOCITY]
ORDER = [1, 7, 9, 11, 13, 2, 8, 10, 12, 14, 0, 3, 4, 5, 6, 15, 16, 17, 18]
PLACE = {q: n for n, q in enumerate(ORDER)}
DT = 0.04
ROOM = 63 * 1024 * 1024


def lane_of(shape):
    return lax.broadcasted_iota(jnp.int32, shape, len(shape) - 1)


def sub_of(shape):
    return lax.broadcasted_iota(jnp.int32, shape, len(shape) - 2)


def turn(value, amount, axis):
    size = value.shape[axis]
    amount = amount % size
    return value if amount == 0 else pltpu.roll(value, amount, axis)


def collide_flow(state, post, velocity, span):
    total, moved = None, [None, None, None]
    for q in range(19):
        value = state[q, :, :, span]
        total = value if total is None else total + value
        for axis in range(3):
            if VELOCITY[q][axis] == 1:
                moved[axis] = value if moved[axis] is None else moved[axis] + value
            elif VELOCITY[q][axis] == -1:
                moved[axis] = -value if moved[axis] is None else moved[axis] - value
    inverse = 1.0 / total
    speed = [part * inverse for part in moved]
    for axis in range(3):
        velocity[axis, :, :, span] = speed[axis]
    base = 1.0 - 1.5 * (speed[0] * speed[0] + speed[1] * speed[1] + speed[2] * speed[2])
    post[1:5, PLACE[0], :, span] = (1.25 / 3.0) * total * base - 0.25 * state[0, :, :, span]
    axial = (1.25 / 18.0) * total
    diagonal = (1.25 / 36.0) * total
    for q in range(1, 19):
        p = OPPOSITE[q]
        if p < q:
            continue
        along = None
        for axis in range(3):
            c = VELOCITY[q][axis]
            if c:
                term = speed[axis] if c == 1 else -speed[axis]
                along = term if along is None else along + term
        even = base + 4.5 * along * along
        odd = 3.0 * along
        scale = axial if q < 7 else diagonal
        post[1:5, PLACE[q], :, span] = scale * (even + odd) - 0.25 * state[q, :, :, span]
        post[1:5, PLACE[p], :, span] = scale * (even - odd) - 0.25 * state[p, :, :, span]


def collide_heat(state, post, velocity, span, x_done=None):
    keep = 1.0 - 1.0 / 0.7
    warmth = state[0, :, :, span]
    for q in range(1, 7):
        warmth = warmth + state[q, :, :, span]
    part = (0.125 / 0.7) * warmth
    for axis in range(3):
        tilt = part * (4.0 * velocity[axis, :, :, span])
        for q in (1 + 2 * axis, 2 + 2 * axis):
            sign = tilt if q == 1 + 2 * axis else -tilt
            post[1:5, q, :, span] = keep * state[q, :, :, span] + (part + sign)
        if axis == 0 and x_done is not None:
            x_done()
    post[1:5, 0, :, span] = keep * state[0, :, :, span] + (0.25 / 0.7) * warmth


def pick_rows(pick, value):
    parts, rest = [], value
    for _ in range(3):
        parts.append(rest.astype(jnp.bfloat16))
        rest = rest - parts[-1].astype(F32)
    found = jnp.dot(
        pick.astype(jnp.bfloat16), jnp.concatenate(parts, axis=1), preferred_element_type=F32
    )
    width = value.shape[1]
    return found[:, 0:width] + (found[:, width : 2 * width] + found[:, 2 * width :])


def lifted(value, cz, bounce):
    if cz == 0:
        return value
    layer = sub_of(value.shape)
    if cz == 1:
        return jnp.where(layer == 0, bounce, turn(value, 1, 1))
    return jnp.where(layer == 7, bounce, turn(value, 7, 1))


def stream(post, places, covered, put):
    for q, place in enumerate(places):
        cx, cy, cz = VELOCITY[q]
        value = turn(post[1 - cx : 5 - cx, place], cy, 2)
        bounce = None
        if cz:
            bounce = post[1:5, places[OPPOSITE[q]]]
            if covered is not None and q == 5:
                bounce = jnp.where(covered > 0.5, -bounce, bounce)
        put(q, lifted(value, cz, bounce))


FLOW_PLACES = [PLACE[q] for q in range(19)]
HEAT_PLACES = list(range(7))


def conduct_of(warmth, k):
    return k * (1.0 + 0.5 * warmth)


def fluxes(field, k, low_x, low_xk, high_x, high_xk, gates):
    gate_low_x, gate_high_x, gate_low_y, gate_high_y = gates
    shape = field[0].shape
    lane, layer = lane_of(shape), sub_of(shape)
    cond = [conduct_of(field[x], k[x]) for x in range(2)]
    result = []

    def face(a, ca, b, cb):
        return 2.0 * ca * cb / (ca + cb) * (b - a)

    inner = face(field[0], cond[0], field[1], cond[1])
    for x in range(2):
        here, c = field[x], cond[x]
        if x == 0:
            total = inner + gate_low_x * face(here, c, low_x, conduct_of(low_x, low_xk))
        else:
            total = gate_high_x * face(here, c, high_x, conduct_of(high_x, high_xk)) - inner
        above = face(here, c, turn(here, -1, 1), turn(c, -1, 1))
        below = -turn(above, 1, 1)
        total = total + jnp.where(lane == 127, gate_high_y, 1.0) * above
        total = total + jnp.where(lane == 0, gate_low_y, 1.0) * below
        up = face(here, c, turn(here, 7, 0), turn(c, 7, 0))
        down = -turn(up, 1, 0)
        total = total + jnp.where(layer == 0, 0.0, down) + jnp.where(layer == 7, 0.0, up)
        result.append(total)
    return result


def kernel(
    nx,
    ny,
    f_hbm,
    g_hbm,
    s_hbm,
    m_hbm,
    owner_hbm,
    tally_hbm,
    wall_hbm,
    face_hbm,
    f_out,
    g_out,
    s_out,
    f_in,
    g_in,
    s_in,
    m_in,
    owner_in,
    tally_in,
    wall_in,
    face_in,
    flow,
    heat,
    post_f,
    post_g,
    speeds,
    solid_k,
    solid_low_x,
    solid_high_x,
    solid_low_y,
    solid_high_y,
    columns,
    columns_low,
    columns_high,
    quick,
    got_quick,
    wall_mask,
    covered_ref,
    cell_ref,
    early,
    near_early,
    got_early,
    late,
    near_late,
    got_late,
    third,
    near_third,
    got_third,
    surface,
    got_surface,
    mid,
    got_mid,
    answer_out,
    got_answer,
    i_sem,
    n_send,
    n_recv,
    g_send,
    g_recv,
):
    i, j = lax.axis_index("gx"), lax.axis_index("gy")
    right, left = lax.rem(i + 1, nx), lax.rem(i + nx - 1, nx)
    upper, lower = lax.rem(j + 1, ny), lax.rem(j + ny - 1, ny)
    along = ny // 4
    y = lax.rem(j // 2, along)
    corner = j // (2 * along) * 2 + lax.rem(j, 2)

    def seat(corner_there, y_there):
        return corner_there // 2 * (2 * along) + 2 * y_there + lax.rem(corner_there, 2)

    barrier = pltpu.get_barrier_semaphore()
    greeted = [(i, seat(lax.rem(corner + d, 4), y)) for d in (2, 3, 1)]
    greeted += [(i, seat(corner, lax.rem(y + d, along))) for d in (4, 3, 5, 2, 6, 1, 7)]
    greeted += [(right, j), (left, j), (i, upper), (i, lower)]
    for device in greeted:
        pl.semaphore_signal(barrier, inc=1, device_id=device, device_id_type=MESH)

    arrivals = []
    for n, (source, target) in enumerate(
        (
            (g_hbm, g_in),
            (f_hbm, f_in),
            (s_hbm, s_in),
            (m_hbm, m_in),
            (owner_hbm, owner_in),
            (tally_hbm, tally_in),
            (wall_hbm, wall_in),
            (face_hbm, face_in),
        )
    ):
        made = pltpu.make_async_copy(source, target, i_sem.at[n])
        made.start()
        arrivals.append(made)

    sent = []

    def copy(source, target, device, goes=None, comes=None):
        n = len(sent)
        made = pltpu.make_async_remote_copy(
            src_ref=source,
            dst_ref=target,
            send_sem=n_send.at[n],
            recv_sem=n_recv.at[n],
            device_id=device,
            device_id_type=MESH,
        )
        if goes is None:
            made.start()
        else:
            pl.when(goes)(made.start)
        sent.append((made, goes))
        return made, comes

    def settle(copies):
        for made, comes in copies:
            if comes is None:
                made.wait_recv()
            else:
                pl.when(comes)(made.wait_recv)

    def to_right(source, target):
        return copy(source, target, (right, j), i < nx - 1, i > 0)

    def to_left(source, target):
        return copy(source, target, (left, j), i > 0, i < nx - 1)

    def send_flow(t):
        return [
            copy(post_f.at[t, 4, pl.ds(0, 5)], post_f.at[t, 0, pl.ds(0, 5)], (right, j)),
            copy(post_f.at[t, 1, pl.ds(5, 5)], post_f.at[t, 5, pl.ds(5, 5)], (left, j)),
        ]

    def send_heat(t):
        return [
            copy(post_g.at[t, 4, 1], post_g.at[t, 0, 1], (right, j)),
            copy(post_g.at[t, 1, 2], post_g.at[t, 5, 2], (left, j)),
        ]

    def send_solid(r, lanes):
        return [
            to_right(solid_k.at[2 * r + 1, :, lanes], solid_low_x.at[r, :, lanes]),
            to_left(solid_k.at[2 * r, :, lanes], solid_high_x.at[r, :, lanes]),
        ]

    def round_first(source, near, pair):
        for d in (2, 3, 1):
            there = lax.rem(corner + d, 4)
            pltpu.make_async_remote_copy(
                src_ref=source.at[0],
                dst_ref=near.at[corner // 2, lax.rem(corner, 2)],
                send_sem=g_send.at[pair],
                recv_sem=g_recv.at[pair],
                device_id=(i, seat(there, y)),
                device_id_type=MESH,
            ).start()
        near[corner // 2, lax.rem(corner, 2)] = source[0]

    def round_second(near, target, pair):
        few = target.at[0, pl.ds(0, 3)]
        pltpu.make_async_copy(few, few, g_recv.at[pair]).wait()
        for d in (4, 3, 5, 2, 6, 1, 7):
            pltpu.make_async_remote_copy(
                src_ref=near,
                dst_ref=target.at[:, pl.ds(2 * y, 2)],
                send_sem=g_send.at[pair + 1],
                recv_sem=g_recv.at[pair + 1],
                device_id=(i, seat(corner, lax.rem(y + d, along))),
                device_id_type=MESH,
            ).start()
        for half in range(2):
            for c in range(2):
                target[half, 2 * y + c] = near[half, c]

    def second_wait(target, sems):
        most = target.at[:, pl.ds(0, ny // 2 - 2)]
        pltpu.make_async_copy(most, most, sems).wait()

    def rows_of(ref, n):
        return jnp.concatenate([ref[half, :, n, :] for half in range(2)], axis=0)

    def to_all(source, target, pair):
        @pl.loop(0, ny - 1)
        def _(o):
            there = lax.rem(j + 1 + lax.rem(o + ny // 2 - 1, ny - 1), ny)
            pltpu.make_async_remote_copy(
                src_ref=source.at[there],
                dst_ref=target.at[j],
                send_sem=g_send.at[pair],
                recv_sem=g_recv.at[pair],
                device_id=(i, there),
                device_id_type=MESH,
            ).start()

        target[j] = source[j]

    def got_bytes(target, blocks, pair):
        span = pl.ds(0, blocks)
        pltpu.make_async_copy(target.at[span], target.at[span], g_recv.at[pair]).wait()

    def sent_bytes(target, blocks, pair):
        span = pl.ds(0, blocks)
        pltpu.make_async_copy(target.at[span], target.at[span], g_send.at[pair]).wait()

    here, beyond, whole = pl.ds(0, 128), pl.ds(128, 128), pl.ds(0, 256)

    lane_8, sub_8 = lane_of((8, 128)), sub_of((8, 128))
    arrivals[0].wait()
    for q in range(7):
        for x in range(4):
            heat[q, x, :, here] = g_in[q, pl.ds(x, 8, stride=4), :]
    for n in (2, 3):
        arrivals[n].wait()
    for x in range(2):
        solid_k[x, :, here] = s_in[pl.ds(x, 8, stride=2), :]
        solid_k[6 + x, :, here] = 0.2 + 0.8 * m_in[pl.ds(x, 8, stride=2), :].astype(F32)
    solid_0 = [solid_k[x, :, here] for x in range(2)]
    k_here = [solid_k[6 + x, :, here] for x in range(2)]

    square = (128, 128)
    lane, sub = lane_of(square), sub_of(square)
    lane_32, sub_32 = lane_of((32, 128)), sub_of((32, 128))
    row_lane = lane_of((1, 128))
    diagonal = lane == sub

    def as_row(col):
        return jnp.sum(jnp.where(diagonal, jnp.broadcast_to(col, square), 0.0), axis=0, keepdims=True)

    for n in (4, 5, 6, 7):
        arrivals[n].wait()
    owner = owner_in[...]
    face_index = face_in[...]
    wall = wall_in[...]
    live = lane_of((1, 128)) < jnp.broadcast_to(tally_in[...], (1, 128))
    cell_row = jnp.where(live, owner * 256 + face_index, -1).astype(F32)
    small = [owner, face_index >> 7, face_index & 127, wall >> 7, wall & 127]
    rows_8 = jnp.zeros((8, 128), F32)
    for n, row in enumerate([value.astype(F32) for value in small] + [jnp.where(live, 1.0, 0.0)]):
        rows_8 = jnp.where(sub_8 == n, row, rows_8)
    turned = lax.dot_general(
        jnp.where(diagonal, 1.0, 0.0).astype(jnp.bfloat16),
        rows_8.astype(jnp.bfloat16),
        (((1,), (1,)), ((), ())),
        preferred_element_type=F32,
    )
    owner_col, face_x_col, face_y_col, wall_x_col, wall_y_col, live_col = (
        jnp.sum(jnp.where(lane_of((128, 8)) == n, turned, 0.0), axis=1, keepdims=True) for n in range(6)
    )
    owner_row = owner.astype(F32)
    face_col = 128.0 * face_x_col + face_y_col
    cell_col = jnp.where(live_col > 0.5, 256.0 * owner_col + face_col, -1.0)
    rank_col = jnp.sum(
        jnp.where((jnp.broadcast_to(owner_row, square) == owner_col) & (lane < sub), 1.0, 0.0),
        axis=1,
        keepdims=True,
    )
    lane_f = lane.astype(F32)
    wall_hit = jnp.where(lane_f == wall_y_col, live_col, 0.0)
    for x in range(4):
        wall_mask[x] = jnp.where(wall_x_col == float(x), wall_hit, 0.0)
    def at_wall(rows):
        total = wall_mask[0] * rows[0]
        for x in range(1, 4):
            total = total + wall_mask[x] * rows[x]
        return jnp.sum(total, axis=1, keepdims=True)

    def on_wall(col):
        return [jnp.sum(wall_mask[x] * col, axis=0, keepdims=True) for x in range(4)]

    def fill(buffer, n, value):
        buffer[:, n, :] = jnp.broadcast_to(value, (buffer.shape[0], 128))

    warmth = heat[0, :, 0:1, here]
    for q in range(1, 7):
        warmth = warmth + heat[q, :, 0:1, here]
    t1_col = at_wall([warmth[x] for x in range(4)])
    fill(early, 0, cell_row)
    fill(early, 1, as_row(t1_col))
    k_top = [k_here[x][7:8] for x in range(2)]
    k_inner = jnp.where(row_lane == 1, turn(k_top[1], 1, 1), turn(k_top[1], 127, 1))
    fill(early, 2, jnp.where((row_lane == 0) | (row_lane == 127), k_top[0], k_inner))
    for x in range(2):
        fill(early, 3 + x, solid_0[x][7:8])

    named = on_wall(cell_col + 1.0)
    named_8 = jnp.zeros((8, 128), F32)
    for x in range(4):
        named_8 = jnp.where((sub_8 & 3) == x, named[x], named_8)
    columns[5] = named_8
    pl.semaphore_wait(barrier, len(greeted))
    solid_x_halo = send_solid(0, here) + send_solid(3, here)
    round_first(early, near_early, 0)

    arrivals[1].wait()
    for q in range(19):
        for x in range(4):
            flow[q, x, :, here] = f_in[q, pl.ds(x, 8, stride=4), :]
    units = [(flow, q, x) for q in range(19) for x in range(4)] + [(heat, q, x) for q in range(7) for x in range(4)]
    for tile in range(5):
        packed = jnp.zeros((8, 128), F32)
        for n, (ref, q, x) in enumerate(units[21 * tile : 21 * tile + 21]):
            inside = (lane_8 >= 6 * n) & (lane_8 < 6 * n + 6)
            packed = jnp.where(inside, turn(ref[q, x, :, here], 6 * n + 3, 1), packed)
        columns[tile] = packed
    column_halo = [copy(columns, columns_low, (i, upper)), copy(columns, columns_high, (i, lower))]
    both = [solid_k.at[pl.ds(0, 2), :, here], solid_k.at[pl.ds(6, 2), :, here]]
    solid_y_halo = [
        made
        for n, part in enumerate(both)
        for made in (copy(part, solid_low_y.at[n], (i, upper)), copy(part, solid_high_y.at[n], (i, lower)))
    ]

    collide_flow(flow, post_f.at[0], speeds.at[0], here)
    collide_heat(heat, post_g.at[0], speeds.at[0], here)
    up = down = jnp.zeros((1, 128), F32)
    for x in range(4):
        up = jnp.where(row_lane == x, turn(post_g[0, x + 1, 3, 0:1, here], x + 1, 1), up)
        down = jnp.where(row_lane == x, turn(post_g[0, x + 1, 4, 0:1, here], x, 1), down)
    quick[0], quick[1] = up, down
    quick[2], quick[3] = post_g[0, 4, 1, 0:1, here], post_g[0, 1, 2, 0:1, here]
    for x in range(4):
        covered_ref[x, :, here] = jnp.broadcast_to(jnp.sum(wall_mask[x], axis=0, keepdims=True), (8, 128))

    quick_halo = [
        copy(quick.at[0], got_quick.at[0], (i, upper)),
        copy(quick.at[1], got_quick.at[1], (i, lower)),
        copy(quick.at[2], got_quick.at[2], (right, j)),
        copy(quick.at[3], got_quick.at[3], (left, j)),
    ]

    gates_x = (jnp.where(i == 0, 0.0, 1.0), jnp.where(i == nx - 1, 0.0, 1.0))
    gates_y = (jnp.where(j == 0, 0.0, 1.0), jnp.where(j == ny - 1, 0.0, 1.0))

    def conduct(field, r, k, span, y_gates):
        change = fluxes(
            field,
            k,
            jnp.where(i > 0, solid_low_x[r, :, span], field[0]),
            jnp.where(i > 0, solid_low_x[3, :, span], k[0]),
            jnp.where(i < nx - 1, solid_high_x[r, :, span], field[1]),
            jnp.where(i < nx - 1, solid_high_x[3, :, span], k[1]),
            gates_x + y_gates,
        )
        return [field[x] + DT * change[x] for x in range(2)]

    settle(solid_x_halo)
    inner_1 = conduct(solid_0, 0, k_here, here, (0.0, 0.0))
    for x in range(2):
        late[0, x : x + 1, :] = inner_1[x][7:8]
    round_first(late, near_late, 2)

    round_second(near_early, got_early, 0)
    settle(quick_halo)
    rest_rows = []
    for x in range(4):
        post = lambda q, at=x: post_g[0, at + 1, q, 0:1, here]
        total = post(0) + (post_g[0, x, 1, 0:1, here] if x else got_quick[2])
        total = total + (post_g[0, x + 2, 2, 0:1, here] if x < 3 else got_quick[3])
        total = total + jnp.where(row_lane == 0, turn(got_quick[0], 128 - x, 1), turn(post(3), 1, 1))
        total = total + jnp.where(row_lane == 127, turn(got_quick[1], 127 - x, 1), turn(post(4), 127, 1))
        wall_post = post(6)
        total = total + jnp.where(covered_ref[x, 0:1, here] > 0.5, -wall_post, wall_post)
        rest_rows.append(total + post_g[0, x + 1, 6, 1:2, here])
    a2_col = at_wall(rest_rows)
    fill(third, 0, as_row(a2_col))
    round_first(third, near_third, 4)

    settle(solid_y_halo)
    for x in range(2):
        for n, at in ((0, 0), (1, 6)):
            solid_k[at + x, :, beyond] = jnp.where(lane_8 < 64, solid_high_y[n, x], solid_low_y[n, x])
    solid_x_halo = send_solid(0, beyond) + send_solid(3, beyond)
    settle(column_halo)
    for tile in range(5):
        low, high = columns_low[tile], columns_high[tile]
        for n, (ref, q, x) in enumerate(units[21 * tile : 21 * tile + 21]):
            ref[q, x, :, beyond] = jnp.where(lane_8 < 64, turn(high, 125 - 6 * n, 1), turn(low, 125 - 6 * n, 1))
    named_beyond = jnp.where(lane_8 < 64, columns_high[5], columns_low[5])
    collide_flow(flow, post_f.at[0], speeds.at[0], beyond)
    collide_heat(heat, post_g.at[0], speeds.at[0], beyond)
    heat_halo = send_heat(0)
    flow_halo = send_flow(0)
    round_second(near_late, got_late, 2)

    for x in range(4):
        covered_ref[x, :, beyond] = jnp.where(jnp.broadcast_to(named_beyond[x : x + 1], (8, 128)) > 0.5, 1.0, 0.0)
    halo_lanes = (126, 127, 0, 1)
    halo_cells = [
        jnp.sum(
            jnp.where(lane_8 == jnp.where(sub_8 < 4, halo_lanes[n], halo_lanes[n + 1]), named_beyond, 0.0),
            axis=1,
            keepdims=True,
        )
        - 1.0
        for n in (0, 2)
    ]
    rows_col = jnp.concatenate([cell_col] + halo_cells, axis=0)
    cell_ref[0:144] = jnp.broadcast_to(rows_col, (144, 128))
    rows_cell = cell_ref[0:144].astype(jnp.int32)
    above = (sub_8 & 3) >= 2
    halo_column = jnp.where(above, (sub_8 & 3) - 2, 126 + (sub_8 & 3))
    cell_ref[144:152] = (
        (j + jnp.where(above, 1, -1)) * 256 + 128 * (sub_8 >> 2) + halo_column
    ).astype(F32)
    lane_144 = lane_of((144, 128))
    face_hit = jnp.where(lane_144 == (rows_cell & 127), 1.0, 0.0)
    rows_place = ((rows_cell >> 8) & 31) + 32 * ((rows_cell >> 7) & 1)
    pick = jnp.where(lane_144 == rows_place, 1.0, 0.0)[:, 0:64]

    def put_heat(q, value):
        heat[q] = value

    def put_flow(q, value):
        flow[q] = value

    settle(heat_halo)
    stream(post_g.at[0], HEAT_PLACES, covered_ref[...], put_heat)
    settle(flow_halo)
    stream(post_f.at[0], FLOW_PLACES, None, put_flow)
    collide_flow(flow, post_f.at[1], speeds.at[1], whole)
    flow_halo = send_flow(1)

    settle(solid_x_halo)
    k = [solid_k[6 + x] for x in range(2)]
    field_0 = [solid_k[x] for x in range(2)]
    p1 = conduct(field_0, 0, k, whole, gates_y)

    second_wait(got_early, g_recv.at[1])

    cells = rows_of(got_early, 0).astype(jnp.int32)
    named_here = (cells >> 8) == j
    earlier = jnp.dot(
        jnp.where(named_here, 1.0, 0.0).astype(jnp.bfloat16),
        jnp.where(sub < lane, 1.0, 0.0).astype(jnp.bfloat16),
        preferred_element_type=F32,
    )
    slot = jnp.where(named_here, earlier, -1.0)

    def slot_columns(value):
        return [
            jnp.broadcast_to(
                jnp.sum(jnp.where(slot == float(c), value, 0.0), axis=1, keepdims=True), (32, 128)
            )
            for c in range(CAP)
        ]

    faces = slot_columns(((cells & 255) + 1).astype(F32))

    def own_sums(fields):
        result = []
        for x in range(2):
            place = (lane_32 + (128 * x + 1)).astype(F32)
            totals = [jnp.zeros((32, 128), F32) for _ in fields]
            for c in range(CAP):
                hit = faces[c] == place
                for n, field in enumerate(fields):
                    totals[n] = totals[n] + jnp.where(hit, 1.0 if field is None else field[c], 0.0)
            result.append([jnp.sum(total, axis=0, keepdims=True) for total in totals])
        return result

    def halo_sums(cols):
        result = []
        for x in range(2):
            rows = [jnp.zeros((1, 128), F32) for _ in cols]
            for n, col in enumerate(cols):
                for m, at in enumerate(halo_lanes):
                    rows[n] = jnp.where(row_lane == at, col[4 * x + m : 4 * x + m + 1], rows[n])
            result.append(rows)
        return result

    def joined(own, halo):
        return [
            [jnp.concatenate([a, b], axis=1) for a, b in zip(own[x], halo[x])] for x in range(2)
        ]

    top_256 = sub_of((8, 256)) == 7

    def on_top(value, row):
        return value + jnp.where(top_256, jnp.broadcast_to(row, (8, 256)), 0.0)

    def same_cell(value_of, count, spans):
        halves = []
        for first, last in spans:
            cells = cell_ref[first:last]

            def body(b, carry, cells=cells):
                hit = cells == got_early[b // 16, lax.rem(b, 16), 0:1, :]
                total = carry[0] + jnp.where(hit, value_of(b), 0.0)
                if count:
                    return total, carry[1] + jnp.where(hit, 1.0, 0.0)
                return (total,)

            zero = jnp.zeros((last - first, 128), F32)
            halves.append(lax.fori_loop(0, ny, body, (zero, zero) if count else (zero,), unroll=2))
        return [jnp.concatenate(parts, axis=0) for parts in zip(*halves)]

    total_1, number = same_cell(lambda b: got_early[b // 16, lax.rem(b, 16), 1:2, :], True, ((0, 80), (80, 152)))
    number_col = jnp.sum(number, axis=1, keepdims=True)
    total_1_col = jnp.sum(total_1, axis=1, keepdims=True)
    sums = joined(own_sums([slot_columns(rows_of(got_early, 1)), None]), halo_sums([total_1_col[144:152], number_col[144:152]]))
    many = [sums[x][1] for x in range(2)]
    solid_1 = [on_top(p1[x], DT * (sums[x][0] - many[x] * field_0[x][7:8])) for x in range(2)]
    for x in range(2):
        solid_k[2 + x] = solid_1[x]
    solid_halo = send_solid(1, whole)

    edge_k = rows_of(got_early, 2)
    crossing = []
    for x in range(2):
        inside = rows_of(got_early, 3 + x)
        inside_k = edge_k if x == 0 else jnp.where(lane_32 == 0, turn(edge_k, 127, 1), turn(edge_k, 1, 1))
        outside, outside_k = (turn(turn(part, 31, 0), 127, 1) for part in (inside, inside_k))
        c, cb = conduct_of(inside, inside_k), conduct_of(outside, outside_k)
        rise = 2.0 * c * cb / (c + cb) * (outside - inside)
        rise = jnp.where((lane_32 == 127) & (sub_32 != ny - 1), rise, 0.0)
        crossing.append(DT * (rise - turn(turn(rise, 1, 0), 1, 1)))

    known = jnp.concatenate(
        [jnp.concatenate(crossing, axis=0), jnp.concatenate([rows_of(got_early, 3 + x) for x in range(2)], axis=0)],
        axis=1,
    )
    known = pick_rows(pick, known)
    known = face_hit * (known[:, 0:128] - DT * number_col[0:144] * known[:, 128:256])
    known_col = jnp.sum(known, axis=1, keepdims=True) + DT * total_1_col[0:144]
    round_second(near_third, got_third, 4)

    def surface_at_rows(rows):
        return jnp.sum(face_hit * pick_rows(pick, jnp.concatenate(rows, axis=0)), axis=1, keepdims=True)

    second_wait(got_late, g_recv.at[3])
    w1_col = known_col + surface_at_rows([rows_of(got_late, x) for x in range(2)])

    def warm_wall(col):
        rows = on_wall(col[0:128])
        for x in range(4):
            outer = jnp.zeros((1, 128), F32)
            for n, at in enumerate(halo_lanes):
                outer = jnp.where(row_lane == at, col[128 + 4 * n + x : 129 + 4 * n + x], outer)
            outer = jnp.where(covered_ref[x, 0:1, beyond] > 0.5, outer, 0.0)
            heat[5, x, 0:1, here] = heat[5, x, 0:1, here] + 0.25 * rows[x]
            heat[5, x, 0:1, beyond] = heat[5, x, 0:1, beyond] + 0.25 * outer

    warm_wall(w1_col)
    heat_halo = []
    collide_heat(heat, post_g.at[1], speeds.at[1], whole, lambda: heat_halo.extend(send_heat(1)))

    settle(solid_halo)
    p2 = conduct(solid_1, 1, k, whole, gates_y)
    p2 = [on_top(p2[x], (-0.75 * DT) * many[x] * solid_1[x][7:8]) for x in range(2)]
    for x in range(2):
        fill(surface, x, p2[x][7:8, 0:128])
    to_all(surface, got_surface, 8)

    settle(heat_halo)
    post = post_g.at[1]
    warmth = post[1:5, 0, 0:1] + post[0:4, 1, 0:1] + post[2:6, 2, 0:1]
    warmth = warmth + turn(post[1:5, 3, 0:1], 1, 2) + turn(post[1:5, 4, 0:1], -1, 2)
    bounce = post[1:5, 6, 0:1]
    warmth = warmth + jnp.where(covered_ref[:, 0:1] > 0.5, -bounce, bounce) + post[1:5, 6, 1:2]
    a3_col = at_wall([warmth[x, :, 0:128] for x in range(4)])
    fill(mid, 0, as_row(a3_col))
    to_all(mid, got_mid, 6)
    stream(post_g.at[1], HEAT_PLACES, covered_ref[...], put_heat)

    second_wait(got_third, g_recv.at[5])
    rest_of = lambda b: got_third[b // 16, lax.rem(b, 16)]
    (beyond_2,) = same_cell(rest_of, False, ((144, 152),))
    rest = joined(own_sums([slot_columns(rows_of(got_third, 0))]), halo_sums([jnp.sum(beyond_2, axis=1, keepdims=True)]))
    solid_2 = [on_top(p2[x], DT * rest[x][0]) for x in range(2)]
    for x in range(2):
        solid_k[4 + x] = solid_2[x]
    solid_halo = send_solid(2, whole)
    (total_2,) = same_cell(rest_of, False, ((0, 80), (80, 144)))
    total_2_col = jnp.sum(total_2, axis=1, keepdims=True)

    settle(flow_halo)
    stream(post_f.at[1], FLOW_PLACES, None, put_flow)
    collide_flow(flow, post_f.at[2], speeds.at[2], whole)
    flow_halo = send_flow(2)

    settle(solid_halo)
    p3 = conduct(solid_2, 2, k, whole, gates_y)
    p3 = [on_top(p3[x], (-0.75 * DT) * many[x] * solid_2[x][7:8])[:, 0:128] for x in range(2)]
    answer = jnp.zeros((32, 128), F32)
    for c in range(CAP):
        first = faces[c] == (lane_32 + 1).astype(F32)
        second = faces[c] == (lane_32 + 129).astype(F32)
        at_cell = jnp.where(first, p3[0][7:8], jnp.where(second, p3[1][7:8], 0.0))
        answer = jnp.where(lane_32 == c, jnp.sum(at_cell, axis=1, keepdims=True), answer)
    answer_out[:, 0, :] = answer
    to_all(answer_out, got_answer, 7)

    got_bytes(got_surface, ny - 1, 8)
    w2_col = surface_at_rows([got_surface[:, x, :] for x in range(2)]) + DT * total_2_col
    warm_wall(w2_col)
    heat_halo = []
    collide_heat(heat, post_g.at[2], speeds.at[2], whole, lambda: heat_halo.extend(send_heat(2)))

    settle(flow_halo)

    def write_flow(q, value):
        for x in range(4):
            f_out[q, pl.ds(x, 8, stride=4), :] = value[x, :, 0:128]

    stream(post_f.at[2], FLOW_PLACES, None, write_flow)

    got_bytes(got_mid, ny - 1, 6)
    (total_3,) = same_cell(lambda b: got_mid[b], False, ((0, 64), (64, 128)))
    got_bytes(got_answer, ny - 1, 7)
    pick_owner = jnp.where(lane_of((128, 32)).astype(F32) == owner_col, 1.0, 0.0)
    found = pick_rows(pick_owner, got_answer[:, 0, :])
    w3_col = jnp.sum(jnp.where(lane_f == rank_col, found, 0.0) + DT * total_3, axis=1, keepdims=True)
    w3_rows = on_wall(w3_col)
    last = own_sums([slot_columns(got_mid[:, 0, :])])
    for x in range(2):
        s_out[pl.ds(x, 8, stride=2), :] = p3[x] + jnp.where(sub_8 == 7, DT * last[x][0], 0.0)


    settle(heat_halo)

    def write_heat(q, value):
        for x in range(4):
            row = value[x, :, 0:128]
            if q == 5:
                row = row + jnp.where(sub_8 == 0, 0.25 * w3_rows[x], 0.0)
            g_out[q, pl.ds(x, 8, stride=4), :] = row

    stream(post_g.at[2], HEAT_PLACES, covered_ref[...], write_heat)

    for n, target in enumerate((got_early, got_late, got_third)):
        few = target.at[0, pl.ds(0, 3)]
        pltpu.make_async_copy(few, few, g_send.at[2 * n]).wait()
        second_wait(target, g_send.at[2 * n + 1])
    sent_bytes(got_mid, ny - 1, 6)
    sent_bytes(got_answer, ny - 1, 7)
    sent_bytes(got_surface, ny - 1, 8)
    for made, goes in sent:
        if goes is None:
            made.wait_send()
        else:
            pl.when(goes)(made.wait_send)


def finish(*refs):
    sources, targets, sems = refs[0:3], refs[3:6], refs[6]
    copies = [pltpu.make_async_copy(a, b, sems.at[n]) for n, (a, b) in enumerate(zip(sources, targets))]
    for made in copies:
        made.start()
    for made in copies:
        made.wait()


def on_device(nx, ny, flow, heat, solid, metal, owner, tally, wall, face):
    vmem = functools.partial(pltpu.VMEM, dtype=F32)
    tile, wide = (8, 128), (8, 256)
    copies = 40
    results = (
        jax.ShapeDtypeStruct((19, 32, 128), F32),
        jax.ShapeDtypeStruct((7, 32, 128), F32),
        jax.ShapeDtypeStruct((16, 128), F32),
    )
    out = pl.pallas_call(
        functools.partial(kernel, nx, ny),
        out_shape=tuple(pltpu.VMEM(result.shape, result.dtype) for result in results),
        in_specs=[pl.BlockSpec(memory_space=pltpu.HBM)] * 8,
        out_specs=[pl.BlockSpec(memory_space=pltpu.VMEM)] * 3,
        scratch_shapes=[
            vmem((19, 32, 128)),
            vmem((7, 32, 128)),
            vmem((16, 128)),
            pltpu.VMEM((16, 128), jnp.int32),
            pltpu.VMEM((1, 128), jnp.int32),
            pltpu.VMEM((1, 1), jnp.int32),
            pltpu.VMEM((1, 128), jnp.int32),
            pltpu.VMEM((1, 128), jnp.int32),
            vmem((19, 4) + wide),
            vmem((7, 4) + wide),
            vmem((STEPS, 6, 19) + wide),
            vmem((STEPS, 6, 7) + wide),
            vmem((STEPS, 3, 4) + wide),
            vmem((8,) + wide),
            vmem((4,) + wide),
            vmem((4,) + wide),
            vmem((2, 2) + tile),
            vmem((2, 2) + tile),
            vmem((6,) + tile),
            vmem((6,) + tile),
            vmem((6,) + tile),
            vmem((4, 1, 128)),
            vmem((4, 1, 128)),
            vmem((4, 128, 128)),
            vmem((4,) + wide),
            vmem((152, 128)),
            vmem((1, 5, 128)),
            vmem((2, 2, 5, 128)),
            vmem((2, 16, 5, 128)),
            vmem((1, 2, 128)),
            vmem((2, 2, 2, 128)),
            vmem((2, 16, 2, 128)),
            vmem((1, 1, 128)),
            vmem((2, 2, 1, 128)),
            vmem((2, 16, 1, 128)),
            vmem((32, 2, 128)),
            vmem((32, 2, 128)),
            vmem((32, 1, 128)),
            vmem((32, 1, 128)),
            vmem((32, 1, 128)),
            vmem((32, 1, 128)),
            pltpu.SemaphoreType.DMA((8,)),
            pltpu.SemaphoreType.DMA((copies,)),
            pltpu.SemaphoreType.DMA((copies,)),
            pltpu.SemaphoreType.DMA((9,)),
            pltpu.SemaphoreType.DMA((9,)),
        ],
        compiler_params=pltpu.CompilerParams(
            collective_id=0, has_side_effects=True, vmem_limit_bytes=ROOM
        ),
        name="coupled_steps",
    )(
        flow.reshape(19, 32, 128),
        heat.reshape(7, 32, 128),
        solid.reshape(16, 128),
        metal.reshape(16, 128),
        owner.reshape(1, 128),
        tally,
        wall,
        face,
    )
    out = pl.pallas_call(
        finish,
        out_shape=results,
        in_specs=[pl.BlockSpec(memory_space=pltpu.VMEM)] * 3,
        out_specs=[pl.BlockSpec(memory_space=pltpu.HBM)] * 3,
        scratch_shapes=[pltpu.SemaphoreType.DMA((3,))],
        compiler_params=pltpu.CompilerParams(vmem_limit_bytes=1024 * 1024),
        name="write_out",
    )(*out)
    return out[0].reshape(19, 8, 4, 128), out[1].reshape(7, 8, 4, 128), out[2].reshape(8, 2, 128)


def solution(mesh):
    placed = (
        P(None, None, "gx", "gy"),
        P(None, None, "gx", "gy"),
        P(None, "gx", "gy"),
        P(None, "gx", "gy"),
        P("gx", "gy", None),
        P("gx", "gy"),
        P("gx", "gy"),
        P("gx", "gy"),
    )
    return jax.shard_map(
        functools.partial(on_device, mesh.shape["gx"], mesh.shape["gy"]),
        mesh=mesh,
        in_specs=placed,
        out_specs=(P(None, None, "gx", "gy"), P(None, None, "gx", "gy"), P(None, "gx", "gy")),
        check_vma=False,
    )
```
